32 devices in a mesh: dp: 8 (over y, x, core), seq: 4 (over z).
Axes of the slice: x: 2, y: 2, z: 4, core: 2. Of those that a mesh axis runs over, the one named last changes fastest.
Arguments:
- hidden_in: bfloat16 [32, 512, 768], P('dp', 'seq'), may hold values from -6 to 6
- query_lengths: int32 [32], P('dp'), may hold values from 1 to 64, as said below
- doc_lengths: int32 [32], P('dp'), may hold values from 32 to 448, as said below
- w_query: bfloat16 [768, 768], replicated, may hold values from -0.109375 to 0.109375
- w_key: bfloat16 [768, 768], replicated, may hold values from -0.109375 to 0.109375
- w_value: bfloat16 [768, 768], replicated, may hold values from -0.21875 to 0.21875
- w_attn_out: bfloat16 [768, 768], replicated, may hold values from -0.875 to 0.875
- w_inner: bfloat16 [768, 3072], replicated, may hold values from -0.21875 to 0.21875
- w_outer: bfloat16 [3072, 768], replicated, may hold values from -0.109375 to 0.109375
- gain_attn: bfloat16 [768], replicated, may hold values from 0.5 to 1.5
- gain_ffn: bfloat16 [768], replicated, may hold values from 0.5 to 1.5
- bias_table: bfloat16 [32, 12], replicated, may hold values from -4 to 4
- cotangent: bfloat16 [32, 512, 768], P('dp', 'seq'), may hold values from -6 to 6
Outputs:
- layer_out: bfloat16 [32, 512, 768], P('dp', 'seq')
- grad_in: bfloat16 [32, 512, 768], P('dp', 'seq')
- grad_query: float32 [768, 768], P('dp')
- grad_key: float32 [768, 768], P('dp')
- grad_value: float32 [768, 768], P('dp')
- grad_attn_out: float32 [768, 768], P('dp')
- grad_inner: float32 [768, 3072], P('dp')
- grad_outer: float32 [3072, 768], P('dp')
- grad_gain_attn: float32 [768], P('dp')
- grad_gain_ffn: float32 [768], P('dp')
- grad_table: float32 [32, 12], replicated
The draws below stay inside these ranges and needn't reach their ends.
Inputs may be any that keep to these rules, and one draw needn't show every extreme that they name: `query_lengths`: in each aligned block of 2 rows one row has exactly 64 query tokens and fills all 512 slots. `doc_lengths`: A row's query and document tokens together take at most 512 slots; its other slots are padding. The row that fills all 512 slots has exactly 448 document tokens.
All inputs are finite; a program needn't handle non-finite values.
Results may differ from the reference program's by a relative error of at most 0.018.
Values may be sent and summed in bfloat16 or wider, within the bound.
A program may use at most 256 MiB of HBM per device.

```python
import math
import jax
import jax.numpy as jnp
from jax import lax

D = 768
H = 12
DH = 64
FF = 3072
NB = 32
LEN = 512
QMAX = 64
ROWS_DEV = 2
ROWS = 32


def lengths_pair(key):
    row_index = jnp.arange(ROWS)
    chosen = jax.random.randint(jax.random.fold_in(key, 11), (ROWS // ROWS_DEV,), 0, ROWS_DEV)
    whole_row = row_index % ROWS_DEV == jnp.repeat(chosen, ROWS_DEV)
    query_len = jax.random.randint(jax.random.fold_in(key, 12), (ROWS,), 1, QMAX + 1)
    query_len = jnp.where(whole_row, QMAX, query_len)
    doc_floor = QMAX // 2
    doc_len = doc_floor + jax.random.randint(jax.random.fold_in(key, 13), (ROWS,), 0, LEN - query_len - doc_floor + 1)
    doc_len = jnp.minimum(doc_len, LEN - QMAX)
    doc_len = jnp.where(whole_row, LEN - QMAX, doc_len)
    return (query_len.astype(jnp.int32), doc_len.astype(jnp.int32))


def draw_query_lengths(key, part):
    return lengths_pair(key)[0]


def draw_doc_lengths(key, part):
    return lengths_pair(key)[1]


def shard_levels(stream_key, dims, pieces, smallest, top_value):
    loudness, own = 1.0, jax.random.fold_in(stream_key, 6)
    for position, shards_of in pieces:
        heights = jnp.exp(jax.random.uniform(jax.random.fold_in(own, position), (shards_of,), jnp.float32, smallest / len(pieces), top_value / len(pieces)))
        loudness = loudness * jnp.repeat(heights, dims[position] // shards_of).reshape([-1 if axis == position else 1 for axis in range(len(dims))])
    return loudness


def scatter_about(stream_key, dims, spread, bound, cuts=(), held_as=jnp.bfloat16):
    array = jax.random.normal(stream_key, dims, jnp.float32) * spread
    if len(cuts) > 0:
        array = shard_levels(stream_key, dims, cuts, -0.22, 0.18) * array
    return jnp.clip(array, min=-bound, max=bound).astype(held_as)


def setup_inputs(seed: int = 0) -> dict:
    seeds = jax.random.split(jax.random.key(seed), 14)
    return {
        "hidden_in": scatter_about(seeds[0], (ROWS, LEN, D), 1.0, 6.0, ((0, 8), (1, 4))),
        "query_lengths": draw_query_lengths(jax.random.fold_in(seeds[13], 71), 0),
        "doc_lengths": draw_doc_lengths(jax.random.fold_in(seeds[13], 71), 0),
        "w_query": scatter_about(seeds[3], (D, D), (4 * D) ** -0.5, 0.109375),
        "w_key": scatter_about(seeds[4], (D, D), (4 * D) ** -0.5, 0.109375),
        "w_value": scatter_about(seeds[5], (D, D), D ** -0.5, 0.21875),
        "w_attn_out": scatter_about(seeds[6], (D, D), (D // 16) ** -0.5, 0.875),
        "w_inner": scatter_about(seeds[7], (D, FF), D ** -0.5, 0.21875),
        "w_outer": scatter_about(seeds[8], (FF, D), FF ** -0.5, 0.109375),
        "gain_attn": jnp.clip(1.0 + 0.1 * jax.random.normal(seeds[9], (D,), jnp.float32), 0.5, 1.5).astype(jnp.bfloat16),
        "gain_ffn": jnp.clip(1.0 + 0.1 * jax.random.normal(seeds[10], (D,), jnp.float32), 0.5, 1.5).astype(jnp.bfloat16),
        "bias_table": scatter_about(seeds[11], (NB, H), 1.0, 4.0),
        "cotangent": scatter_about(seeds[12], (ROWS, LEN, D), 1.0, 6.0, ((0, 8), (1, 4))),
    }


EPS = 1e-06
NEG = -1000000000.0
LIMITS = (12, 16, 23, 32, 46, 64, 91)
HIGH = lax.Precision.HIGHEST

@jax.custom_vjp
def low(v):
    return lax.optimization_barrier(v.astype(jnp.bfloat16)).astype(jnp.float32)

@jax.custom_vjp
def low_back(v):
    return v

def low_keep(v):
    return (low(v), None)

def low_pass(kept, grad):
    return (grad,)

def back_keep(v):
    return (v, None)

def back_low(kept, grad):
    return (low(grad),)
low.defvjp(low_keep, low_pass)
low_back.defvjp(back_keep, back_low)

def rms_scale(values, gain_vec):
    factor = lax.rsqrt(lax.optimization_barrier(jnp.mean(values * values, axis=-1, keepdims=True)) + EPS)
    return values * factor * gain_vec

def buckets(relative):
    distance = jnp.abs(relative)
    far_bucket = 8 + sum(((distance >= thresh).astype(jnp.int32) for thresh in LIMITS))
    return jnp.where(relative > 0, 16, 0) + jnp.where(distance < 8, distance, far_bucket)

def reference(hidden_in, query_lengths, doc_lengths, w_query, w_key, w_value, w_attn_out, w_inner, w_outer, gain_attn, gain_ffn, bias_table, cotangent):
    group_rows = math.gcd(ROWS, max(1, 4096 // LEN))
    group_count = ROWS // group_rows
    positions = jnp.arange(LEN)
    relative = positions[None, :] - positions[:, None]
    one_hot = (buckets(relative)[:, :, None] == jnp.arange(NB)[None, None, :]).astype(jnp.float32).reshape(LEN * LEN, NB)
    key_live = positions[None, :] < (query_lengths + doc_lengths)[:, None]

    def forward(resid_in, wq, wk, wv, wo, wi, wf, gain_one, gain_two, table_f):
        pos_bias = jnp.dot(one_hot, table_f, precision=HIGH).reshape(LEN, LEN, H).transpose(2, 0, 1)

        def block_fn(pair):
            x_group, live_group = pair
            normed = low(rms_scale(x_group, gain_one))

            def project(weight):
                return low(low_back(jnp.einsum('gtd,de->gte', normed, weight, precision=HIGH)))
            queries = project(wq).reshape(group_rows, LEN, H, DH)
            keys_all = project(wk).reshape(group_rows, LEN, H, DH)
            values_all = project(wv).reshape(group_rows, LEN, H, DH)
            scores = jnp.einsum('gqhd,gkhd->ghqk', queries, keys_all, precision=HIGH) + pos_bias[None]
            scores = low_back(jnp.where(live_group[:, None, None, :], scores, NEG))
            row_max = lax.optimization_barrier(jnp.max(scores, axis=-1, keepdims=True))
            exponent = jnp.exp(scores - row_max)
            probs = low(exponent / lax.optimization_barrier(jnp.sum(exponent, axis=-1, keepdims=True)))
            attended = jnp.einsum('ghqk,gkhd->gqhd', probs, values_all, precision=HIGH)
            attended = low(low_back(attended)).reshape(group_rows, LEN, D)
            resid_mid = x_group + low_back(jnp.einsum('gtd,de->gte', attended, wo, precision=HIGH))
            normed_two = low(rms_scale(resid_mid, gain_two))
            inner = low_back(jnp.einsum('gtd,df->gtf', normed_two, wi, precision=HIGH))
            active = low(jax.nn.gelu(inner, approximate=True))
            return resid_mid + jnp.einsum('gtf,fd->gtd', active, wf, precision=HIGH)
        result = lax.map(jax.checkpoint(block_fn), (resid_in.reshape(group_count, group_rows, LEN, D), key_live.reshape(group_count, group_rows, LEN)))
        return result.reshape(ROWS, LEN, D)
    primals = tuple((arr.astype(jnp.float32) for arr in (hidden_in, w_query, w_key, w_value, w_attn_out, w_inner, w_outer, gain_attn, gain_ffn, bias_table)))
    result, pullback = jax.vjp(forward, *primals)
    grads = pullback(cotangent.astype(jnp.float32))
    return (result.astype(jnp.bfloat16), grads[0].astype(jnp.bfloat16), grads[1], grads[2], grads[3], grads[4], grads[5], grads[6], grads[7], grads[8], grads[9])
```

```python
from functools import partial

import jax
import jax.numpy as jnp
from jax import lax
from jax.sharding import PartitionSpec as P

EPS = 1e-06
NEG = -1000000000.0
LIMITS = (12, 16, 23, 32, 46, 64, 91)
HIGH = lax.Precision.HIGHEST


def rms_scale(values, gain_vec):
    factor = lax.rsqrt(jnp.mean(values * values, axis=-1, keepdims=True) + EPS)
    return values * factor * gain_vec


def buckets(relative):
    distance = jnp.abs(relative)
    far_bucket = 8 + sum(((distance >= thresh).astype(jnp.int32) for thresh in LIMITS))
    return jnp.where(relative > 0, 16, 0) + jnp.where(distance < 8, distance, far_bucket)


def position_bias(table_f, query_pos, key_pos):
    relative = key_pos[None, :] - query_pos[:, None]
    bucket_count, head_count = table_f.shape
    one_hot = (buckets(relative)[:, :, None] == jnp.arange(bucket_count)[None, None, :]).astype(
        jnp.float32
    )
    one_hot = one_hot.reshape(query_pos.shape[0] * key_pos.shape[0], bucket_count)
    pos_bias = jnp.dot(one_hot, table_f, precision=HIGH).reshape(
        query_pos.shape[0], key_pos.shape[0], head_count
    )
    return (one_hot, pos_bias.transpose(2, 0, 1))


def split_heads(arr, head_count):
    return arr.reshape(arr.shape[0], arr.shape[1], head_count, arr.shape[2] // head_count)


def scores_of(query_rows, key_rows, pos_bias, key_live):
    head_count = pos_bias.shape[0]
    scores = jnp.einsum(
        "rqhd,rkhd->rhqk",
        split_heads(query_rows, head_count),
        split_heads(key_rows, head_count),
        preferred_element_type=jnp.float32,
    )
    scores = scores + pos_bias[None]
    return jnp.where(key_live[:, None, None, :], scores, NEG)


def outer_sum(left, right):
    return lax.dot_general(
        left, right, (((0,), (0,)), ((), ())), preferred_element_type=jnp.float32
    )


def back_dot(grad_rows, weight):
    return lax.dot_general(
        grad_rows, weight, (((1,), (1,)), ((), ())), preferred_element_type=jnp.float32
    )


def on_device(
    hidden_in,
    query_lengths,
    doc_lengths,
    w_query,
    w_key,
    w_value,
    w_attn_out,
    w_inner,
    w_outer,
    gain_attn,
    gain_ffn,
    bias_table,
    cotangent,
):
    def to_rows(blocks):
        return lax.all_to_all(blocks, "seq", split_axis=0, concat_axis=1, tiled=True)

    def to_blocks(rows):
        return lax.all_to_all(rows, "seq", split_axis=1, concat_axis=0, tiled=True)

    hidden_rows = to_rows(hidden_in)
    cot_rows = to_rows(cotangent)
    row_count, length, width = hidden_rows.shape
    head_count = bias_table.shape[1]
    tokens = row_count * length
    first = lax.axis_index("seq") * row_count
    total_len = lax.dynamic_slice_in_dim(query_lengths + doc_lengths, first, row_count)
    gain_one = gain_attn.astype(jnp.float32)
    gain_two = gain_ffn.astype(jnp.float32)
    table_f = bias_table.astype(jnp.float32)

    def low_dot(rows, weight):
        return jnp.dot(rows, weight, preferred_element_type=jnp.float32).astype(jnp.bfloat16)

    resid_in = hidden_rows.astype(jnp.float32).reshape(tokens, width)
    cot_flat = cot_rows.reshape(tokens, width)
    normed_one = rms_scale(resid_in, gain_one).astype(jnp.bfloat16)
    query_low = low_dot(normed_one, w_query).reshape(row_count, length, width)
    key_low = low_dot(normed_one, w_key).reshape(row_count, length, width)
    value_low = low_dot(normed_one, w_value).reshape(row_count, length, width)
    pos = jnp.arange(length)
    key_live = pos[None, :] < total_len[:, None]
    one_hot, pos_bias = position_bias(table_f, pos, pos)
    scores = scores_of(query_low, key_low, pos_bias, key_live)
    row_max = jnp.max(scores, axis=-1, keepdims=True)
    exponent = jnp.exp(scores - row_max)
    probs = exponent / jnp.sum(exponent, axis=-1, keepdims=True)
    probs_low = probs.astype(jnp.bfloat16)
    value_heads = split_heads(value_low, head_count)
    attended_low = (
        jnp.einsum("rhqk,rkhd->rqhd", probs_low, value_heads, preferred_element_type=jnp.float32)
        .reshape(tokens, width)
        .astype(jnp.bfloat16)
    )
    resid_mid = resid_in + jnp.dot(attended_low, w_attn_out, preferred_element_type=jnp.float32)
    normed_two = rms_scale(resid_mid, gain_two).astype(jnp.bfloat16)
    inner = jnp.dot(normed_two, w_inner, preferred_element_type=jnp.float32)
    gelu_out, gelu_back = jax.vjp(partial(jax.nn.gelu, approximate=True), inner)
    active = gelu_out.astype(jnp.bfloat16)
    layer_rows = (
        (resid_mid + jnp.dot(active, w_outer, preferred_element_type=jnp.float32))
        .astype(jnp.bfloat16)
        .reshape(row_count, length, width)
    )
    grad_outer_w = outer_sum(active, cot_flat).astype(jnp.bfloat16)
    grad_inner_low = gelu_back(back_dot(cot_flat, w_outer))[0].astype(jnp.bfloat16)
    grad_inner_w = outer_sum(normed_two, grad_inner_low).astype(jnp.bfloat16)
    grad_normed_two = back_dot(grad_inner_low, w_inner)
    norm_out, norm_two_back = jax.vjp(rms_scale, resid_mid, gain_two)
    grad_mid_norm, gain_two_grad = norm_two_back(grad_normed_two)
    grad_mid = cot_flat.astype(jnp.float32) + grad_mid_norm
    grad_mid_low = grad_mid.astype(jnp.bfloat16)
    grad_attn_out_w = outer_sum(attended_low, grad_mid_low).astype(jnp.bfloat16)
    grad_attended = back_dot(grad_mid_low, w_attn_out).astype(jnp.bfloat16)
    grad_heads = split_heads(grad_attended.reshape(row_count, length, width), head_count)
    grad_prob = jnp.einsum(
        "rqhd,rkhd->rhqk", grad_heads, value_heads, preferred_element_type=jnp.float32
    )
    delta = jnp.sum(probs * grad_prob, axis=-1, keepdims=True)
    dscore = (probs * (grad_prob - delta)).astype(jnp.bfloat16)
    key_heads = split_heads(key_low, head_count)
    query_heads = split_heads(query_low, head_count)

    def joined(heads):
        return heads.reshape(tokens, width).astype(jnp.bfloat16)

    grad_query_low = joined(
        jnp.einsum("rhqk,rkhd->rqhd", dscore, key_heads, preferred_element_type=jnp.float32)
    )
    grad_key_low = joined(
        jnp.einsum("rhqk,rqhd->rkhd", dscore, query_heads, preferred_element_type=jnp.float32)
    )
    grad_value_low = joined(
        jnp.einsum("rhqk,rqhd->rkhd", probs_low, grad_heads, preferred_element_type=jnp.float32)
    )
    score_sum = jnp.sum(dscore, axis=0, dtype=jnp.float32).reshape(head_count, length * length)
    table_grad = lax.dot_general(one_hot, score_sum, (((0,), (1,)), ((), ())), precision=HIGH)
    grad_query_w = outer_sum(normed_one, grad_query_low).astype(jnp.bfloat16)
    grad_key_w = outer_sum(normed_one, grad_key_low).astype(jnp.bfloat16)
    grad_value_w = outer_sum(normed_one, grad_value_low).astype(jnp.bfloat16)
    grad_normed_one = (
        back_dot(grad_query_low, w_query)
        + back_dot(grad_key_low, w_key)
        + back_dot(grad_value_low, w_value)
    )
    norm_first, norm_one_back = jax.vjp(rms_scale, resid_in, gain_one)
    grad_resid_norm, gain_one_grad = norm_one_back(grad_normed_one)
    grad_rows = (grad_mid + grad_resid_norm).astype(jnp.bfloat16)
    layer_out = to_blocks(layer_rows)
    grad_in = to_blocks(grad_rows.reshape(row_count, length, width))

    def share(part):
        piece = lax.psum_scatter(part, "dp", scatter_dimension=0, tiled=True)
        return lax.psum(piece, "seq").astype(jnp.float32)

    small = jnp.concatenate([gain_one_grad, gain_two_grad, table_grad.reshape(-1)])
    small = lax.psum(small, ("dp", "seq"))
    gain_rows = width // lax.axis_size("dp")
    gain_at = lax.axis_index("dp") * gain_rows
    return (
        layer_out,
        grad_in,
        share(grad_query_w),
        share(grad_key_w),
        share(grad_value_w),
        share(grad_attn_out_w),
        share(grad_inner_w),
        share(grad_outer_w),
        lax.dynamic_slice_in_dim(small, gain_at, gain_rows),
        lax.dynamic_slice_in_dim(small, width + gain_at, gain_rows),
        small[2 * width :].reshape(bias_table.shape),
    )


def solution(mesh):
    return jax.shard_map(
        on_device,
        mesh=mesh,
        in_specs=(
            P("dp", "seq", None),
            P("dp"),
            P("dp"),
            P(),
            P(),
            P(),
            P(),
            P(),
            P(),
            P(),
            P(),
            P(),
            P("dp", "seq", None),
        ),
        out_specs=(
            P("dp", "seq", None),
            P("dp", "seq", None),
            P("dp", None),
            P("dp", None),
            P("dp", None),
            P("dp", None),
            P("dp", None),
            P("dp", None),
            P("dp"),
            P("dp"),
            P(),
        ),
        check_vma=False,
    )
```

```python
from functools import partial

import jax
import jax.numpy as jnp
from jax import lax
from jax.experimental import pallas as pl
from jax.experimental.pallas import tpu as pltpu
from jax.sharding import PartitionSpec as P

EPS = 1e-06
NEG = -1000000000.0
LIMITS = (12, 16, 23, 32, 46, 64, 91)
HIGH = lax.Precision.HIGHEST
MESH = pl.DeviceIdType.MESH
BF = jnp.bfloat16
F32 = jnp.float32

GROUP = 8
LANES = 128
WIDE = 256
CHUNKS = 10
SLOTS = 3
CHUNK_ROWS = 768


def dot_nn(left, right):
    return jnp.dot(left, right, preferred_element_type=F32)


def dot_nt(left, right):
    return lax.dot_general(left, right, (((1,), (1,)), ((), ())), preferred_element_type=F32)


def dot_tn(left, right):
    return lax.dot_general(left, right, (((0,), (0,)), ((), ())), preferred_element_type=F32)


def buckets(relative):
    distance = jnp.abs(relative)
    far_bucket = 8 + sum(((distance >= thresh).astype(jnp.int32) for thresh in LIMITS))
    return jnp.where(relative > 0, 16, 0) + jnp.where(distance < 8, distance, far_bucket)


def loop(count, body):
    lax.fori_loop(0, count, lambda index, none: (body(index), none)[1], None)


def at(index, size):
    if isinstance(index, int):
        return pl.ds(index * size, size)
    return pl.ds(pl.multiple_of(index * size, size), size)


def layer_kernel(
    lo_count,
    hidden,
    cot,
    query_len,
    doc_len,
    wq_hbm,
    wk_hbm,
    wv_hbm,
    wo_hbm,
    w1_hbm,
    w2_hbm,
    gain1,
    gain2,
    table,
    layer_out,
    grad_in,
    shares,
    small_out,
    x_row,
    c_row,
    wq,
    wk,
    wv,
    wo,
    w1,
    w2,
    n1,
    q,
    k,
    v,
    probs,
    o,
    n2,
    turned,
    mid,
    acc_a,
    acc_b,
    z,
    du,
    bias,
    vec,
    sums,
    d_three,
    dsc,
    tacc,
    grads,
    r_core,
    r_first,
    r_second,
    z_end,
    z_mid,
    small,
    small_in,
    w_sem,
    own_sem,
    x_send,
    x_recv,
    c_send,
    c_recv,
    y_send,
    y_recv,
    i_send,
    i_recv,
    core_send,
    core_recv,
    first_send,
    first_recv,
    second_send,
    second_recv,
    end_send,
    end_recv,
    mid_send,
    mid_recv,
    back_send,
    back_recv,
    share_sem,
    small_send,
    small_recv,
):
    dp = lax.axis_index("dp")
    sq = lax.axis_index("seq")
    seq_count, block, width = hidden.shape
    length = x_row.shape[0]
    heads = table.shape[1]
    pairs = heads // 2
    head_group = WIDE // LANES
    row_share = width // GROUP
    parts = w1_hbm.shape[1] // (GROUP * LANES)
    part_cols = GROUP * LANES
    vec_len = vec.shape[1]

    high = dp // lo_count
    bit0 = lax.rem(high, 2)
    bit1 = lax.rem(high // 2, 2)
    bit2 = lax.rem(high // 4, 2)
    step1 = 2 * lo_count * (1 - 2 * bit1)
    step2 = 4 * lo_count * (1 - 2 * bit2)
    core_dev = (dp + lo_count * (1 - 2 * bit0), sq)
    first_dev = (dp + (1 - bit0) * step1 + bit0 * step2, sq)
    second_dev = (dp + bit0 * step1 + (1 - bit0) * step2, sq)
    first_bit = (1 - bit0) * bit1 + bit0 * bit2
    second_bit = (1 - bit0) * bit2 + bit0 * bit1
    pair_dev = (dp, sq + 1 - 2 * lax.rem(sq, 2))
    mid_dev = (dp, 3 - sq)
    is_end = jnp.logical_or(sq == 0, sq == seq_count - 1)
    is_mid = jnp.logical_not(is_end)
    row_devs = [lax.rem(sq + step, seq_count) for step in range(1, seq_count)]

    def remote(src, dst, send, recv, device):
        return pltpu.make_async_remote_copy(
            src_ref=src, dst_ref=dst, send_sem=send, recv_sem=recv, device_id=device, device_id_type=MESH
        )

    barrier = pltpu.get_barrier_semaphore()
    for device in [core_dev, first_dev, second_dev] + [(dp, other) for other in row_devs]:
        pl.semaphore_signal(barrier, inc=1, device_id=device, device_id_type=MESH)
    pl.semaphore_wait(barrier, 3 + len(row_devs))

    def deal(src_of, dst_of, send, recv):
        def copy(index):
            other = row_devs[index]
            return remote(src_of(other), dst_of(sq), send.at[index], recv.at[sq], (dp, other))

        def start():
            for index in range(len(row_devs)):
                copy(index).start()

        def arrived(other):
            remote(src_of(other), dst_of(other), send.at[0], recv.at[other], (dp, other)).wait_recv()

        def sent():
            for index in range(len(row_devs)):
                copy(index).wait_send()

        return start, arrived, sent

    x_start, x_arrived, x_sent = deal(
        lambda other: hidden.at[other], lambda src: x_row.at[at(src, block)], x_send, x_recv
    )
    c_start, c_arrived, c_sent = deal(
        lambda other: cot.at[other], lambda src: c_row.at[at(src, block)], c_send, c_recv
    )
    y_start, y_arrived, y_sent = deal(
        lambda other: z.at[at(other, block), pl.ds(0, width)], lambda src: layer_out.at[src], y_send, y_recv
    )
    i_start, i_arrived, i_sent = deal(
        lambda other: n2.at[at(other, block)], lambda src: grad_in.at[src], i_send, i_recv
    )
    own_x = pltpu.make_async_copy(hidden.at[sq], x_row.at[at(sq, block)], own_sem.at[0])
    own_c = pltpu.make_async_copy(cot.at[sq], c_row.at[at(sq, block)], own_sem.at[1])
    own_y = pltpu.make_async_copy(z.at[at(sq, block), pl.ds(0, width)], layer_out.at[sq], own_sem.at[2])
    own_i = pltpu.make_async_copy(n2.at[at(sq, block)], grad_in.at[sq], own_sem.at[3])

    x_start()
    own_x.start()
    square = [
        pltpu.make_async_copy(src, dst, w_sem.at[index])
        for index, (src, dst) in enumerate(((wq_hbm, wq), (wk_hbm, wk), (wv_hbm, wv), (wo_hbm, wo)))
    ]
    for copy in square:
        copy.start()

    def part_copies(part):
        slot = part % 2
        span = parts * LANES
        copies = []
        for share in range(GROUP):
            place = pl.ds(share * span + part * LANES, LANES)
            cols = pl.ds(share * LANES, LANES)
            copies.append(pltpu.make_async_copy(w1_hbm.at[:, place], w1.at[slot, :, cols], w_sem.at[4 + 2 * part]))
            copies.append(pltpu.make_async_copy(w2_hbm.at[place], w2.at[slot, cols], w_sem.at[5 + 2 * part]))
        return copies

    def part_wait(part):
        slot = part % 2
        pltpu.make_async_copy(w1.at[slot], w1.at[slot], w_sem.at[4 + 2 * part]).wait()
        pltpu.make_async_copy(w2.at[slot], w2.at[slot], w_sem.at[5 + 2 * part]).wait()

    for part in range(2):
        for copy in part_copies(part):
            copy.start()
    own_c.start()

    def rows_of(chunk):
        return CHUNK_ROWS if chunk < 2 * parts else 6 * row_share

    def piece(ref, *index):
        chunk = index[0]
        return ref.at[index + (slice(None),) * (len(ref.shape) - 2 - len(index)) + (pl.ds(0, rows_of(chunk)),)]

    def grad_half(chunk, side):
        return grads.at[chunk % SLOTS, side, :, :, pl.ds(0, rows_of(chunk))]

    def core_copy(chunk):
        return remote(
            grad_half(chunk, 1 - bit0), piece(r_core, chunk), core_send.at[chunk], core_recv.at[chunk], core_dev
        )

    def first_copy(chunk):
        return remote(
            piece(r_core, chunk, 1 - first_bit),
            piece(r_first, chunk),
            first_send.at[chunk],
            first_recv.at[chunk],
            first_dev,
        )

    def second_copy(chunk):
        return remote(
            piece(r_first, chunk, 1 - second_bit),
            piece(r_second, chunk),
            second_send.at[chunk],
            second_recv.at[chunk],
            second_dev,
        )

    def end_copy(chunk):
        return remote(
            piece(r_second, chunk), piece(z_end, chunk), end_send.at[chunk], end_recv.at[chunk], pair_dev
        )

    def mid_copy(chunk):
        return remote(
            piece(r_second, chunk), piece(z_mid, chunk), mid_send.at[chunk], mid_recv.at[chunk], mid_dev
        )

    def back_copy(chunk):
        return remote(
            piece(z_end, chunk), piece(shares, chunk), back_send.at[chunk], back_recv.at[chunk], pair_dev
        )

    def share_copy(chunk):
        return pltpu.make_async_copy(piece(z_end, chunk), piece(shares, chunk), share_sem.at[chunk])

    def core_done(chunk):
        copy = core_copy(chunk)
        copy.wait_recv()
        rows = pl.ds(0, rows_of(chunk))

        def add(index):
            one, two = index // 2, lax.rem(index, 2)
            r_core[chunk, one, two, rows] += grads[chunk % SLOTS, bit0, one, two, rows]

        loop(4, add)
        first_copy(chunk).start()
        copy.wait_send()

    def first_done(chunk):
        first_copy(chunk).wait_recv()
        rows = pl.ds(0, rows_of(chunk))

        def add(index):
            r_first[chunk, index, rows] += r_core[chunk, first_bit, index, rows]

        loop(2, add)
        second_copy(chunk).start()

    def second_done(chunk):
        second_copy(chunk).wait_recv()
        rows = pl.ds(0, rows_of(chunk))
        r_second[chunk, rows] += r_first[chunk, second_bit, rows]

        @pl.when(is_end)
        def _():
            end_copy(chunk).start()

    def end_done(chunk):
        rows = pl.ds(0, rows_of(chunk))

        @pl.when(is_mid)
        def _():
            end_copy(chunk).wait_recv()
            r_second[chunk, rows] += z_end[chunk, rows]
            mid_copy(chunk).start()

    def mid_done(chunk):
        rows = pl.ds(0, rows_of(chunk))

        @pl.when(is_mid)
        def _():
            mid_copy(chunk).wait_recv()
            z_end[chunk, rows] = r_second[chunk, rows] + z_mid[chunk, rows]
            back_copy(chunk).start()
            share_copy(chunk).start()

    def back_done(chunk):
        @pl.when(is_end)
        def _():
            back_copy(chunk).wait_recv()

    stages = (core_done, first_done, second_done, end_done, mid_done, back_done)

    def settle():
        for chunk in range(CHUNKS):
            first_copy(chunk).wait_send()
            second_copy(chunk).wait_send()

        @pl.when(is_end)
        def _():
            for chunk in range(CHUNKS):
                end_copy(chunk).wait_send()

        @pl.when(is_mid)
        def _():
            for chunk in range(CHUNKS):
                mid_copy(chunk).wait_send()
                back_copy(chunk).wait_send()
                share_copy(chunk).wait()

    def tick(spot):
        for stage, chunk in PLAN.get(spot, ()):
            stages[stage](chunk)

    def place_of(share):
        one, two, three = share % 2, (share // 2) % 2, share // 4
        return (one, two, three) if one == 0 else (one, three, two)

    distance = lax.broadcasted_iota(jnp.int32, (1, vec_len), 1) - vec_len // 2
    bucket_row = buckets(distance)
    bucket_count = table.shape[0]
    one_hot = (
        jnp.broadcast_to(bucket_row, (bucket_count, vec_len))
        == lax.broadcasted_iota(jnp.int32, (bucket_count, vec_len), 0)
    ).astype(F32)
    vec[pl.ds(0, heads), :] = dot_tn(table[...], one_hot.astype(BF))
    sub = lax.broadcasted_iota(jnp.int32, (8, vec_len), 0)

    def build_bias(head):
        rows = jnp.broadcast_to(vec[pl.ds(head, 1), :], (8, vec_len))
        for shift in (1, 2, 4):
            rows = jnp.where((sub & shift) != 0, pltpu.roll(rows, shift, 1), rows)
        shift = 8
        while shift < block:
            rows = jnp.concatenate([rows, pltpu.roll(rows, shift, 1)], axis=0)
            shift *= 2
        bias[head] = rows.astype(BF)

    loop(heads, build_bias)

    total_len = query_len[sq] + doc_len[sq]
    key_mask = jnp.where(
        lax.broadcasted_iota(jnp.int32, (1, length), 1) < total_len, jnp.float32(0), jnp.float32(NEG)
    )
    low_lanes = lax.broadcasted_iota(jnp.int32, (1, LANES), 1) < LANES // 2

    def half_of(values, half):
        keep = low_lanes if half == 0 else jnp.logical_not(low_lanes)
        return jnp.where(keep, values, jnp.zeros_like(values))

    gain_one = gain1[...].astype(F32)
    gain_two = gain2[...].astype(F32)

    own_x.wait()
    for other in row_devs:
        x_arrived(other)
    c_start()

    def norm_first(index):
        rows = at(index, block)
        values = x_row[rows, :].astype(F32)
        factor = lax.rsqrt(jnp.mean(values * values, axis=-1, keepdims=True) + EPS)
        n1[rows, :] = (values * factor * gain_one).astype(BF)

    loop(seq_count, norm_first)
    for copy in square:
        copy.wait()

    def project(index):
        cols = at(index, WIDE)
        q[:, cols] = dot_nn(n1[...], wq[:, cols]).astype(BF)
        k[:, cols] = dot_nn(n1[...], wk[:, cols]).astype(BF)
        v[:, cols] = dot_nn(n1[...], wv[:, cols]).astype(BF)

    loop(width // WIDE, project)

    def attend(pair):
        cols = at(pair, LANES)
        keys = k[:, cols]
        values = v[:, cols]
        for tile in range(length // WIDE):
            rows = pl.ds(tile * WIDE, WIDE)
            queries = q[rows, cols]
            total = None
            for half in range(2):
                head = 2 * pair + half
                scores = dot_nt(half_of(queries, half), keys)
                weights = []
                for part in range(WIDE // block):
                    start = vec_len // 2 - tile * WIDE - part * block
                    here = scores[part * block : (part + 1) * block]
                    here = here + bias[head, :, pl.ds(start, length)].astype(F32) + key_mask
                    here = jnp.exp(here - jnp.max(here, axis=-1, keepdims=True))
                    scale = 1.0 / jnp.sum(here, axis=-1, keepdims=True)
                    weights.append((here * scale).astype(BF))
                weights = jnp.concatenate(weights, axis=0)
                probs[head, rows, :] = weights
                term = dot_nn(weights, half_of(values, half))
                total = term if total is None else total + term
            o[rows, cols] = total.astype(BF)

    loop(pairs, attend)

    def attn_out(index):
        cols = at(index, WIDE)
        mid[:, cols] = x_row[:, cols].astype(F32) + dot_nn(o[...], wo[:, cols])

    loop(width // WIDE, attn_out)

    def norm_second(index):
        rows = at(index, block)
        values = mid[rows, :]
        factor = lax.rsqrt(jnp.mean(values * values, axis=-1, keepdims=True) + EPS)
        n2[rows, :] = (values * factor * gain_two).astype(BF)

    loop(seq_count, norm_second)

    def turn(source):
        def body(index):
            span = at(index, LANES)
            turned[span, :] = source[:, span].T

        loop(width // LANES, body)

    def put(chunk, values, row_of):
        for share in range(GROUP):
            for side in range(values.shape[1] // LANES):
                one, two, three = place_of(share)
                grads[chunk % SLOTS, one, two, three, pl.ds(row_of(side), row_share), :] = values[
                    share * row_share : (share + 1) * row_share, side * LANES : (side + 1) * LANES
                ].astype(BF)

    turn(n2)
    own_c.wait()
    for other in row_devs:
        c_arrived(other)

    for part in range(parts):
        slot = part % 2
        outer_chunk, inner_chunk = 2 * part, 2 * part + 1
        part_wait(part)

        def hidden_units(index):
            cols = at(index, WIDE)
            inner = dot_nn(n2[...], w1[slot, :, cols])
            back = dot_nt(c_row[...], w2[slot, cols, :])
            square_in = inner * inner
            bend = jnp.tanh(inner * (0.7978845608028654 + (0.7978845608028654 * 0.044715) * square_in))
            half_in = 0.5 * inner
            z[:, cols] = (half_in + half_in * bend).astype(BF)
            slope = 0.7978845608028654 + (3 * 0.7978845608028654 * 0.044715) * square_in
            slope = 0.5 + 0.5 * bend + half_in * (1 - bend * bend) * slope
            du[:, cols] = (back * slope).astype(BF)

        loop(part_cols // WIDE, hidden_units)
        tick(("units", part))

        def outer_tile(index):
            values = dot_tn(z[:, at(index, WIDE)], c_row[...])
            bit_one, bit_two = lax.rem(index, 2), index // 2
            for side in range(2):
                one, two = (bit_one, bit_two) if side == 0 else (bit_two, bit_one)
                for col in range(width // LANES):
                    grads[outer_chunk % SLOTS, side, one, two, pl.ds(col * LANES, LANES), :] = values[
                        side * LANES : (side + 1) * LANES, col * LANES : (col + 1) * LANES
                    ].astype(BF)

        loop(part_cols // WIDE, outer_tile)
        core_copy(outer_chunk).start()
        tick(("outer", part))

        def inner_tile(index):
            values = dot_nn(turned[...], du[:, at(index, WIDE)])
            put(inner_chunk, values, lambda side: pl.multiple_of((2 * index + side) * row_share, row_share))

        loop(part_cols // WIDE, inner_tile)
        core_copy(inner_chunk).start()
        tick(("inner", part))

        def add_up(index):
            cols = at(index, WIDE)
            term = dot_nn(z[...], w2[slot, :, cols])
            back = dot_nt(du[...], w1[slot, cols, :])
            if part == 0:
                acc_a[:, cols] = term
                acc_b[:, cols] = back
            else:
                acc_a[:, cols] += term
                acc_b[:, cols] += back

        loop(width // WIDE, add_up)
        if part + 2 < parts:
            for copy in part_copies(part + 2):
                copy.start()
        tick(("sums", part))

    sums[...] = jnp.zeros_like(sums)

    def back_second(index):
        rows = at(index, block)
        values = mid[rows, :]
        back = acc_b[rows, :]
        z[rows, pl.ds(0, width)] = (values + acc_a[rows, :]).astype(BF)
        factor = lax.rsqrt(jnp.mean(values * values, axis=-1, keepdims=True) + EPS)
        sums[1:2, :] += jnp.sum(back * values * factor, axis=0, keepdims=True)
        scaled = back * gain_two
        inside = jnp.mean(scaled * values, axis=-1, keepdims=True)
        total = c_row[rows, :].astype(F32) + factor * scaled - values * (factor * factor * factor * inside)
        acc_b[rows, :] = total
        n2[rows, :] = total.astype(BF)

    loop(seq_count, back_second)
    y_start()
    own_y.start()
    turn(o)
    attn_chunk = 2 * parts

    def attn_out_tile(index):
        cols = at(index, WIDE)
        values = dot_nn(turned[...], n2[:, cols])
        put(attn_chunk, values, lambda side: pl.multiple_of((2 * index + side) * row_share, row_share))
        c_row[:, cols] = dot_nt(n2[...], wo[cols, :]).astype(BF)

    loop(width // WIDE, attn_out_tile)
    core_copy(attn_chunk).start()
    turn(n1)
    tick(("attn_out", 0))

    def attend_back(group, inside):
        pair = group * head_group + inside
        cols = at(pair, LANES)
        keys = k[:, cols]
        values = v[:, cols]
        queries = q[:, cols]
        backs = c_row[:, cols]
        product = backs.astype(F32) * o[:, cols].astype(F32)
        for half in range(2):
            head = 2 * pair + half
            dot_sum = jnp.sum(half_of(product, half), axis=-1, keepdims=True)
            tacc[...] = jnp.zeros_like(tacc)
            for tile in range(length // WIDE):
                rows = pl.ds(tile * WIDE, WIDE)
                back = dot_nt(half_of(backs[tile * WIDE : (tile + 1) * WIDE], half), values)
                for part in range(WIDE // block):
                    base = tile * WIDE + part * block
                    start = vec_len // 2 - base
                    score = probs[head, pl.ds(base, block), :].astype(F32) * (
                        back[part * block : (part + 1) * block] - dot_sum[base : base + block]
                    )
                    tacc[:, pl.ds(start, length)] += score
                    dsc[half, pl.ds(base, block), :] = score.astype(BF)
            rows = tacc[...]
            size = block
            while size > 8:
                size //= 2
                rows = rows[:size] + pltpu.roll(rows[size:], vec_len - size, 1)
            for shift in (4, 2, 1):
                rows = jnp.where((sub & shift) != 0, pltpu.roll(rows, vec_len - shift, 1), rows)
            vec[pl.ds(head, 1), :] = jnp.sum(rows, axis=0, keepdims=True)
        out = at(inside, LANES)
        d_three[0, :, out] = (
            dot_nn(dsc[0], half_of(keys, 0)) + dot_nn(dsc[1], half_of(keys, 1))
        ).astype(BF)
        d_three[1, :, out] = (
            dot_tn(dsc[0], half_of(queries, 0)) + dot_tn(dsc[1], half_of(queries, 1))
        ).astype(BF)
        d_three[2, :, out] = (
            dot_tn(probs[2 * pair], half_of(backs, 0)) + dot_tn(probs[2 * pair + 1], half_of(backs, 1))
        ).astype(BF)

    for group in range(width // WIDE):
        chunk = attn_chunk + 1 + group
        for inside in range(head_group):
            attend_back(group, inside)
            tick(("heads", head_group * group + inside))

        def group_tile(index):
            values = dot_nn(turned[...], d_three[index])
            put(chunk, values, lambda side: pl.multiple_of((2 * index + side) * row_share, row_share))

        loop(3, group_tile)
        core_copy(chunk).start()
        cols = pl.ds(group * WIDE, WIDE)
        term = dot_nt(d_three[0], wq[:, cols]) + dot_nt(d_three[1], wk[:, cols]) + dot_nt(d_three[2], wv[:, cols])
        if group == 0:
            acc_a[...] = term
        else:
            acc_a[...] += term
        tick(("group", group))

    def back_first(index):
        rows = at(index, block)
        values = x_row[rows, :].astype(F32)
        back = acc_a[rows, :]
        factor = lax.rsqrt(jnp.mean(values * values, axis=-1, keepdims=True) + EPS)
        sums[0:1, :] += jnp.sum(back * values * factor, axis=0, keepdims=True)
        scaled = back * gain_one
        inside = jnp.mean(scaled * values, axis=-1, keepdims=True)
        total = acc_b[rows, :] + factor * scaled - values * (factor * factor * factor * inside)
        n2[rows, :] = total.astype(BF)

    loop(seq_count, back_first)
    table_sum = lax.dot_general(
        one_hot,
        vec[pl.ds(0, heads), :],
        (((1,), (1,)), ((), ())),
        precision=HIGH,
        preferred_element_type=F32,
    )
    small[0, pl.ds(0, 8), :] = sums[...]
    small[0, pl.ds(8, bucket_count), :] = jnp.zeros((bucket_count, width), F32)
    small[0, pl.ds(8, bucket_count), pl.ds(0, heads)] = table_sum

    def small_copy(step, device):
        return remote(small.at[step], small_in.at[step], small_send.at[step], small_recv.at[step], device)

    def small_step(step, device):
        copy = small_copy(step, device)
        copy.start()
        return copy

    copy = small_step(0, core_dev)
    i_start()
    own_i.start()
    copy.wait_recv()
    small[1] = small[0] + small_in[0]
    copy = small_step(1, (dp + step1, sq))
    copy.wait_recv()
    small[2] = small[1] + small_in[1]
    copy = small_step(2, (dp + step2, sq))
    copy.wait_recv()
    small[3] = small[2] + small_in[2]
    copy = small_step(3, pair_dev)
    copy.wait_recv()
    small[4] = small[3] + small_in[3]
    copy = small_step(4, (dp, lax.rem(sq + 2, 4)))
    copy.wait_recv()
    small_out[...] = small[4] + small_in[4]
    for step in range(5):
        small_copy(step, core_dev).wait_send()
    tick(("end", 0))
    settle()
    own_y.wait()
    own_i.wait()
    for other in row_devs:
        y_arrived(other)
        i_arrived(other)
    x_sent()
    c_sent()
    y_sent()
    i_sent()


def make_plan():
    spots = []
    for part in range(3):
        spots += [("units", part), ("outer", part), ("inner", part), ("sums", part)]
    spots.append(("attn_out", 0))
    for group in range(3):
        spots += [("heads", 2 * group), ("heads", 2 * group + 1), ("group", group)]
    spots.append(("end", 0))
    cost = {"units": 2.5, "outer": 1.5, "inner": 1.5, "sums": 2.0, "attn_out": 4.0, "heads": 3.0, "group": 2.0, "end": 4.0}
    made = {("outer", p): 2 * p for p in range(3)}
    made.update({("inner", p): 2 * p + 1 for p in range(3)})
    made.update({("attn_out", 0): 6, ("group", 0): 7, ("group", 1): 8, ("group", 2): 9})
    now, ready, plan = 0.0, {}, {}
    link = 0.0
    for spot in spots:
        now += cost[spot[0]]
        if spot in made:
            chunk = made[spot]
            core = now + 4.0
            link = max(link, core) + 6.5
            ready[chunk] = [core, link + 2.0, link + 6.0, link + 13.0, link + 19.0, link + 25.0]
        plan[spot] = []
        for chunk in sorted(ready):
            while ready[chunk] and (ready[chunk][0] <= now or spot[0] == "end"):
                if spot[0] == "end":
                    break
                ready[chunk].pop(0)
                plan[spot].append((5 - len(ready[chunk]), chunk))
    rest = []
    for chunk in sorted(ready):
        for left, when in enumerate(ready[chunk]):
            rest.append((when, 6 - len(ready[chunk]) + left, chunk))
    plan[("end", 0)] += [(stage, chunk) for when, stage, chunk in sorted(rest)]
    return plan


PLAN = make_plan()


def unpack_kernel(
    parts,
    row_share,
    shares,
    layer_in,
    grad_in_in,
    layer_out,
    grad_in,
    gq,
    gk,
    gv,
    go,
    gi,
    gf,
    sems,
):
    one = pltpu.make_async_copy(layer_in, layer_out, sems.at[0])
    two = pltpu.make_async_copy(grad_in_in, grad_in, sems.at[1])
    one.start()
    two.start()
    blocks = gq.shape[1] // LANES
    for part in range(parts):
        for col in range(blocks):
            gf[pl.ds(part * LANES, LANES), pl.ds(col * LANES, LANES)] = shares[
                2 * part, pl.ds(col * LANES, LANES), :
            ].astype(F32)
        for share in range(GROUP):
            gi[:, pl.ds((share * parts + part) * LANES, LANES)] = shares[
                2 * part + 1, pl.ds(share * row_share, row_share), :
            ].astype(F32)
    for col in range(blocks):
        go[:, pl.ds(col * LANES, LANES)] = shares[2 * parts, pl.ds(col * row_share, row_share), :].astype(F32)
    for group in range(blocks // 2):
        for index, ref in enumerate((gq, gk, gv)):
            for side in range(2):
                ref[:, pl.ds(group * WIDE + side * LANES, LANES)] = shares[
                    2 * parts + 1 + group, pl.ds((2 * index + side) * row_share, row_share), :
                ].astype(F32)
    one.wait()
    two.wait()


def on_device(
    dp_count,
    hidden_in,
    query_lengths,
    doc_lengths,
    w_query,
    w_key,
    w_value,
    w_attn_out,
    w_inner,
    w_outer,
    gain_attn,
    gain_ffn,
    bias_table,
    cotangent,
):
    rows, block, width = hidden_in.shape
    length = rows * block
    heads = bias_table.shape[1]
    ffn = w_inner.shape[1]
    part_cols = GROUP * LANES
    parts = ffn // part_cols
    vec_len = 2 * length
    lo_count = dp_count // GROUP
    row_share = width // GROUP

    def vm(*shape, dtype=BF):
        return pltpu.VMEM(shape, dtype)

    def dma(count):
        return pltpu.SemaphoreType.DMA((count,))

    hbm = pl.BlockSpec(memory_space=pl.ANY)
    vmem = pl.BlockSpec(memory_space=pltpu.VMEM)
    smem = pl.BlockSpec(memory_space=pltpu.SMEM)
    small_rows = 8 + bias_table.shape[0]
    layer_raw, grad_raw, shares, small = pl.pallas_call(
        partial(layer_kernel, lo_count),
        out_shape=(
            jax.ShapeDtypeStruct(hidden_in.shape, BF),
            jax.ShapeDtypeStruct(hidden_in.shape, BF),
            jax.ShapeDtypeStruct((CHUNKS, CHUNK_ROWS, LANES), BF),
            jax.ShapeDtypeStruct((small_rows, width), F32),
        ),
        in_specs=[hbm, hbm, smem, smem] + [hbm] * 6 + [vmem] * 3,
        out_specs=(hbm, hbm, hbm, vmem),
        scratch_shapes=[
            vm(length, width),
            vm(length, width),
            vm(width, width),
            vm(width, width),
            vm(width, width),
            vm(width, width),
            vm(2, width, part_cols),
            vm(2, part_cols, width),
            vm(length, width),
            vm(length, width),
            vm(length, width),
            vm(length, width),
            vm(heads, length, length),
            vm(length, width),
            vm(length, width),
            vm(width, length),
            vm(length, width, dtype=F32),
            vm(length, width, dtype=F32),
            vm(length, width, dtype=F32),
            vm(length, part_cols),
            vm(length, part_cols),
            vm(heads, block, vec_len),
            vm(16, vec_len, dtype=F32),
            vm(8, width, dtype=F32),
            vm(3, length, WIDE),
            vm(2, length, length),
            vm(block, vec_len, dtype=F32),
            vm(SLOTS, 2, 2, 2, CHUNK_ROWS, LANES),
            vm(CHUNKS, 2, 2, CHUNK_ROWS, LANES),
            vm(CHUNKS, 2, CHUNK_ROWS, LANES),
            vm(CHUNKS, CHUNK_ROWS, LANES),
            vm(CHUNKS, CHUNK_ROWS, LANES),
            vm(CHUNKS, CHUNK_ROWS, LANES),
            vm(5, small_rows, width, dtype=F32),
            vm(5, small_rows, width, dtype=F32),
            dma(4 + 2 * parts),
            dma(4),
        ]
        + [dma(rows)] * 8
        + [dma(CHUNKS)] * 13
        + [dma(5)] * 2,
        compiler_params=pltpu.CompilerParams(
            collective_id=0, has_side_effects=True, vmem_limit_bytes=64 * 2**20 - 2**19
        ),
    )(
        hidden_in,
        cotangent,
        query_lengths,
        doc_lengths,
        w_query,
        w_key,
        w_value,
        w_attn_out,
        w_inner,
        w_outer,
        gain_attn.reshape(1, width),
        gain_ffn.reshape(1, width),
        bias_table,
    )
    square = jax.ShapeDtypeStruct((row_share, width), F32)
    layer_out, grad_in, *grads = pl.pallas_call(
        partial(unpack_kernel, parts, row_share),
        out_shape=(
            jax.ShapeDtypeStruct(hidden_in.shape, BF),
            jax.ShapeDtypeStruct(hidden_in.shape, BF),
            square,
            square,
            square,
            square,
            jax.ShapeDtypeStruct((row_share, ffn), F32),
            jax.ShapeDtypeStruct((ffn // GROUP, width), F32),
        ),
        in_specs=[vmem, hbm, hbm],
        out_specs=(hbm, hbm) + (vmem,) * 6,
        scratch_shapes=[dma(2)],
        compiler_params=pltpu.CompilerParams(vmem_limit_bytes=32 * 2**20),
    )(shares, layer_raw, grad_raw)
    if lo_count > 1:
        high = lax.axis_index("dp") // lo_count

        def spread(part):
            whole = jnp.zeros((GROUP,) + part.shape, F32)
            whole = lax.dynamic_update_index_in_dim(whole, part, high, 0)
            whole = whole.reshape((GROUP * part.shape[0],) + part.shape[1:])
            return lax.psum_scatter(whole, "dp", scatter_dimension=0, tiled=True)

        grads = [spread(part) for part in grads]
        small = lax.psum(small, "dp") / GROUP
    gain_rows = width // dp_count
    gains = lax.dynamic_slice_in_dim(small[:2], lax.axis_index("dp") * gain_rows, gain_rows, axis=1)
    return (layer_out, grad_in, *grads, gains[0], gains[1], small[8:, :heads])


def solution(mesh):
    return jax.shard_map(
        partial(on_device, mesh.shape["dp"]),
        mesh=mesh,
        in_specs=(
            P("dp", "seq", None),
            P("dp"),
            P("dp"),
            P(),
            P(),
            P(),
            P(),
            P(),
            P(),
            P(),
            P(),
            P(),
            P("dp", "seq", None),
        ),
        out_specs=(
            P("dp", "seq", None),
            P("dp", "seq", None),
            P("dp", None),
            P("dp", None),
            P("dp", None),
            P("dp", None),
            P("dp", None),
            P("dp", None),
            P("dp"),
            P("dp"),
            P(),
        ),
        check_vma=False,
    )
```

```python
from functools import partial

import jax
import jax.numpy as jnp
from jax import lax
from jax.experimental import pallas as pl
from jax.experimental.pallas import tpu as pltpu
from jax.sharding import PartitionSpec as P

EPS = 1e-06
NEG = -1000000000.0
LIMITS = (12, 16, 23, 32, 46, 64, 91)
HIGH = lax.Precision.HIGHEST
MESH = pl.DeviceIdType.MESH
BF = jnp.bfloat16
F32 = jnp.float32

GROUP = 8
LANES = 128
WIDE = 256
SLOTS = 6
OUTER_SPLIT = ((2, 1), (2, 1), (2, 1))
INNER_SPLIT = ((2, 2), (2, 2), (2, 2))
ATTN_SPLIT = (2, 1)
GROUP_SPLIT = ((2, 1), (2, 1), (2, 1))


def chunk_rows(row_share):
    rows = []
    for outer, inner in zip(OUTER_SPLIT, INNER_SPLIT):
        rows += [count * 2 * LANES for count in outer] + [count * 2 * row_share for count in inner]
    for split in (ATTN_SPLIT,) + GROUP_SPLIT:
        rows += [count * 2 * row_share for count in split]
    return rows


CHUNKS = len(chunk_rows(96))


def dot_nn(left, right):
    return jnp.dot(left, right, preferred_element_type=F32)


def dot_nt(left, right):
    return lax.dot_general(left, right, (((1,), (1,)), ((), ())), preferred_element_type=F32)


def dot_tn(left, right):
    return lax.dot_general(left, right, (((0,), (0,)), ((), ())), preferred_element_type=F32)


def buckets(relative):
    distance = jnp.abs(relative)
    far_bucket = 8 + sum(((distance >= thresh).astype(jnp.int32) for thresh in LIMITS))
    return jnp.where(relative > 0, 16, 0) + jnp.where(distance < 8, distance, far_bucket)


def loop(count, body):
    lax.fori_loop(0, count, lambda index, none: (body(index), none)[1], None)


def at(index, size):
    if isinstance(index, int):
        return pl.ds(index * size, size)
    return pl.ds(pl.multiple_of(index * size, size), size)


def layer_kernel(
    lo_count,
    hidden,
    cot,
    query_len,
    doc_len,
    wq_hbm,
    wk_hbm,
    wv_hbm,
    wo_hbm,
    w1_hbm,
    w2_hbm,
    gain1_hbm,
    gain2_hbm,
    table_hbm,
    layer_out,
    grad_in,
    shares,
    small_out,
    x_row,
    c_row,
    wq,
    wk,
    wv,
    wo,
    w1,
    w2,
    n1,
    q,
    k,
    v,
    probs,
    o,
    n2,
    gain1,
    gain2,
    table,
    z_turned,
    turned,
    mid,
    acc_a,
    acc_b,
    z,
    du,
    bias,
    vec,
    sums,
    d_three,
    dsc,
    tacc,
    grads,
    r_core,
    r_first,
    r_second,
    z_end,
    z_mid,
    small,
    small_in,
    w_sem,
    own_sem,
    x_send,
    x_recv,
    c_send,
    c_recv,
    y_send,
    y_recv,
    i_send,
    i_recv,
    core_send,
    core_recv,
    first_send,
    first_recv,
    second_send,
    second_recv,
    end_send,
    end_recv,
    mid_send,
    mid_recv,
    back_send,
    back_recv,
    share_sem,
    small_send,
    small_recv,
):
    dp = lax.axis_index("dp")
    sq = lax.axis_index("seq")
    seq_count, block, width = hidden.shape
    length = x_row.shape[0]
    heads, bucket_count = table.shape
    pairs = heads // 2
    head_group = WIDE // LANES
    row_share = width // GROUP
    parts = w1_hbm.shape[1] // (GROUP * LANES)
    part_cols = GROUP * LANES
    vec_len = vec.shape[1]

    high = dp // lo_count
    bit0 = lax.rem(high, 2)
    bit1 = lax.rem(high // 2, 2)
    bit2 = lax.rem(high // 4, 2)
    step1 = 2 * lo_count * (1 - 2 * bit1)
    step2 = 4 * lo_count * (1 - 2 * bit2)
    core_dev = (dp + lo_count * (1 - 2 * bit0), sq)
    first_dev = (dp + (1 - bit0) * step1 + bit0 * step2, sq)
    second_dev = (dp + bit0 * step1 + (1 - bit0) * step2, sq)
    first_bit = (1 - bit0) * bit1 + bit0 * bit2
    second_bit = (1 - bit0) * bit2 + bit0 * bit1
    pair_dev = (dp, sq + 1 - 2 * lax.rem(sq, 2))
    mid_dev = (dp, 3 - sq)
    is_end = jnp.logical_or(sq == 0, sq == seq_count - 1)
    is_mid = jnp.logical_not(is_end)
    row_devs = [lax.rem(sq + step, seq_count) for step in range(1, seq_count)]

    def remote(src, dst, send, recv, device):
        return pltpu.make_async_remote_copy(
            src_ref=src, dst_ref=dst, send_sem=send, recv_sem=recv, device_id=device, device_id_type=MESH
        )

    barrier = pltpu.get_barrier_semaphore()
    for device in [core_dev, first_dev, second_dev] + [(dp, other) for other in row_devs]:
        pl.semaphore_signal(barrier, inc=1, device_id=device, device_id_type=MESH)
    pl.semaphore_wait(barrier, 3 + len(row_devs))

    def deal(src_of, dst_of, send, recv):
        def copy(index):
            other = row_devs[index]
            return remote(src_of(other), dst_of(sq), send.at[index], recv.at[sq], (dp, other))

        def start(index):
            copy(index).start()

        def arrived(other):
            remote(src_of(other), dst_of(other), send.at[0], recv.at[other], (dp, other)).wait_recv()

        def sent():
            for index in range(len(row_devs)):
                copy(index).wait_send()

        return start, arrived, sent

    x_start, x_arrived, x_sent = deal(
        lambda other: hidden.at[other], lambda src: x_row.at[at(src, block)], x_send, x_recv
    )
    c_start, c_arrived, c_sent = deal(
        lambda other: cot.at[other], lambda src: c_row.at[at(src, block)], c_send, c_recv
    )
    y_start, y_arrived, y_sent = deal(
        lambda other: z.at[at(other, block), pl.ds(0, width)], lambda src: layer_out.at[src], y_send, y_recv
    )
    i_start, i_arrived, i_sent = deal(
        lambda other: n2.at[at(other, block)], lambda src: grad_in.at[src], i_send, i_recv
    )
    own_x = pltpu.make_async_copy(hidden.at[sq], x_row.at[at(sq, block)], own_sem.at[0])
    own_c = pltpu.make_async_copy(cot.at[sq], c_row.at[at(sq, block)], own_sem.at[1])
    own_y = pltpu.make_async_copy(z.at[at(sq, block), pl.ds(0, width)], layer_out.at[sq], own_sem.at[2])
    own_i = pltpu.make_async_copy(n2.at[at(sq, block)], grad_in.at[sq], own_sem.at[3])

    for index in range(len(row_devs)):
        x_start(index)
    own_x.start()
    params = [
        pltpu.make_async_copy(src, dst, own_sem.at[4 + index])
        for index, (src, dst) in enumerate(((gain1_hbm, gain1), (gain2_hbm, gain2), (table_hbm, table)))
    ]
    for copy in params:
        copy.start()
    square = [
        pltpu.make_async_copy(src, dst, w_sem.at[index])
        for index, (src, dst) in enumerate(((wq_hbm, wq), (wk_hbm, wk), (wv_hbm, wv), (wo_hbm, wo)))
    ]
    for copy in square:
        copy.start()

    def part_copies(part):
        slot = part % 2
        span = parts * LANES
        copies = []
        for share in range(GROUP):
            place = pl.ds(share * span + part * LANES, LANES)
            cols = pl.ds(share * LANES, LANES)
            copies.append(pltpu.make_async_copy(w1_hbm.at[:, place], w1.at[slot, :, cols], w_sem.at[4 + 2 * part]))
            copies.append(pltpu.make_async_copy(w2_hbm.at[place], w2.at[slot, cols], w_sem.at[5 + 2 * part]))
        return copies

    def part_wait(part):
        slot = part % 2
        pltpu.make_async_copy(w1.at[slot], w1.at[slot], w_sem.at[4 + 2 * part]).wait()
        pltpu.make_async_copy(w2.at[slot], w2.at[slot], w_sem.at[5 + 2 * part]).wait()

    for part in range(2):
        for copy in part_copies(part):
            copy.start()
    own_c.start()

    sizes = chunk_rows(row_share)

    def span(chunk):
        return pl.ds(sum(sizes[:chunk]), sizes[chunk])

    def piece(ref, chunk, *index):
        lead = index + (slice(None),) * (len(ref.shape) - 2 - len(index))
        return ref.at[lead + (span(chunk),)]

    def grad_half(chunk, side):
        return grads.at[chunk % SLOTS, side, :, :, pl.ds(0, sizes[chunk])]

    def core_copy(chunk):
        return remote(
            grad_half(chunk, 1 - bit0), piece(r_core, chunk), core_send.at[chunk], core_recv.at[chunk], core_dev
        )

    def first_copy(chunk):
        return remote(
            piece(r_core, chunk, 1 - first_bit),
            piece(r_first, chunk),
            first_send.at[chunk],
            first_recv.at[chunk],
            first_dev,
        )

    def second_copy(chunk):
        return remote(
            piece(r_first, chunk, 1 - second_bit),
            piece(r_second, chunk),
            second_send.at[chunk],
            second_recv.at[chunk],
            second_dev,
        )

    def end_copy(chunk):
        return remote(
            piece(r_second, chunk), piece(z_end, chunk), end_send.at[chunk], end_recv.at[chunk], pair_dev
        )

    def mid_copy(chunk):
        return remote(
            piece(r_second, chunk), piece(z_mid, chunk), mid_send.at[chunk], mid_recv.at[chunk], mid_dev
        )

    def back_copy(chunk):
        return remote(
            piece(z_end, chunk), piece(shares, chunk), back_send.at[chunk], back_recv.at[chunk], pair_dev
        )

    def share_copy(chunk):
        return pltpu.make_async_copy(piece(z_end, chunk), piece(shares, chunk), share_sem.at[chunk])

    def core_done(chunk):
        copy = core_copy(chunk)
        copy.wait_recv()
        for one in range(2):
            for two in range(2):
                r_core[one, two, span(chunk)] += grads[chunk % SLOTS, bit0, one, two, pl.ds(0, sizes[chunk])]
        first_copy(chunk).start()
        copy.wait_send()

    def first_done(chunk):
        first_copy(chunk).wait_recv()
        for one in range(2):
            r_first[one, span(chunk)] += r_core[first_bit, one, span(chunk)]
        second_copy(chunk).start()

    def second_done(chunk):
        second_copy(chunk).wait_recv()
        r_second[span(chunk)] += r_first[second_bit, span(chunk)]

        @pl.when(is_end)
        def _():
            end_copy(chunk).start()

    def end_done(chunk):
        @pl.when(is_mid)
        def _():
            end_copy(chunk).wait_recv()
            r_second[span(chunk)] += z_end[span(chunk)]
            mid_copy(chunk).start()

    def mid_done(chunk):
        @pl.when(is_mid)
        def _():
            mid_copy(chunk).wait_recv()
            z_end[span(chunk)] = r_second[span(chunk)] + z_mid[span(chunk)]
            back_copy(chunk).start()
            share_copy(chunk).start()

    def back_done(chunk):
        @pl.when(is_end)
        def _():
            back_copy(chunk).wait_recv()

    stages = (core_done, first_done, second_done, end_done, mid_done, back_done)

    def settle():
        for chunk in range(CHUNKS):
            first_copy(chunk).wait_send()
            second_copy(chunk).wait_send()

        @pl.when(is_end)
        def _():
            for chunk in range(CHUNKS):
                end_copy(chunk).wait_send()

        @pl.when(is_mid)
        def _():
            for chunk in range(CHUNKS):
                mid_copy(chunk).wait_send()
                back_copy(chunk).wait_send()
                share_copy(chunk).wait()

    def small_copy(step):
        device = (core_dev, (dp + step1, sq), (dp + step2, sq), pair_dev, (dp, lax.rem(sq + 2, 4)))[step]
        return remote(small.at[step], small_in.at[step], small_send.at[step], small_recv.at[step], device)

    def small_done(step):
        small_copy(step).wait_recv()
        if step < 4:
            small[step + 1] = small[step] + small_in[step]
            small_copy(step + 1).start()
        else:
            small_out[...] = small[step] + small_in[step]

    def tick(spot):
        for what, index in PLAN.get(spot, ()):
            if what == "y":
                y_start(index)
            elif what == "i":
                i_start(index)
            elif what == "s":
                small_done(index)
            else:
                stages[what](index)

    def tiles(split, first, kind, part, body):
        done = 0
        for place, count in enumerate(split):
            chunk = first + place
            if count == 1:
                body(chunk, done, 0)
            else:
                loop(count, lambda index: body(chunk, done + index, index))
            core_copy(chunk).start()
            tick((kind, part, place))
            done += count
        return first + len(split)

    def halves(count, kind, part, body):
        for place in range(2):
            loop(count // 2, lambda index: body(place * (count // 2) + index))
            tick((kind, part, place))

    def place_of(share):
        one, two, three = share % 2, (share // 2) % 2, share // 4
        return (one, two, three) if one == 0 else (one, three, two)

    for copy in params:
        copy.wait()
    distance = lax.broadcasted_iota(jnp.int32, (1, vec_len), 1) - vec_len // 2
    bucket_row = buckets(distance)
    one_hot = (
        jnp.broadcast_to(bucket_row, (bucket_count, vec_len))
        == lax.broadcasted_iota(jnp.int32, (bucket_count, vec_len), 0)
    ).astype(F32)
    vec[pl.ds(0, heads), :] = dot_nn(table[...], one_hot.astype(BF))
    sub = lax.broadcasted_iota(jnp.int32, (8, vec_len), 0)

    def build_bias(head):
        rows = jnp.broadcast_to(vec[pl.ds(head, 1), :], (8, vec_len))
        for shift in (1, 2, 4):
            rows = jnp.where((sub & shift) != 0, pltpu.roll(rows, shift, 1), rows)
        shift = 8
        while shift < block:
            rows = jnp.concatenate([rows, pltpu.roll(rows, shift, 1)], axis=0)
            shift *= 2
        bias[head] = rows.astype(BF)

    loop(heads, build_bias)

    total_len = query_len[sq] + doc_len[sq]
    key_mask = jnp.where(
        lax.broadcasted_iota(jnp.int32, (1, length), 1) < total_len, jnp.float32(0), jnp.float32(NEG)
    )
    low_lanes = lax.broadcasted_iota(jnp.int32, (1, LANES), 1) < LANES // 2

    def half_of(values, half):
        keep = low_lanes if half == 0 else jnp.logical_not(low_lanes)
        return jnp.where(keep, values, jnp.zeros_like(values))

    gain_one = gain1[...].astype(F32).reshape(1, width)
    gain_two = gain2[...].astype(F32).reshape(1, width)

    own_x.wait()
    for other in row_devs:
        x_arrived(other)
    for index in range(len(row_devs)):
        c_start(index)

    def norm_first(index):
        rows = at(index, block)
        values = x_row[rows, :].astype(F32)
        factor = lax.rsqrt(jnp.mean(values * values, axis=-1, keepdims=True) + EPS)
        n1[rows, :] = (values * factor * gain_one).astype(BF)

    loop(seq_count, norm_first)
    for copy in square:
        copy.wait()

    def project(index):
        cols = at(index, WIDE)
        q[:, cols] = dot_nn(n1[...], wq[:, cols]).astype(BF)
        k[:, cols] = dot_nn(n1[...], wk[:, cols]).astype(BF)
        v[:, cols] = dot_nn(n1[...], wv[:, cols]).astype(BF)

    loop(width // WIDE, project)

    def attend(pair):
        cols = at(pair, LANES)
        keys = k[:, cols]
        values = v[:, cols]
        for tile in range(length // WIDE):
            rows = pl.ds(tile * WIDE, WIDE)
            queries = q[rows, cols]
            total = None
            for half in range(2):
                head = 2 * pair + half
                scores = dot_nt(half_of(queries, half), keys)
                weights = []
                for part in range(WIDE // block):
                    start = vec_len // 2 - tile * WIDE - part * block
                    here = scores[part * block : (part + 1) * block]
                    here = here + bias[head, :, pl.ds(start, length)].astype(F32) + key_mask
                    here = jnp.exp(here - jnp.max(here, axis=-1, keepdims=True))
                    scale = 1.0 / jnp.sum(here, axis=-1, keepdims=True)
                    weights.append((here * scale).astype(BF))
                weights = jnp.concatenate(weights, axis=0)
                probs[head, rows, :] = weights
                term = dot_nn(weights, half_of(values, half))
                total = term if total is None else total + term
            o[rows, cols] = total.astype(BF)

    loop(pairs, attend)

    def attn_out(index):
        cols = at(index, WIDE)
        mid[:, cols] = x_row[:, cols].astype(F32) + dot_nn(o[...], wo[:, cols])

    loop(width // WIDE, attn_out)

    def norm_second(index):
        rows = at(index, block)
        values = mid[rows, :]
        factor = lax.rsqrt(jnp.mean(values * values, axis=-1, keepdims=True) + EPS)
        n2[rows, :] = (values * factor * gain_two).astype(BF)

    loop(seq_count, norm_second)

    def turn(source):
        def body(index):
            span = at(index, LANES)
            turned[span, :] = source[:, span].T

        loop(width // LANES, body)

    def put(chunk, values, tile):
        rows = values.shape[0] // GROUP
        for share in range(GROUP):
            for side in range(2):
                one, two, three = place_of(share)
                place = (2 * tile + side) * rows
                if not isinstance(tile, int):
                    place = pl.multiple_of(place, rows)
                grads[chunk % SLOTS, one, two, three, pl.ds(place, rows), :] = values[
                    share * rows : (share + 1) * rows, side * LANES : (side + 1) * LANES
                ].astype(BF)

    turn(n2)
    own_c.wait()
    for other in row_devs:
        c_arrived(other)

    chunk = 0
    for part in range(parts):
        slot = part % 2
        part_wait(part)

        def hidden_units(index):
            cols = at(index, WIDE)
            inner = dot_nn(n2[...], w1[slot, :, cols])
            back = dot_nt(c_row[...], w2[slot, cols, :])
            square_in = inner * inner
            bend = jnp.tanh(inner * (0.7978845608028654 + (0.7978845608028654 * 0.044715) * square_in))
            half_in = 0.5 * inner
            active = (half_in + half_in * bend).astype(BF)
            z[:, cols] = active
            z_turned[cols, :] = active.T
            slope = 0.7978845608028654 + (3 * 0.7978845608028654 * 0.044715) * square_in
            slope = 0.5 + 0.5 * bend + half_in * (1 - bend * bend) * slope
            du[:, cols] = (back * slope).astype(BF)

        halves(part_cols // WIDE, "u", part, hidden_units)

        def outer_tile(chunk, tile, place):
            put(chunk, dot_nn(z_turned[...], c_row[:, at(tile, WIDE)]), place)

        chunk = tiles(OUTER_SPLIT[part], chunk, "o", part, outer_tile)

        def inner_tile(chunk, tile, place):
            put(chunk, dot_nn(turned[...], du[:, at(tile, WIDE)]), place)

        chunk = tiles(INNER_SPLIT[part], chunk, "n", part, inner_tile)

        def add_up(index):
            cols = at(index, WIDE)
            term = dot_nn(z[...], w2[slot, :, cols])
            back = dot_nt(du[...], w1[slot, cols, :])
            if part == 0:
                acc_a[:, cols] = term
                acc_b[:, cols] = back
            else:
                acc_a[:, cols] += term
                acc_b[:, cols] += back

        add_up(0)
        tick(("s", part, 0))
        loop(width // WIDE - 1, lambda index: add_up(index + 1))
        if part + 2 < parts:
            for copy in part_copies(part + 2):
                copy.start()
        tick(("s", part, 1))

    sums[...] = jnp.zeros_like(sums)

    def back_second(index):
        rows = at(index, block)
        values = mid[rows, :]
        back = acc_b[rows, :]
        z[rows, pl.ds(0, width)] = (values + acc_a[rows, :]).astype(BF)
        factor = lax.rsqrt(jnp.mean(values * values, axis=-1, keepdims=True) + EPS)
        sums[1:2, :] += jnp.sum(back * values * factor, axis=0, keepdims=True)
        scaled = back * gain_two
        inside = jnp.mean(scaled * values, axis=-1, keepdims=True)
        total = c_row[rows, :].astype(F32) + factor * scaled - values * (factor * factor * factor * inside)
        acc_b[rows, :] = total
        n2[rows, :] = total.astype(BF)

    loop(seq_count, back_second)
    own_y.start()
    tick(("y", 0, 0))
    turn(o)

    def attn_out_tile(chunk, tile, place):
        cols = at(tile, WIDE)
        put(chunk, dot_nn(turned[...], n2[:, cols]), place)
        c_row[:, cols] = dot_nt(n2[...], wo[cols, :]).astype(BF)

    chunk = tiles(ATTN_SPLIT, chunk, "a", 0, attn_out_tile)
    turn(n1)

    def attend_back(group, inside):
        pair = group * head_group + inside
        cols = at(pair, LANES)
        keys = k[:, cols]
        values = v[:, cols]
        queries = q[:, cols]
        backs = c_row[:, cols]
        product = backs.astype(F32) * o[:, cols].astype(F32)
        for half in range(2):
            head = 2 * pair + half
            dot_sum = jnp.sum(half_of(product, half), axis=-1, keepdims=True)
            tacc[...] = jnp.zeros_like(tacc)
            for tile in range(length // WIDE):
                rows = pl.ds(tile * WIDE, WIDE)
                back = dot_nt(half_of(backs[tile * WIDE : (tile + 1) * WIDE], half), values)
                for part in range(WIDE // block):
                    base = tile * WIDE + part * block
                    start = vec_len // 2 - base
                    score = probs[head, pl.ds(base, block), :].astype(F32) * (
                        back[part * block : (part + 1) * block] - dot_sum[base : base + block]
                    )
                    tacc[:, pl.ds(start, length)] += score
                    dsc[half, pl.ds(base, block), :] = score.astype(BF)
            rows = tacc[...]
            size = block
            while size > 8:
                size //= 2
                rows = rows[:size] + pltpu.roll(rows[size:], vec_len - size, 1)
            for shift in (4, 2, 1):
                rows = jnp.where((sub & shift) != 0, pltpu.roll(rows, vec_len - shift, 1), rows)
            vec[pl.ds(head, 1), :] = jnp.sum(rows, axis=0, keepdims=True)
        out = at(inside, LANES)
        d_three[0, :, out] = (
            dot_nn(dsc[0], half_of(keys, 0)) + dot_nn(dsc[1], half_of(keys, 1))
        ).astype(BF)
        d_three[1, :, out] = (
            dot_tn(dsc[0], half_of(queries, 0)) + dot_tn(dsc[1], half_of(queries, 1))
        ).astype(BF)
        d_three[2, :, out] = (
            dot_tn(probs[2 * pair], half_of(backs, 0)) + dot_tn(probs[2 * pair + 1], half_of(backs, 1))
        ).astype(BF)

    for group in range(width // WIDE):
        for inside in range(head_group):
            attend_back(group, inside)
            tick(("h", head_group * group + inside, 0))

        def group_tile(chunk, tile, place):
            put(chunk, dot_nn(turned[...], d_three[tile]), place)

        chunk = tiles(GROUP_SPLIT[group], chunk, "g", group, group_tile)
        cols = pl.ds(group * WIDE, WIDE)
        term = dot_nt(d_three[0], wq[:, cols]) + dot_nt(d_three[1], wk[:, cols]) + dot_nt(d_three[2], wv[:, cols])
        if group == 0:
            acc_a[...] = term
        else:
            acc_a[...] += term
        tick(("d", group, 0))

    def back_first(index):
        rows = at(index, block)
        values = x_row[rows, :].astype(F32)
        back = acc_a[rows, :]
        factor = lax.rsqrt(jnp.mean(values * values, axis=-1, keepdims=True) + EPS)
        sums[0:1, :] += jnp.sum(back * values * factor, axis=0, keepdims=True)
        scaled = back * gain_one
        inside = jnp.mean(scaled * values, axis=-1, keepdims=True)
        total = acc_b[rows, :] + factor * scaled - values * (factor * factor * factor * inside)
        n2[rows, :] = total.astype(BF)

    loop(seq_count, back_first)
    table_sum = lax.dot_general(
        vec[pl.ds(0, heads), :],
        one_hot,
        (((1,), (1,)), ((), ())),
        precision=HIGH,
        preferred_element_type=F32,
    )
    small[0] = jnp.zeros(small.shape[1:], F32)
    for share in range(GROUP):
        own = pl.ds(share, 1)
        small[0, own, pl.ds(0, row_share)] = sums[0:1, share * row_share : (share + 1) * row_share]
        small[0, own, pl.ds(LANES, row_share)] = sums[1:2, share * row_share : (share + 1) * row_share]
    small[0, pl.ds(8, heads), pl.ds(0, bucket_count)] = table_sum
    small_copy(0).start()
    own_i.start()
    tick(("e", 0, 0))
    for step in range(5):
        small_copy(step).wait_send()
    settle()
    own_y.wait()
    own_i.wait()
    for other in row_devs:
        y_arrived(other)
        i_arrived(other)
    x_sent()
    c_sent()
    y_sent()
    i_sent()


PLAN = {
    ("n", 0, 1): ((0, 1),),
    ("s", 0, 0): ((0, 2),),
    ("o", 1, 1): ((0, 0),),
    ("n", 1, 0): ((1, 1),),
    ("n", 1, 1): ((0, 3), (1, 2), (0, 6)),
    ("s", 1, 1): ((1, 0), (2, 1), (0, 4)),
    ("u", 2, 0): ((2, 2), (0, 5)),
    ("n", 2, 0): ((1, 6), (2, 0)),
    ("s", 2, 1): ((1, 3), (3, 2), (2, 6)),
    ("y", 0, 0): ((0, 10), ("y", 0), (1, 5), ("y", 1), (0, 7), (0, 11), (0, 8)),
    ("a", 0, 0): ((1, 4),),
    ("h", 0, 0): ((2, 3), (0, 9)),
    ("h", 1, 0): ((2, 4), (4, 2), (5, 2), (2, 5)),
    ("d", 0, 0): ((3, 1), (0, 13), ("y", 2)),
    ("h", 2, 0): ((3, 0),),
    ("h", 3, 0): ((1, 7),),
    ("g", 1, 0): ((4, 1),),
    ("g", 1, 1): ((5, 1), (1, 11), (3, 3), (1, 13), (1, 8), (0, 12)),
    ("d", 1, 0): ((2, 7),),
    ("h", 4, 0): ((3, 6), (3, 5), (4, 0), (1, 9)),
    ("h", 5, 0): ((3, 4), (2, 11)),
    ("g", 2, 1): ((2, 8), (0, 15), (4, 3)),
    ("d", 2, 0): ((1, 12),),
    ("e", 0, 0): (("i", 0), (1, 15), ("s", 0), (1, 10), (0, 16), (0, 14), (4, 4), (2, 15), (2, 9), ("s", 1), (3, 7), ("i", 1), (0, 17), (1, 14), ("s", 2), (1, 17), (2, 10), (5, 0), (4, 7), (2, 17), (0, 18), (2, 12), (0, 19), (4, 5), (3, 9), (3, 8), (2, 14), (1, 16), (5, 4), (3, 15), (2, 13), (4, 6), ("s", 3), (1, 18), (4, 9), (2, 16), (4, 8), (3, 10), (5, 5), (5, 3), (5, 6), (3, 12), (2, 18), (3, 17), (3, 11), ("i", 2), (1, 19), (4, 15), (5, 9), (4, 10), (3, 16), (5, 8), (5, 10), (5, 7), (4, 12), (2, 19), (3, 13), (3, 14), (4, 11), (4, 17), (4, 13), (3, 18), (5, 13), (4, 16), ("s", 4), (4, 14), (5, 16), (3, 19), (5, 15), (4, 19), (5, 17), (5, 11), (5, 14), (4, 18), (5, 19), (5, 12), (5, 18)),
}


def unpack_kernel(parts, row_share, shares_hbm, small_hbm, layer_in, grad_in_in, *refs):
    outs, held, (shares, small, through, sems, in_sems) = refs[:11], refs[11:20], refs[20:]
    moves = [pltpu.make_async_copy(through.at[index], outs[index], sems.at[index]) for index in range(2)]
    loads = [
        pltpu.make_async_copy(src, dst, in_sems.at[index])
        for index, (src, dst) in enumerate(
            ((shares_hbm, shares), (small_hbm, small), (layer_in, through.at[0]), (grad_in_in, through.at[1]))
        )
    ]
    for copy in loads:
        copy.start()
    for copy in loads[:2]:
        copy.wait()
    gq, gk, gv, go, gi, gf, gain_a, gain_f, table = held
    blocks = gq.shape[1] // LANES
    part_rows = blocks * LANES + GROUP * row_share

    def take(start, rows):
        return shares[pl.ds(start, rows), :].astype(F32)

    def give(index):
        moves.append(pltpu.make_async_copy(held[index], outs[2 + index], sems.at[2 + index]))
        moves[-1].start()

    for part in range(parts):
        for col in range(blocks):
            gf[pl.ds(part * LANES, LANES), pl.ds(col * LANES, LANES)] = take(part * part_rows + col * LANES, LANES)
    give(5)
    for part in range(parts):
        base = part * part_rows + blocks * LANES
        for share in range(GROUP):
            gi[:, pl.ds((share * parts + part) * LANES, LANES)] = take(base + share * row_share, row_share)
    give(4)
    base = parts * part_rows
    for col in range(blocks):
        go[:, pl.ds(col * LANES, LANES)] = take(base + col * row_share, row_share)
    give(3)
    for index, ref in enumerate((gq, gk, gv)):
        for group in range(blocks // 2):
            for side in range(2):
                place = base + (1 + group) * blocks * row_share + (2 * index + side) * row_share
                ref[:, pl.ds(group * WIDE + side * LANES, LANES)] = take(place, row_share)
        give(index)
    own = lax.broadcasted_iota(jnp.int32, (GROUP, row_share), 0) == lax.axis_index("dp") % GROUP
    for first, ref in ((0, gain_a), (LANES, gain_f)):
        ref[...] = jnp.sum(jnp.where(own, small[pl.ds(0, GROUP), pl.ds(first, row_share)], 0.0), axis=0)
    table[...] = small[pl.ds(8, table.shape[0]), pl.ds(0, table.shape[1])]
    for index in (6, 7, 8):
        give(index)
    for index in range(2):
        loads[2 + index].wait()
        moves[index].start()
    for copy in moves:
        copy.wait()


def on_device(
    dp_count,
    hidden_in,
    query_lengths,
    doc_lengths,
    w_query,
    w_key,
    w_value,
    w_attn_out,
    w_inner,
    w_outer,
    gain_attn,
    gain_ffn,
    bias_table,
    cotangent,
):
    rows, block, width = hidden_in.shape
    length = rows * block
    bucket_count, heads = bias_table.shape
    ffn = w_inner.shape[1]
    part_cols = GROUP * LANES
    parts = ffn // part_cols
    vec_len = 2 * length
    lo_count = dp_count // GROUP
    row_share = width // GROUP

    def vm(*shape, dtype=BF):
        return pltpu.VMEM(shape, dtype)

    def dma(count):
        return pltpu.SemaphoreType.DMA((count,))

    hbm = pl.BlockSpec(memory_space=pl.ANY)
    vmem = pl.BlockSpec(memory_space=pltpu.VMEM)
    smem = pl.BlockSpec(memory_space=pltpu.SMEM)
    small_rows = 8 + heads
    small_cols = 2 * LANES
    total_rows = sum(chunk_rows(row_share))
    layer_raw, grad_raw, shares, small = pl.pallas_call(
        partial(layer_kernel, lo_count),
        out_shape=(
            jax.ShapeDtypeStruct(hidden_in.shape, BF),
            jax.ShapeDtypeStruct(hidden_in.shape, BF),
            jax.ShapeDtypeStruct((total_rows, LANES), BF),
            jax.ShapeDtypeStruct((small_rows, small_cols), F32),
        ),
        in_specs=[hbm, hbm, smem, smem] + [hbm] * 9,
        out_specs=(hbm, hbm, hbm, vmem),
        scratch_shapes=[
            vm(length, width),
            vm(length, width),
            vm(width, width),
            vm(width, width),
            vm(width, width),
            vm(width, width),
            vm(2, width, part_cols),
            vm(2, part_cols, width),
            vm(length, width),
            vm(length, width),
            vm(length, width),
            vm(length, width),
            vm(heads, length, length),
            vm(length, width),
            vm(length, width),
            vm(width),
            vm(width),
            vm(heads, bucket_count),
            vm(part_cols, length),
            vm(width, length),
            vm(length, width, dtype=F32),
            vm(length, width, dtype=F32),
            vm(length, width, dtype=F32),
            vm(length, part_cols),
            vm(length, part_cols),
            vm(heads, block, vec_len),
            vm(16, vec_len, dtype=F32),
            vm(8, width, dtype=F32),
            vm(3, length, WIDE),
            vm(2, length, length),
            vm(block, vec_len, dtype=F32),
            vm(SLOTS, 2, 2, 2, max(chunk_rows(row_share)), LANES),
            vm(2, 2, total_rows, LANES),
            vm(2, total_rows, LANES),
            vm(total_rows, LANES),
            vm(total_rows, LANES),
            vm(total_rows, LANES),
            vm(5, small_rows, small_cols, dtype=F32),
            vm(5, small_rows, small_cols, dtype=F32),
            dma(4 + 2 * parts),
            dma(7),
        ]
        + [dma(rows)] * 8
        + [dma(CHUNKS)] * 13
        + [dma(5)] * 2,
        compiler_params=pltpu.CompilerParams(
            collective_id=0, has_side_effects=True, vmem_limit_bytes=64 * 2**20 - 2**19
        ),
    )(
        hidden_in,
        cotangent,
        query_lengths,
        doc_lengths,
        w_query,
        w_key,
        w_value,
        w_attn_out,
        w_inner,
        w_outer,
        gain_attn,
        gain_ffn,
        bias_table.T,
    )
    grad_shapes = [(row_share, width)] * 4 + [(row_share, ffn), (ffn // GROUP, width), (row_share,), (row_share,)]
    grad_shapes.append((heads, bucket_count))
    layer_out, grad_in, *grads = pl.pallas_call(
        partial(unpack_kernel, parts, row_share),
        out_shape=[jax.ShapeDtypeStruct(hidden_in.shape, BF)] * 2
        + [jax.ShapeDtypeStruct(shape, F32) for shape in grad_shapes],
        in_specs=[hbm] * 4,
        out_specs=[hbm] * 11,
        scratch_shapes=[vm(*shape, dtype=F32) for shape in grad_shapes]
        + [vm(total_rows, LANES), vm(small_rows, small_cols, dtype=F32), vm(2, *hidden_in.shape), dma(11), dma(4)],
        compiler_params=pltpu.CompilerParams(vmem_limit_bytes=64 * 2**20 - 2**19),
    )(shares, small, layer_raw, grad_raw)
    if lo_count > 1:
        high = lax.axis_index("dp") // lo_count

        def spread(part):
            whole = jnp.zeros((GROUP,) + part.shape, F32)
            whole = lax.dynamic_update_index_in_dim(whole, part, high, 0)
            whole = whole.reshape((GROUP * part.shape[0],) + part.shape[1:])
            return lax.psum_scatter(whole, "dp", scatter_dimension=0, tiled=True)

        small = lax.psum(small, "dp") / GROUP
        gain_rows = width // dp_count
        start = lax.axis_index("dp") * gain_rows
        gains = [
            lax.dynamic_slice_in_dim(small[:GROUP, first : first + row_share].reshape(width), start, gain_rows)
            for first in (0, LANES)
        ]
        grads = [spread(part) for part in grads[:6]] + gains + [small[8 : 8 + heads, :bucket_count]]
    return (layer_out, grad_in, *grads[:8], grads[8].T)


def solution(mesh):
    return jax.shard_map(
        partial(on_device, mesh.shape["dp"]),
        mesh=mesh,
        in_specs=(
            P("dp", "seq", None),
            P("dp"),
            P("dp"),
            P(),
            P(),
            P(),
            P(),
            P(),
            P(),
            P(),
            P(),
            P(),
            P("dp", "seq", None),
        ),
        out_specs=(
            P("dp", "seq", None),
            P("dp", "seq", None),
            P("dp", None),
            P("dp", None),
            P("dp", None),
            P("dp", None),
            P("dp", None),
            P("dp", None),
            P("dp"),
            P("dp"),
            P(),
        ),
        check_vma=False,
    )
```

```python
from functools import partial

import jax
import jax.numpy as jnp
from jax import lax
from jax.experimental import pallas as pl
from jax.experimental.pallas import tpu as pltpu
from jax.sharding import PartitionSpec as P

EPS = 1e-06
NEG = -1000000000.0
LIMITS = (12, 16, 23, 32, 46, 64, 91)
HIGH = lax.Precision.HIGHEST
MESH = pl.DeviceIdType.MESH
BF = jnp.bfloat16
F32 = jnp.float32

GROUP = 8
LANES = 128
WIDE = 256
SLOTS = 5
OUTER_SPLIT = ((2, 1), (2, 1), (2, 1))
INNER_SPLIT = ((2, 2), (2, 2), (2, 2))
ATTN_SPLIT = (2, 1)
GROUP_SPLIT = ((2, 1), (2, 1), (2, 1))


def chunk_rows(row_share):
    rows = []
    for outer, inner in zip(OUTER_SPLIT, INNER_SPLIT):
        rows += [count * 2 * LANES for count in outer] + [count * 2 * row_share for count in inner]
    for split in (ATTN_SPLIT,) + GROUP_SPLIT:
        rows += [count * 2 * row_share for count in split]
    return rows


CHUNKS = len(chunk_rows(96))


def dot_nn(left, right):
    return jnp.dot(left, right, preferred_element_type=F32)


def dot_nt(left, right):
    return lax.dot_general(left, right, (((1,), (1,)), ((), ())), preferred_element_type=F32)


def dot_tn(left, right):
    return lax.dot_general(left, right, (((0,), (0,)), ((), ())), preferred_element_type=F32)


def buckets(relative):
    distance = jnp.abs(relative)
    far_bucket = 8 + sum(((distance >= thresh).astype(jnp.int32) for thresh in LIMITS))
    return jnp.where(relative > 0, 16, 0) + jnp.where(distance < 8, distance, far_bucket)


def loop(count, body):
    lax.fori_loop(0, count, lambda index, none: (body(index), none)[1], None)


def at(index, size):
    if isinstance(index, int):
        return pl.ds(index * size, size)
    return pl.ds(pl.multiple_of(index * size, size), size)


def layer_kernel(
    lo_count,
    hidden,
    cot,
    query_len,
    doc_len,
    wq_hbm,
    wk_hbm,
    wv_hbm,
    wo_hbm,
    w1_hbm,
    w2_hbm,
    gain1_hbm,
    gain2_hbm,
    table_hbm,
    layer_out,
    grad_in,
    shares,
    small_out,
    x_row,
    c_row,
    wq,
    wk,
    wv,
    wo,
    w1,
    w2,
    n1,
    q,
    k,
    v,
    probs,
    o,
    n2,
    gain1,
    gain2,
    table,
    z_turned,
    turned,
    mid,
    acc_b,
    z,
    du,
    bias,
    vec,
    sums,
    d_three,
    dsc,
    tacc,
    grads,
    r_core,
    r_first,
    r_second,
    z_end,
    z_mid,
    small,
    small_in,
    w_sem,
    own_sem,
    x_send,
    x_recv,
    c_send,
    c_recv,
    y_send,
    y_recv,
    i_send,
    i_recv,
    core_send,
    core_recv,
    first_send,
    first_recv,
    second_send,
    second_recv,
    end_send,
    end_recv,
    mid_send,
    mid_recv,
    back_send,
    back_recv,
    share_sem,
    small_send,
    small_recv,
):
    dp = lax.axis_index("dp")
    sq = lax.axis_index("seq")
    seq_count, block, width = hidden.shape
    length = x_row.shape[0]
    heads, bucket_count = table.shape
    pairs = heads // 2
    head_group = WIDE // LANES
    row_share = width // GROUP
    parts = w1_hbm.shape[1] // (GROUP * LANES)
    part_cols = GROUP * LANES
    vec_len = vec.shape[1]

    high = dp // lo_count
    bit0 = lax.rem(high, 2)
    bit1 = lax.rem(high // 2, 2)
    bit2 = lax.rem(high // 4, 2)
    step1 = 2 * lo_count * (1 - 2 * bit1)
    step2 = 4 * lo_count * (1 - 2 * bit2)
    core_dev = (dp + lo_count * (1 - 2 * bit0), sq)
    first_dev = (dp + (1 - bit0) * step1 + bit0 * step2, sq)
    second_dev = (dp + bit0 * step1 + (1 - bit0) * step2, sq)
    first_bit = (1 - bit0) * bit1 + bit0 * bit2
    second_bit = (1 - bit0) * bit2 + bit0 * bit1
    pair_dev = (dp, sq + 1 - 2 * lax.rem(sq, 2))
    mid_dev = (dp, 3 - sq)
    is_end = jnp.logical_or(sq == 0, sq == seq_count - 1)
    is_mid = jnp.logical_not(is_end)
    row_devs = [lax.rem(sq + step, seq_count) for step in range(1, seq_count)]

    def remote(src, dst, send, recv, device):
        return pltpu.make_async_remote_copy(
            src_ref=src, dst_ref=dst, send_sem=send, recv_sem=recv, device_id=device, device_id_type=MESH
        )

    barrier = pltpu.get_barrier_semaphore()
    for device in [core_dev, first_dev, second_dev] + [(dp, other) for other in row_devs]:
        pl.semaphore_signal(barrier, inc=1, device_id=device, device_id_type=MESH)
    pl.semaphore_wait(barrier, 3 + len(row_devs))

    def deal(src_of, dst_of, send, recv):
        def copy(index):
            other = row_devs[index]
            return remote(src_of(other), dst_of(sq), send.at[index], recv.at[sq], (dp, other))

        def start(index):
            copy(index).start()

        def arrived(other):
            remote(src_of(other), dst_of(other), send.at[0], recv.at[other], (dp, other)).wait_recv()

        def sent():
            for index in range(len(row_devs)):
                copy(index).wait_send()

        return start, arrived, sent

    x_start, x_arrived, x_sent = deal(
        lambda other: hidden.at[other], lambda src: x_row.at[at(src, block)], x_send, x_recv
    )
    c_start, c_arrived, c_sent = deal(
        lambda other: cot.at[other], lambda src: c_row.at[at(src, block)], c_send, c_recv
    )
    y_start, y_arrived, y_sent = deal(
        lambda other: dsc.at[at(other, block), pl.ds(0, width)], lambda src: layer_out.at[src], y_send, y_recv
    )
    i_start, i_arrived, i_sent = deal(
        lambda other: n2.at[at(other, block)], lambda src: grad_in.at[src], i_send, i_recv
    )
    own_x = pltpu.make_async_copy(hidden.at[sq], x_row.at[at(sq, block)], own_sem.at[0])
    own_c = pltpu.make_async_copy(cot.at[sq], c_row.at[at(sq, block)], own_sem.at[1])
    own_y = pltpu.make_async_copy(dsc.at[at(sq, block), pl.ds(0, width)], layer_out.at[sq], own_sem.at[2])
    own_i = pltpu.make_async_copy(n2.at[at(sq, block)], grad_in.at[sq], own_sem.at[3])

    for index in range(len(row_devs)):
        x_start(index)
    own_x.start()
    params = [
        pltpu.make_async_copy(src, dst, own_sem.at[4 + index])
        for index, (src, dst) in enumerate(((gain1_hbm, gain1), (gain2_hbm, gain2), (table_hbm, table)))
    ]
    for copy in params:
        copy.start()
    square = [
        pltpu.make_async_copy(src, dst, w_sem.at[index])
        for index, (src, dst) in enumerate(((wq_hbm, wq), (wk_hbm, wk), (wv_hbm, wv), (wo_hbm, wo)))
    ]
    for copy in square:
        copy.start()

    def part_copies(part):
        span = parts * LANES
        copies = []
        for share in range(GROUP):
            place = pl.ds(share * span + part * LANES, LANES)
            cols = pl.ds(share * LANES, LANES)
            copies.append(pltpu.make_async_copy(w1_hbm.at[:, place], w1.at[part, :, cols], w_sem.at[4 + 2 * part]))
            copies.append(pltpu.make_async_copy(w2_hbm.at[place], w2.at[part, cols], w_sem.at[5 + 2 * part]))
        return copies

    def part_wait(part):
        pltpu.make_async_copy(w1.at[part], w1.at[part], w_sem.at[4 + 2 * part]).wait()
        pltpu.make_async_copy(w2.at[part], w2.at[part], w_sem.at[5 + 2 * part]).wait()

    for part in range(parts):
        for copy in part_copies(part):
            copy.start()
    own_c.start()

    sizes = chunk_rows(row_share)

    def span(chunk):
        return pl.ds(sum(sizes[:chunk]), sizes[chunk])

    def piece(ref, chunk, *index):
        lead = index + (slice(None),) * (len(ref.shape) - 2 - len(index))
        return ref.at[lead + (span(chunk),)]

    def grad_half(chunk, side):
        return grads.at[chunk % SLOTS, side, :, :, pl.ds(0, sizes[chunk])]

    def core_copy(chunk):
        return remote(
            grad_half(chunk, 1 - bit0), piece(r_core, chunk), core_send.at[chunk], core_recv.at[chunk], core_dev
        )

    def first_copy(chunk):
        return remote(
            piece(r_core, chunk, 1 - first_bit),
            piece(r_first, chunk),
            first_send.at[chunk],
            first_recv.at[chunk],
            first_dev,
        )

    def second_copy(chunk):
        return remote(
            piece(r_first, chunk, 1 - second_bit),
            piece(r_second, chunk),
            second_send.at[chunk],
            second_recv.at[chunk],
            second_dev,
        )

    def end_copy(chunk):
        return remote(
            piece(r_second, chunk), piece(z_end, chunk), end_send.at[chunk], end_recv.at[chunk], pair_dev
        )

    def mid_copy(chunk):
        return remote(
            piece(r_second, chunk), piece(z_mid, chunk), mid_send.at[chunk], mid_recv.at[chunk], mid_dev
        )

    def back_copy(chunk):
        return remote(
            piece(z_end, chunk), piece(shares, chunk), back_send.at[chunk], back_recv.at[chunk], pair_dev
        )

    def share_copy(chunk):
        return pltpu.make_async_copy(piece(z_end, chunk), piece(shares, chunk), share_sem.at[chunk])

    def core_done(chunk):
        copy = core_copy(chunk)
        copy.wait_recv()
        for one in range(2):
            for two in range(2):
                r_core[one, two, span(chunk)] += grads[chunk % SLOTS, bit0, one, two, pl.ds(0, sizes[chunk])]
        first_copy(chunk).start()
        copy.wait_send()

    def first_done(chunk):
        first_copy(chunk).wait_recv()
        for one in range(2):
            r_first[one, span(chunk)] += r_core[first_bit, one, span(chunk)]
        second_copy(chunk).start()

    def second_done(chunk):
        second_copy(chunk).wait_recv()
        r_second[span(chunk)] += r_first[second_bit, span(chunk)]

        @pl.when(is_end)
        def _():
            end_copy(chunk).start()

    def end_done(chunk):
        @pl.when(is_mid)
        def _():
            end_copy(chunk).wait_recv()
            r_second[span(chunk)] += z_end[span(chunk)]
            mid_copy(chunk).start()

    def mid_done(chunk):
        @pl.when(is_mid)
        def _():
            mid_copy(chunk).wait_recv()
            z_end[span(chunk)] = r_second[span(chunk)] + z_mid[span(chunk)]
            back_copy(chunk).start()
            share_copy(chunk).start()

    def back_done(chunk):
        @pl.when(is_end)
        def _():
            back_copy(chunk).wait_recv()

    stages = (core_done, first_done, second_done, end_done, mid_done, back_done)

    def settle():
        for chunk in range(CHUNKS):
            first_copy(chunk).wait_send()
            second_copy(chunk).wait_send()

        @pl.when(is_end)
        def _():
            for chunk in range(CHUNKS):
                end_copy(chunk).wait_send()

        @pl.when(is_mid)
        def _():
            for chunk in range(CHUNKS):
                mid_copy(chunk).wait_send()
                back_copy(chunk).wait_send()
                share_copy(chunk).wait()

    def small_copy(step):
        device = (core_dev, (dp + step1, sq), (dp + step2, sq), pair_dev, (dp, lax.rem(sq + 2, 4)))[step]
        return remote(small.at[step], small_in.at[step], small_send.at[step], small_recv.at[step], device)

    def small_done(step):
        small_copy(step).wait_recv()
        if step < 4:
            small[step + 1] = small[step] + small_in[step]
            small_copy(step + 1).start()
        else:
            small_out[...] = small[step] + small_in[step]

    def tick(spot):
        for what, index in PLAN.get(spot, ()):
            if what == "y":
                y_start(index)
            elif what == "i":
                i_start(index)
            elif what == "s":
                small_done(index)
            else:
                stages[what](index)

    def tiles(split, first, kind, part, body):
        done = 0
        for place, count in enumerate(split):
            chunk = first + place
            if count == 1:
                body(chunk, done, 0)
            else:
                loop(count, lambda index: body(chunk, done + index, index))
            core_copy(chunk).start()
            tick((kind, part, place))
            done += count
        return first + len(split)

    def place_of(share):
        one, two, three = share % 2, (share // 2) % 2, share // 4
        return (one, two, three) if one == 0 else (one, three, two)

    for copy in params:
        copy.wait()
    distance = lax.broadcasted_iota(jnp.int32, (1, vec_len), 1) - vec_len // 2
    bucket_row = buckets(distance)
    one_hot = (
        jnp.broadcast_to(bucket_row, (bucket_count, vec_len))
        == lax.broadcasted_iota(jnp.int32, (bucket_count, vec_len), 0)
    ).astype(F32)
    vec[pl.ds(0, heads), :] = dot_nn(table[...], one_hot.astype(BF))
    sub = lax.broadcasted_iota(jnp.int32, (8, vec_len), 0)

    def build_bias(head):
        rows = jnp.broadcast_to(vec[pl.ds(head, 1), :], (8, vec_len))
        for shift in (1, 2, 4):
            rows = jnp.where((sub & shift) != 0, pltpu.roll(rows, shift, 1), rows)
        shift = 8
        while shift < block:
            rows = jnp.concatenate([rows, pltpu.roll(rows, shift, 1)], axis=0)
            shift *= 2
        bias[head] = rows.astype(BF)

    loop(heads, build_bias)

    total_len = query_len[sq] + doc_len[sq]
    key_mask = jnp.where(
        lax.broadcasted_iota(jnp.int32, (1, length), 1) < total_len, jnp.float32(0), jnp.float32(NEG)
    )
    low_lanes = lax.broadcasted_iota(jnp.int32, (1, LANES), 1) < LANES // 2

    def half_of(values, half):
        keep = low_lanes if half == 0 else jnp.logical_not(low_lanes)
        return jnp.where(keep, values, jnp.zeros_like(values))

    gain_one = gain1[...].astype(F32).reshape(1, width)
    gain_two = gain2[...].astype(F32).reshape(1, width)

    own_x.wait()
    for other in row_devs:
        x_arrived(other)
    for index in range(len(row_devs)):
        c_start(index)

    def norm_first(index):
        rows = at(index, block)
        values = x_row[rows, :].astype(F32)
        factor = lax.rsqrt(jnp.mean(values * values, axis=-1, keepdims=True) + EPS)
        n1[rows, :] = (values * factor * gain_one).astype(BF)

    loop(seq_count, norm_first)
    for copy in square:
        copy.wait()

    def project(index):
        cols = at(index, WIDE)
        q[:, cols] = dot_nn(n1[...], wq[:, cols]).astype(BF)
        k[:, cols] = dot_nn(n1[...], wk[:, cols]).astype(BF)
        v[:, cols] = dot_nn(n1[...], wv[:, cols]).astype(BF)

    loop(width // WIDE, project)

    def attend(pair):
        cols = at(pair, LANES)
        keys = k[:, cols]
        values = v[:, cols]
        for tile in range(length // WIDE):
            rows = pl.ds(tile * WIDE, WIDE)
            queries = q[rows, cols]
            total = None
            for half in range(2):
                head = 2 * pair + half
                scores = dot_nt(half_of(queries, half), keys)
                weights = []
                for part in range(WIDE // block):
                    start = vec_len // 2 - tile * WIDE - part * block
                    here = scores[part * block : (part + 1) * block]
                    here = here + bias[head, :, pl.ds(start, length)].astype(F32) + key_mask
                    here = jnp.exp(here - jnp.max(here, axis=-1, keepdims=True))
                    scale = 1.0 / jnp.sum(here, axis=-1, keepdims=True)
                    weights.append((here * scale).astype(BF))
                weights = jnp.concatenate(weights, axis=0)
                probs[head, rows, :] = weights
                term = dot_nn(weights, half_of(values, half))
                total = term if total is None else total + term
            o[rows, cols] = total.astype(BF)

    loop(pairs, attend)

    def attn_out(index):
        cols = at(index, WIDE)
        mid[:, cols] = x_row[:, cols].astype(F32) + dot_nn(o[...], wo[:, cols])

    loop(width // WIDE, attn_out)

    def norm_second(index):
        rows = at(index, block)
        values = mid[rows, :]
        factor = lax.rsqrt(jnp.mean(values * values, axis=-1, keepdims=True) + EPS)
        n2[rows, :] = (values * factor * gain_two).astype(BF)

    loop(seq_count, norm_second)

    def turn(source):
        def body(index):
            span = at(index, LANES)
            turned[span, :] = source[:, span].T

        loop(width // LANES, body)

    def put(chunk, values, tile):
        rows = values.shape[0] // GROUP
        for share in range(GROUP):
            for side in range(2):
                one, two, three = place_of(share)
                place = (2 * tile + side) * rows
                if not isinstance(tile, int):
                    place = pl.multiple_of(place, rows)
                grads[chunk % SLOTS, one, two, three, pl.ds(place, rows), :] = values[
                    share * rows : (share + 1) * rows, side * LANES : (side + 1) * LANES
                ].astype(BF)

    row_blocks = length // block
    for part in range(parts):
        part_wait(part)

        def forward(index):
            cols = at(index, WIDE)
            inner = dot_nn(n2[...], w1[part, :, cols])
            square_in = inner * inner
            bend = jnp.tanh(inner * (0.7978845608028654 + (0.7978845608028654 * 0.044715) * square_in))
            half_in = 0.5 * inner
            z[part, :, cols] = (half_in + half_in * bend).astype(BF)
            slope = 0.7978845608028654 + (3 * 0.7978845608028654 * 0.044715) * square_in
            slope = (0.5 + 0.5 * bend + half_in * (1 - bend * bend) * slope).astype(BF)
            for rows in range(row_blocks):
                bias[part * row_blocks + rows, :, cols] = slope[rows * block : (rows + 1) * block]

        loop(part_cols // WIDE, forward)

    def layer_tile(index):
        cols = at(index, WIDE)
        total = mid[:, cols]
        for part in range(parts):
            total = total + dot_nn(z[part], w2[part, :, cols])
        dsc[:, cols] = total.astype(BF)

    loop(width // WIDE, layer_tile)
    own_y.start()
    tick(("y", 0, 0))
    turn(n2)
    own_c.wait()
    for other in row_devs:
        c_arrived(other)

    chunk = 0
    for part in range(parts):

        def backward(index):
            cols = at(index, WIDE)
            back = dot_nt(c_row[...], w2[part, cols, :])
            for rows in range(row_blocks):
                span_rows = pl.ds(rows * block, block)
                slope = bias[part * row_blocks + rows, :, cols].astype(F32)
                du[span_rows, cols] = (back[rows * block : (rows + 1) * block] * slope).astype(BF)
            z_turned[cols, :] = z[part, :, cols].T

        loop(part_cols // WIDE, backward)
        tick(("u", part, 0))

        def outer_tile(chunk, tile, place):
            put(chunk, dot_nn(z_turned[...], c_row[:, at(tile, WIDE)]), place)

        chunk = tiles(OUTER_SPLIT[part], chunk, "o", part, outer_tile)

        def inner_tile(chunk, tile, place):
            put(chunk, dot_nn(turned[...], du[:, at(tile, WIDE)]), place)

        chunk = tiles(INNER_SPLIT[part], chunk, "n", part, inner_tile)

        def add_up(index):
            cols = at(index, WIDE)
            back = dot_nt(du[...], w1[part, cols, :])
            if part == 0:
                acc_b[:, cols] = back
            else:
                acc_b[:, cols] += back

        loop(width // WIDE, add_up)
        tick(("s", part, 0))

    sums[...] = jnp.zeros_like(sums)

    def back_second(index):
        rows = at(index, block)
        values = mid[rows, :]
        back = acc_b[rows, :]
        factor = lax.rsqrt(jnp.mean(values * values, axis=-1, keepdims=True) + EPS)
        sums[1:2, :] += jnp.sum(back * values * factor, axis=0, keepdims=True)
        scaled = back * gain_two
        inside = jnp.mean(scaled * values, axis=-1, keepdims=True)
        total = c_row[rows, :].astype(F32) + factor * scaled - values * (factor * factor * factor * inside)
        acc_b[rows, :] = total
        n2[rows, :] = total.astype(BF)

    loop(seq_count, back_second)
    turn(o)
    tick(("r", 0, 0))

    def attn_out_tile(chunk, tile, place):
        cols = at(tile, WIDE)
        put(chunk, dot_nn(turned[...], n2[:, cols]), place)
        c_row[:, cols] = dot_nt(n2[...], wo[cols, :]).astype(BF)

    chunk = tiles(ATTN_SPLIT, chunk, "a", 0, attn_out_tile)
    turn(n1)

    def attend_back(group, inside):
        pair = group * head_group + inside
        cols = at(pair, LANES)
        keys = k[:, cols]
        values = v[:, cols]
        queries = q[:, cols]
        backs = c_row[:, cols]
        product = backs.astype(F32) * o[:, cols].astype(F32)
        for half in range(2):
            head = 2 * pair + half
            dot_sum = jnp.sum(half_of(product, half), axis=-1, keepdims=True)
            tacc[...] = jnp.zeros_like(tacc)
            for tile in range(length // WIDE):
                rows = pl.ds(tile * WIDE, WIDE)
                back = dot_nt(half_of(backs[tile * WIDE : (tile + 1) * WIDE], half), values)
                for part in range(WIDE // block):
                    base = tile * WIDE + part * block
                    start = vec_len // 2 - base
                    score = probs[head, pl.ds(base, block), :].astype(F32) * (
                        back[part * block : (part + 1) * block] - dot_sum[base : base + block]
                    )
                    tacc[:, pl.ds(start, length)] += score
                    dsc[pl.ds(base, block), pl.ds(half * length, length)] = score.astype(BF)
            rows = tacc[...]
            size = block
            while size > 8:
                size //= 2
                rows = rows[:size] + pltpu.roll(rows[size:], vec_len - size, 1)
            for shift in (4, 2, 1):
                rows = jnp.where((sub & shift) != 0, pltpu.roll(rows, vec_len - shift, 1), rows)
            vec[pl.ds(head, 1), :] = jnp.sum(rows, axis=0, keepdims=True)
        out = at(inside, LANES)
        d_three[0, :, out] = (
            dot_nn(dsc[:, pl.ds(0, length)], half_of(keys, 0)) + dot_nn(dsc[:, pl.ds(length, length)], half_of(keys, 1))
        ).astype(BF)
        d_three[1, :, out] = (
            dot_tn(dsc[:, pl.ds(0, length)], half_of(queries, 0)) + dot_tn(dsc[:, pl.ds(length, length)], half_of(queries, 1))
        ).astype(BF)
        d_three[2, :, out] = (
            dot_tn(probs[2 * pair], half_of(backs, 0)) + dot_tn(probs[2 * pair + 1], half_of(backs, 1))
        ).astype(BF)

    own_y.wait()
    y_sent()
    for group in range(width // WIDE):
        for inside in range(head_group):
            attend_back(group, inside)
            tick(("h", head_group * group + inside, 0))

        def group_tile(chunk, tile, place):
            put(chunk, dot_nn(turned[...], d_three[tile]), place)

        chunk = tiles(GROUP_SPLIT[group], chunk, "g", group, group_tile)
        cols = pl.ds(group * WIDE, WIDE)
        term = dot_nt(d_three[0], wq[:, cols]) + dot_nt(d_three[1], wk[:, cols]) + dot_nt(d_three[2], wv[:, cols])
        if group == 0:
            mid[...] = term
        else:
            mid[...] += term
        tick(("d", group, 0))

    def back_first(index):
        rows = at(index, block)
        values = x_row[rows, :].astype(F32)
        back = mid[rows, :]
        factor = lax.rsqrt(jnp.mean(values * values, axis=-1, keepdims=True) + EPS)
        sums[0:1, :] += jnp.sum(back * values * factor, axis=0, keepdims=True)
        scaled = back * gain_one
        inside = jnp.mean(scaled * values, axis=-1, keepdims=True)
        total = acc_b[rows, :] + factor * scaled - values * (factor * factor * factor * inside)
        n2[rows, :] = total.astype(BF)

    loop(seq_count, back_first)
    table_sum = lax.dot_general(
        vec[pl.ds(0, heads), :],
        one_hot,
        (((1,), (1,)), ((), ())),
        precision=HIGH,
        preferred_element_type=F32,
    )
    small[0] = jnp.zeros(small.shape[1:], F32)
    for share in range(GROUP):
        own = pl.ds(share, 1)
        small[0, own, pl.ds(0, row_share)] = sums[0:1, share * row_share : (share + 1) * row_share]
        small[0, own, pl.ds(LANES, row_share)] = sums[1:2, share * row_share : (share + 1) * row_share]
    small[0, pl.ds(8, heads), pl.ds(0, bucket_count)] = table_sum
    small_copy(0).start()
    own_i.start()
    tick(("e", 0, 0))
    for step in range(5):
        small_copy(step).wait_send()
    settle()
    own_i.wait()
    for other in row_devs:
        y_arrived(other)
        i_arrived(other)
    x_sent()
    c_sent()
    i_sent()


PLAN = {
    ("y", 0, 0): (("y", 0),),
    ("u", 0, 0): (("y", 1),),
    ("o", 0, 1): (("y", 2),),
    ("n", 0, 1): ((0, 0), (0, 1)),
    ("s", 0, 0): ((0, 2),),
    ("u", 1, 0): ((0, 3),),
    ("o", 1, 1): ((1, 0),),
    ("n", 1, 0): ((1, 1),),
    ("n", 1, 1): ((0, 4), (0, 5)),
    ("s", 1, 0): ((2, 0), (1, 2)),
    ("u", 2, 0): ((0, 6), (0, 7), (1, 3)),
    ("o", 2, 0): ((2, 1),),
    ("o", 2, 1): ((2, 2),),
    ("n", 2, 1): ((1, 4), (0, 8)),
    ("s", 2, 0): ((0, 9), (2, 3)),
    ("r", 0, 0): ((1, 5), (0, 10)),
    ("a", 0, 0): ((2, 4), (3, 0), (1, 6)),
    ("a", 0, 1): ((2, 5),),
    ("h", 0, 0): ((3, 2), (1, 7)),
    ("h", 1, 0): ((4, 0), (3, 1), (3, 3), (2, 6), (1, 8), (0, 11), (0, 12), (2, 7), (0, 13)),
    ("g", 0, 0): ((4, 1), (4, 2), (1, 9), (5, 1)),
    ("d", 0, 0): ((5, 0),),
    ("h", 2, 0): ((3, 4), (1, 10), (4, 3), (3, 5), (2, 8)),
    ("h", 3, 0): ((2, 9), (1, 11), (5, 2), (0, 14), (0, 15)),
    ("g", 1, 0): ((5, 3), (3, 6), (1, 12)),
    ("g", 1, 1): ((4, 4), (3, 7), (2, 10), (4, 5), (1, 13), (5, 5), (0, 16)),
    ("d", 1, 0): ((2, 11),),
    ("h", 4, 0): ((4, 6), (2, 12), (1, 14), (0, 17)),
    ("h", 5, 0): ((5, 4), (4, 7), (3, 8), (3, 9), (1, 15), (2, 13)),
    ("g", 2, 0): ((5, 6), (2, 14), (1, 16)),
    ("g", 2, 1): ((3, 10), (1, 17), (5, 7), (2, 15)),
    ("e", 0, 0): ((3, 11), (0, 18), (3, 12), (2, 17), (2, 16), (4, 8), (4, 9), (0, 19), ("i", 0), ("s", 0), (4, 10), (1, 18), (1, 19), (3, 13), (4, 11), (3, 14), (5, 11), (2, 18), (5, 8), ("s", 1), (5, 9), (3, 15), (4, 12), (2, 19), ("s", 2), ("i", 1), (4, 15), (3, 16), (3, 17), (4, 13), (5, 12), (5, 10), ("s", 3), (4, 14), (3, 18), (5, 13), (3, 19), ("i", 2), (4, 16), (4, 17), (5, 15), ("s", 4), (5, 16), (5, 17), (4, 18), (5, 14), (4, 19), (5, 18), (5, 19)),
}


def unpack_kernel(parts, row_share, shares_hbm, small_hbm, layer_in, grad_in_in, *refs):
    outs, held, (shares, small, through, sems, in_sems) = refs[:11], refs[11:20], refs[20:]
    moves = [pltpu.make_async_copy(through.at[index], outs[index], sems.at[index]) for index in range(2)]
    loads = [
        pltpu.make_async_copy(src, dst, in_sems.at[index])
        for index, (src, dst) in enumerate(
            ((shares_hbm, shares), (small_hbm, small), (layer_in, through.at[0]), (grad_in_in, through.at[1]))
        )
    ]
    for copy in loads:
        copy.start()
    for copy in loads[:2]:
        copy.wait()
    gq, gk, gv, go, gi, gf, gain_a, gain_f, table = held
    blocks = gq.shape[1] // LANES
    part_rows = blocks * LANES + GROUP * row_share

    def take(start, rows):
        return shares[pl.ds(start, rows), :].astype(F32)

    def give(index):
        moves.append(pltpu.make_async_copy(held[index], outs[2 + index], sems.at[2 + index]))
        moves[-1].start()

    for part in range(parts):
        for col in range(blocks):
            gf[pl.ds(part * LANES, LANES), pl.ds(col * LANES, LANES)] = take(part * part_rows + col * LANES, LANES)
    give(5)
    for part in range(parts):
        base = part * part_rows + blocks * LANES
        for share in range(GROUP):
            gi[:, pl.ds((share * parts + part) * LANES, LANES)] = take(base + share * row_share, row_share)
    give(4)
    base = parts * part_rows
    for col in range(blocks):
        go[:, pl.ds(col * LANES, LANES)] = take(base + col * row_share, row_share)
    give(3)
    for index, ref in enumerate((gq, gk, gv)):
        for group in range(blocks // 2):
            for side in range(2):
                place = base + (1 + group) * blocks * row_share + (2 * index + side) * row_share
                ref[:, pl.ds(group * WIDE + side * LANES, LANES)] = take(place, row_share)
        give(index)
    own = lax.broadcasted_iota(jnp.int32, (GROUP, row_share), 0) == lax.axis_index("dp") % GROUP
    for first, ref in ((0, gain_a), (LANES, gain_f)):
        ref[...] = jnp.sum(jnp.where(own, small[pl.ds(0, GROUP), pl.ds(first, row_share)], 0.0), axis=0)
    table[...] = small[pl.ds(8, table.shape[0]), pl.ds(0, table.shape[1])]
    for index in (6, 7, 8):
        give(index)
    for index in range(2):
        loads[2 + index].wait()
        moves[index].start()
    for copy in moves:
        copy.wait()


def on_device(
    dp_count,
    hidden_in,
    query_lengths,
    doc_lengths,
    w_query,
    w_key,
    w_value,
    w_attn_out,
    w_inner,
    w_outer,
    gain_attn,
    gain_ffn,
    bias_table,
    cotangent,
):
    rows, block, width = hidden_in.shape
    length = rows * block
    bucket_count, heads = bias_table.shape
    ffn = w_inner.shape[1]
    part_cols = GROUP * LANES
    parts = ffn // part_cols
    vec_len = 2 * length
    lo_count = dp_count // GROUP
    row_share = width // GROUP

    def vm(*shape, dtype=BF):
        return pltpu.VMEM(shape, dtype)

    def dma(count):
        return pltpu.SemaphoreType.DMA((count,))

    hbm = pl.BlockSpec(memory_space=pl.ANY)
    vmem = pl.BlockSpec(memory_space=pltpu.VMEM)
    smem = pl.BlockSpec(memory_space=pltpu.SMEM)
    small_rows = 8 + heads
    small_cols = 2 * LANES
    total_rows = sum(chunk_rows(row_share))
    layer_raw, grad_raw, shares, small = pl.pallas_call(
        partial(layer_kernel, lo_count),
        out_shape=(
            jax.ShapeDtypeStruct(hidden_in.shape, BF),
            jax.ShapeDtypeStruct(hidden_in.shape, BF),
            jax.ShapeDtypeStruct((total_rows, LANES), BF),
            jax.ShapeDtypeStruct((small_rows, small_cols), F32),
        ),
        in_specs=[hbm, hbm, smem, smem] + [hbm] * 9,
        out_specs=(hbm, hbm, hbm, vmem),
        scratch_shapes=[
            vm(length, width),
            vm(length, width),
            vm(width, width),
            vm(width, width),
            vm(width, width),
            vm(width, width),
            vm(parts, width, part_cols),
            vm(parts, part_cols, width),
            vm(length, width),
            vm(length, width),
            vm(length, width),
            vm(length, width),
            vm(heads, length, length),
            vm(length, width),
            vm(length, width),
            vm(width),
            vm(width),
            vm(heads, bucket_count),
            vm(part_cols, length),
            vm(width, length),
            vm(length, width, dtype=F32),
            vm(length, width, dtype=F32),
            vm(parts, length, part_cols),
            vm(length, part_cols),
            vm(heads, block, vec_len),
            vm(16, vec_len, dtype=F32),
            vm(8, width, dtype=F32),
            vm(3, length, WIDE),
            vm(length, 2 * length),
            vm(block, vec_len, dtype=F32),
            vm(SLOTS, 2, 2, 2, max(chunk_rows(row_share)), LANES),
            vm(2, 2, total_rows, LANES),
            vm(2, total_rows, LANES),
            vm(total_rows, LANES),
            vm(total_rows, LANES),
            vm(total_rows, LANES),
            vm(5, small_rows, small_cols, dtype=F32),
            vm(5, small_rows, small_cols, dtype=F32),
            dma(4 + 2 * parts),
            dma(7),
        ]
        + [dma(rows)] * 8
        + [dma(CHUNKS)] * 13
        + [dma(5)] * 2,
        compiler_params=pltpu.CompilerParams(
            collective_id=0, has_side_effects=True, vmem_limit_bytes=64 * 2**20 - 2**19
        ),
    )(
        hidden_in,
        cotangent,
        query_lengths,
        doc_lengths,
        w_query,
        w_key,
        w_value,
        w_attn_out,
        w_inner,
        w_outer,
        gain_attn,
        gain_ffn,
        bias_table.T,
    )
    grad_shapes = [(row_share, width)] * 4 + [(row_share, ffn), (ffn // GROUP, width), (row_share,), (row_share,)]
    grad_shapes.append((heads, bucket_count))
    layer_out, grad_in, *grads = pl.pallas_call(
        partial(unpack_kernel, parts, row_share),
        out_shape=[jax.ShapeDtypeStruct(hidden_in.shape, BF)] * 2
        + [jax.ShapeDtypeStruct(shape, F32) for shape in grad_shapes],
        in_specs=[hbm] * 4,
        out_specs=[hbm] * 11,
        scratch_shapes=[vm(*shape, dtype=F32) for shape in grad_shapes]
        + [vm(total_rows, LANES), vm(small_rows, small_cols, dtype=F32), vm(2, *hidden_in.shape), dma(11), dma(4)],
        compiler_params=pltpu.CompilerParams(vmem_limit_bytes=64 * 2**20 - 2**19),
    )(shares, small, layer_raw, grad_raw)
    if lo_count > 1:
        high = lax.axis_index("dp") // lo_count

        def spread(part):
            whole = jnp.zeros((GROUP,) + part.shape, F32)
            whole = lax.dynamic_update_index_in_dim(whole, part, high, 0)
            whole = whole.reshape((GROUP * part.shape[0],) + part.shape[1:])
            return lax.psum_scatter(whole, "dp", scatter_dimension=0, tiled=True)

        small = lax.psum(small, "dp") / GROUP
        gain_rows = width // dp_count
        start = lax.axis_index("dp") * gain_rows
        gains = [
            lax.dynamic_slice_in_dim(small[:GROUP, first : first + row_share].reshape(width), start, gain_rows)
            for first in (0, LANES)
        ]
        grads = [spread(part) for part in grads[:6]] + gains + [small[8 : 8 + heads, :bucket_count]]
    return (layer_out, grad_in, *grads[:8], grads[8].T)


def solution(mesh):
    return jax.shard_map(
        partial(on_device, mesh.shape["dp"]),
        mesh=mesh,
        in_specs=(
            P("dp", "seq", None),
            P("dp"),
            P("dp"),
            P(),
            P(),
            P(),
            P(),
            P(),
            P(),
            P(),
            P(),
            P(),
            P("dp", "seq", None),
        ),
        out_specs=(
            P("dp", "seq", None),
            P("dp", "seq", None),
            P("dp", None),
            P("dp", None),
            P("dp", None),
            P("dp", None),
            P("dp", None),
            P("dp", None),
            P("dp"),
            P("dp"),
            P(),
        ),
        check_vma=False,
    )
```

```python
from functools import partial

import jax
import jax.numpy as jnp
from jax import lax
from jax.experimental import pallas as pl
from jax.experimental.pallas import tpu as pltpu
from jax.sharding import PartitionSpec as P

EPS = 1e-06
NEG = -1000000000.0
LIMITS = (12, 16, 23, 32, 46, 64, 91)
HIGH = lax.Precision.HIGHEST
MESH = pl.DeviceIdType.MESH
BF = jnp.bfloat16
F32 = jnp.float32

GROUP = 8
LANES = 128
WIDE = 256
SLOTS = 5
OUTER_SPLIT = ((2, 1), (2, 1), (2, 1))
INNER_SPLIT = ((2, 2), (2, 2), (2, 2))
ATTN_SPLIT = (3,)
GROUP_SPLIT = ((3,), (3,), (2, 1))


def chunk_rows(row_share):
    rows = []
    for outer, inner in zip(OUTER_SPLIT, INNER_SPLIT):
        rows += [count * 2 * LANES for count in outer] + [count * 2 * row_share for count in inner]
    for split in (ATTN_SPLIT,) + GROUP_SPLIT:
        rows += [count * 2 * row_share for count in split]
    return rows


CHUNKS = len(chunk_rows(96))


def dot_nn(left, right):
    return jnp.dot(left, right, preferred_element_type=F32)


def dot_nt(left, right):
    return lax.dot_general(left, right, (((1,), (1,)), ((), ())), preferred_element_type=F32)


def dot_tn(left, right):
    return lax.dot_general(left, right, (((0,), (0,)), ((), ())), preferred_element_type=F32)


def buckets(relative):
    distance = jnp.abs(relative)
    far_bucket = 8 + sum(((distance >= thresh).astype(jnp.int32) for thresh in LIMITS))
    return jnp.where(relative > 0, 16, 0) + jnp.where(distance < 8, distance, far_bucket)


def loop(count, body):
    lax.fori_loop(0, count, lambda index, none: (body(index), none)[1], None)


def at(index, size):
    if isinstance(index, int):
        return pl.ds(index * size, size)
    return pl.ds(pl.multiple_of(index * size, size), size)


def layer_kernel(
    lo_count,
    hidden,
    cot,
    query_len,
    doc_len,
    wq_hbm,
    wk_hbm,
    wv_hbm,
    wo_hbm,
    w1_hbm,
    w2_hbm,
    gain1_hbm,
    gain2_hbm,
    table_hbm,
    layer_out,
    grad_in,
    shares,
    small_out,
    x_row,
    c_row,
    wq,
    wk,
    wv,
    wo,
    w1,
    w2,
    n1,
    q,
    k,
    v,
    probs,
    o,
    n2,
    gain1,
    gain2,
    table,
    z_turned,
    turned,
    mid,
    acc_b,
    z,
    du,
    bias,
    vec,
    sums,
    dsc,
    tacc,
    grads,
    r_core,
    r_first,
    r_second,
    z_end,
    z_mid,
    small,
    small_in,
    w_sem,
    own_sem,
    x_send,
    x_recv,
    c_send,
    c_recv,
    y_send,
    y_recv,
    i_send,
    i_recv,
    core_send,
    core_recv,
    first_send,
    first_recv,
    second_send,
    second_recv,
    end_send,
    end_recv,
    mid_send,
    mid_recv,
    back_send,
    back_recv,
    share_sem,
    small_send,
    small_recv,
):
    dp = lax.axis_index("dp")
    sq = lax.axis_index("seq")
    seq_count, block, width = hidden.shape
    length = x_row.shape[0]
    heads, bucket_count = table.shape
    pairs = heads // 2
    row_share = width // GROUP
    parts = w1_hbm.shape[1] // (GROUP * LANES)
    part_cols = GROUP * LANES
    vec_len = vec.shape[1]

    high = dp // lo_count
    bit0 = lax.rem(high, 2)
    bit1 = lax.rem(high // 2, 2)
    bit2 = lax.rem(high // 4, 2)
    step1 = 2 * lo_count * (1 - 2 * bit1)
    step2 = 4 * lo_count * (1 - 2 * bit2)
    core_dev = (dp + lo_count * (1 - 2 * bit0), sq)
    first_dev = (dp + (1 - bit0) * step1 + bit0 * step2, sq)
    second_dev = (dp + bit0 * step1 + (1 - bit0) * step2, sq)
    first_bit = (1 - bit0) * bit1 + bit0 * bit2
    second_bit = (1 - bit0) * bit2 + bit0 * bit1
    pair_dev = (dp, sq + 1 - 2 * lax.rem(sq, 2))
    mid_dev = (dp, 3 - sq)
    is_end = jnp.logical_or(sq == 0, sq == seq_count - 1)
    is_mid = jnp.logical_not(is_end)
    row_devs = [lax.rem(sq + step, seq_count) for step in range(1, seq_count)]

    def remote(src, dst, send, recv, device):
        return pltpu.make_async_remote_copy(
            src_ref=src, dst_ref=dst, send_sem=send, recv_sem=recv, device_id=device, device_id_type=MESH
        )

    barrier = pltpu.get_barrier_semaphore()
    for device in [core_dev, first_dev, second_dev] + [(dp, other) for other in row_devs]:
        pl.semaphore_signal(barrier, inc=1, device_id=device, device_id_type=MESH)
    pl.semaphore_wait(barrier, 3 + len(row_devs))

    def deal(src_of, dst_of, send, recv):
        def copy(index):
            other = row_devs[index]
            return remote(src_of(other), dst_of(sq), send.at[index], recv.at[sq], (dp, other))

        def start(index):
            copy(index).start()

        def arrived(other):
            remote(src_of(other), dst_of(other), send.at[0], recv.at[other], (dp, other)).wait_recv()

        def sent():
            for index in range(len(row_devs)):
                copy(index).wait_send()

        return start, arrived, sent

    x_start, x_arrived, x_sent = deal(
        lambda other: hidden.at[other], lambda src: x_row.at[at(src, block)], x_send, x_recv
    )
    c_start, c_arrived, c_sent = deal(
        lambda other: cot.at[other], lambda src: c_row.at[at(src, block)], c_send, c_recv
    )
    y_start, y_arrived, y_sent = deal(
        lambda other: dsc.at[at(other, block), pl.ds(0, width)], lambda src: layer_out.at[src], y_send, y_recv
    )
    i_start, i_arrived, i_sent = deal(
        lambda other: du.at[at(other, block), pl.ds(0, width)], lambda src: grad_in.at[src], i_send, i_recv
    )
    own_x = pltpu.make_async_copy(hidden.at[sq], x_row.at[at(sq, block)], own_sem.at[0])
    own_c = pltpu.make_async_copy(cot.at[sq], c_row.at[at(sq, block)], own_sem.at[1])
    own_y = pltpu.make_async_copy(dsc.at[at(sq, block), pl.ds(0, width)], layer_out.at[sq], own_sem.at[2])
    own_i = pltpu.make_async_copy(du.at[at(sq, block), pl.ds(0, width)], grad_in.at[sq], own_sem.at[3])

    for index in range(len(row_devs)):
        x_start(index)
    own_x.start()
    params = [
        pltpu.make_async_copy(src, dst, own_sem.at[4 + index])
        for index, (src, dst) in enumerate(((gain1_hbm, gain1), (gain2_hbm, gain2), (table_hbm, table)))
    ]
    for copy in params:
        copy.start()
    square = [
        pltpu.make_async_copy(src, dst, w_sem.at[index])
        for index, (src, dst) in enumerate(((wq_hbm, wq), (wk_hbm, wk), (wv_hbm, wv), (wo_hbm, wo)))
    ]
    for copy in square:
        copy.start()

    def part_copies(part):
        span = parts * LANES
        copies = []
        for share in range(GROUP):
            place = pl.ds(share * span + part * LANES, LANES)
            cols = pl.ds(share * LANES, LANES)
            copies.append(pltpu.make_async_copy(w1_hbm.at[:, place], w1.at[part, :, cols], w_sem.at[4 + 2 * part]))
            copies.append(pltpu.make_async_copy(w2_hbm.at[place], w2.at[part, cols], w_sem.at[5 + 2 * part]))
        return copies

    def part_wait(part):
        pltpu.make_async_copy(w1.at[part], w1.at[part], w_sem.at[4 + 2 * part]).wait()
        pltpu.make_async_copy(w2.at[part], w2.at[part], w_sem.at[5 + 2 * part]).wait()

    for part in range(parts):
        for copy in part_copies(part):
            copy.start()
    own_c.start()

    sizes = chunk_rows(row_share)

    def span(chunk):
        return pl.ds(sum(sizes[:chunk]), sizes[chunk])

    def piece(ref, chunk, *index):
        lead = index + (slice(None),) * (len(ref.shape) - 2 - len(index))
        return ref.at[lead + (span(chunk),)]

    def grad_half(chunk, side):
        return grads.at[chunk % SLOTS, side, :, :, pl.ds(0, sizes[chunk])]

    def core_copy(chunk):
        return remote(
            grad_half(chunk, 1 - bit0), piece(r_core, chunk), core_send.at[chunk], core_recv.at[chunk], core_dev
        )

    def first_copy(chunk):
        return remote(
            piece(r_core, chunk, 1 - first_bit),
            piece(r_first, chunk),
            first_send.at[chunk],
            first_recv.at[chunk],
            first_dev,
        )

    def second_copy(chunk):
        return remote(
            piece(r_first, chunk, 1 - second_bit),
            piece(r_second, chunk),
            second_send.at[chunk],
            second_recv.at[chunk],
            second_dev,
        )

    def end_copy(chunk):
        return remote(
            piece(r_second, chunk), piece(z_end, chunk), end_send.at[chunk], end_recv.at[chunk], pair_dev
        )

    def mid_copy(chunk):
        return remote(
            piece(r_second, chunk), piece(z_mid, chunk), mid_send.at[chunk], mid_recv.at[chunk], mid_dev
        )

    def back_copy(chunk):
        return remote(
            piece(z_end, chunk), piece(shares, chunk), back_send.at[chunk], back_recv.at[chunk], pair_dev
        )

    def share_copy(chunk):
        return pltpu.make_async_copy(piece(z_end, chunk), piece(shares, chunk), share_sem.at[chunk])

    def core_done(chunk):
        copy = core_copy(chunk)
        copy.wait_recv()

        def add(index):
            one, two = index // 2, lax.rem(index, 2)
            r_core[one, two, span(chunk)] += grads[chunk % SLOTS, bit0, one, two, pl.ds(0, sizes[chunk])]

        loop(4, add)
        first_copy(chunk).start()
        copy.wait_send()

    def first_done(chunk):
        first_copy(chunk).wait_recv()

        def add(index):
            r_first[index, span(chunk)] += r_core[first_bit, index, span(chunk)]

        loop(2, add)
        second_copy(chunk).start()

    def second_done(chunk):
        second_copy(chunk).wait_recv()
        r_second[span(chunk)] += r_first[second_bit, span(chunk)]

        @pl.when(is_end)
        def _():
            end_copy(chunk).start()

    def end_done(chunk):
        @pl.when(is_mid)
        def _():
            end_copy(chunk).wait_recv()
            r_second[span(chunk)] += z_end[span(chunk)]
            mid_copy(chunk).start()

    def mid_done(chunk):
        @pl.when(is_mid)
        def _():
            mid_copy(chunk).wait_recv()
            z_end[span(chunk)] = r_second[span(chunk)] + z_mid[span(chunk)]
            back_copy(chunk).start()
            share_copy(chunk).start()

    def back_done(chunk):
        @pl.when(is_end)
        def _():
            back_copy(chunk).wait_recv()

    stages = (core_done, first_done, second_done, end_done, mid_done, back_done)

    def settle():
        for chunk in range(CHUNKS):
            first_copy(chunk).wait_send()
            second_copy(chunk).wait_send()

        @pl.when(is_end)
        def _():
            for chunk in range(CHUNKS):
                end_copy(chunk).wait_send()

        @pl.when(is_mid)
        def _():
            for chunk in range(CHUNKS):
                mid_copy(chunk).wait_send()
                back_copy(chunk).wait_send()
                share_copy(chunk).wait()

    def small_copy(step):
        device = (core_dev, (dp + step1, sq), (dp + step2, sq), pair_dev, (dp, lax.rem(sq + 2, 4)))[step]
        return remote(small.at[step], small_in.at[step], small_send.at[step], small_recv.at[step], device)

    def small_done(step):
        small_copy(step).wait_recv()
        if step < 4:
            small[step + 1] = small[step] + small_in[step]
            small_copy(step + 1).start()
        else:
            small_out[...] = small[step] + small_in[step]

    def tick(spot):
        for what, index in PLAN.get(spot, ()):
            if what == "y":
                y_start(index)
            elif what == "i":
                i_start(index)
            elif what == "s":
                small_done(index)
            else:
                stages[what](index)

    def tiles(split, first, kind, part, body):
        done = 0
        for place, count in enumerate(split):
            chunk = first + place
            if count == 1:
                body(chunk, done, 0)
            else:
                loop(count, lambda index: body(chunk, done + index, index))
            core_copy(chunk).start()
            tick((kind, part, place))
            done += count
        return first + len(split)

    def place_of(share):
        one, two, three = share % 2, (share // 2) % 2, share // 4
        return (one, two, three) if one == 0 else (one, three, two)

    for copy in params:
        copy.wait()
    distance = lax.broadcasted_iota(jnp.int32, (1, vec_len), 1) - vec_len // 2
    bucket_row = buckets(distance)
    one_hot = (
        jnp.broadcast_to(bucket_row, (bucket_count, vec_len))
        == lax.broadcasted_iota(jnp.int32, (bucket_count, vec_len), 0)
    ).astype(F32)
    vec[pl.ds(0, heads), :] = dot_nn(table[...], one_hot.astype(BF))
    sub = lax.broadcasted_iota(jnp.int32, (8, vec_len), 0)

    def build_bias(head):
        rows = jnp.broadcast_to(vec[pl.ds(head, 1), :], (8, vec_len))
        for shift in (1, 2, 4):
            rows = jnp.where((sub & shift) != 0, pltpu.roll(rows, shift, 1), rows)
        shift = 8
        while shift < block:
            rows = jnp.concatenate([rows, pltpu.roll(rows, shift, 1)], axis=0)
            shift *= 2
        bias[head] = rows.astype(BF)

    loop(heads, build_bias)

    total_len = query_len[sq] + doc_len[sq]
    key_mask = jnp.where(
        lax.broadcasted_iota(jnp.int32, (1, length), 1) < total_len, jnp.float32(0), jnp.float32(NEG)
    )
    low_lanes = lax.broadcasted_iota(jnp.int32, (1, LANES), 1) < LANES // 2

    def half_of(values, half):
        keep = low_lanes if half == 0 else jnp.logical_not(low_lanes)
        return jnp.where(keep, values, jnp.zeros_like(values))

    gain_one = gain1[...].astype(F32).reshape(1, width)
    gain_two = gain2[...].astype(F32).reshape(1, width)

    own_x.wait()
    for other in row_devs:
        x_arrived(other)
    for index in range(len(row_devs)):
        c_start(index)

    def norm_first(index):
        rows = at(index, block)
        values = x_row[rows, :].astype(F32)
        factor = lax.rsqrt(jnp.mean(values * values, axis=-1, keepdims=True) + EPS)
        n1[rows, :] = (values * factor * gain_one).astype(BF)

    loop(seq_count, norm_first)
    for copy in square:
        copy.wait()

    def project(index):
        cols = at(index, WIDE)
        q[:, cols] = dot_nn(n1[...], wq[:, cols]).astype(BF)
        k[:, cols] = dot_nn(n1[...], wk[:, cols]).astype(BF)
        v[:, cols] = dot_nn(n1[...], wv[:, cols]).astype(BF)

    loop(width // WIDE, project)

    def attend(pair):
        cols = at(pair, LANES)
        keys = k[:, cols]
        values = v[:, cols]
        for tile in range(length // WIDE):
            rows = pl.ds(tile * WIDE, WIDE)
            queries = q[rows, cols]
            total = None
            for half in range(2):
                head = 2 * pair + half
                scores = dot_nt(half_of(queries, half), keys)
                weights = []
                for part in range(WIDE // block):
                    start = vec_len // 2 - tile * WIDE - part * block
                    here = scores[part * block : (part + 1) * block]
                    here = here + bias[head, :, pl.ds(start, length)].astype(F32) + key_mask
                    here = jnp.exp(here - jnp.max(here, axis=-1, keepdims=True))
                    scale = 1.0 / jnp.sum(here, axis=-1, keepdims=True)
                    weights.append((here * scale).astype(BF))
                weights = jnp.concatenate(weights, axis=0)
                probs[head, rows, :] = weights
                term = dot_nn(weights, half_of(values, half))
                total = term if total is None else total + term
            o[rows, cols] = total.astype(BF)

    loop(pairs, attend)

    def attn_out(index):
        cols = at(index, WIDE)
        mid[:, cols] = x_row[:, cols].astype(F32) + dot_nn(o[...], wo[:, cols])

    loop(width // WIDE, attn_out)

    def norm_second(index):
        rows = at(index, block)
        values = mid[rows, :]
        factor = lax.rsqrt(jnp.mean(values * values, axis=-1, keepdims=True) + EPS)
        n2[rows, :] = (values * factor * gain_two).astype(BF)

    loop(seq_count, norm_second)

    def turn(source):
        def body(index):
            span = at(index, LANES)
            turned[span, :] = source[:, span].T

        loop(width // LANES, body)

    def put(chunk, values, tile):
        rows = values.shape[0] // GROUP
        for share in range(GROUP):
            for side in range(2):
                one, two, three = place_of(share)
                place = (2 * tile + side) * rows
                if not isinstance(tile, int):
                    place = pl.multiple_of(place, rows)
                grads[chunk % SLOTS, one, two, three, pl.ds(place, rows), :] = values[
                    share * rows : (share + 1) * rows, side * LANES : (side + 1) * LANES
                ].astype(BF)

    row_blocks = length // block
    for part in range(parts):
        part_wait(part)

        def forward(index):
            cols = at(index, WIDE)
            inner = dot_nn(n2[...], w1[part, :, cols])
            square_in = inner * inner
            bend = jnp.tanh(inner * (0.7978845608028654 + (0.7978845608028654 * 0.044715) * square_in))
            gate = 0.5 + 0.5 * bend
            active = inner * gate
            z[part, :, cols] = active.astype(BF)
            slope = 1.5957691216057308 + (6 * 0.7978845608028654 * 0.044715) * square_in
            slope = (gate + active * ((1 - gate) * slope)).astype(BF)
            for rows in range(row_blocks):
                bias[part * row_blocks + rows, :, cols] = slope[rows * block : (rows + 1) * block]

        def forward_two(index):
            forward(2 * index)
            forward(2 * index + 1)

        loop(part_cols // (2 * WIDE), forward_two)

    def layer_tile(index):
        cols = at(index, WIDE)
        total = mid[:, cols]
        for part in range(parts):
            total = total + dot_nn(z[part], w2[part, :, cols])
        dsc[:, cols] = total.astype(BF)

    loop(width // WIDE, layer_tile)
    own_y.start()
    tick(("y", 0, 0))
    turn(n2)
    own_c.wait()
    for other in row_devs:
        c_arrived(other)

    chunk = 0
    for part in range(parts):

        def backward(index):
            cols = at(index, WIDE)
            back = dot_nt(c_row[...], w2[part, cols, :])
            for rows in range(row_blocks):
                span_rows = pl.ds(rows * block, block)
                slope = bias[part * row_blocks + rows, :, cols].astype(F32)
                du[span_rows, cols] = (back[rows * block : (rows + 1) * block] * slope).astype(BF)
            z_turned[cols, :] = z[part, :, cols].T

        loop(part_cols // WIDE, backward)
        tick(("u", part, 0))

        def outer_tile(chunk, tile, place):
            put(chunk, dot_nn(z_turned[...], c_row[:, at(tile, WIDE)]), place)

        chunk = tiles(OUTER_SPLIT[part], chunk, "o", part, outer_tile)

        def inner_tile(chunk, tile, place):
            put(chunk, dot_nn(turned[...], du[:, at(tile, WIDE)]), place)

        chunk = tiles(INNER_SPLIT[part], chunk, "n", part, inner_tile)

        def add_up(index):
            cols = at(index, WIDE)
            back = dot_nt(du[...], w1[part, cols, :])
            if part == 0:
                acc_b[:, cols] = back
            else:
                acc_b[:, cols] += back

        loop(width // WIDE, add_up)
        tick(("s", part, 0))

    sums[...] = jnp.zeros_like(sums)

    def back_second(index):
        rows = at(index, block)
        values = mid[rows, :]
        back = acc_b[rows, :]
        factor = lax.rsqrt(jnp.mean(values * values, axis=-1, keepdims=True) + EPS)
        sums[1:2, :] += jnp.sum(back * values * factor, axis=0, keepdims=True)
        scaled = back * gain_two
        inside = jnp.mean(scaled * values, axis=-1, keepdims=True)
        total = c_row[rows, :].astype(F32) + factor * scaled - values * (factor * factor * factor * inside)
        acc_b[rows, :] = total
        n2[rows, :] = total.astype(BF)

    loop(seq_count, back_second)
    tick(("r", 0, 0))

    def back_out(index):
        cols = at(index, WIDE)
        c_row[:, cols] = dot_nt(n2[...], wo[cols, :]).astype(BF)

    loop(width // WIDE, back_out)
    tick(("r", 0, 1))

    def attend_back(pair):
        cols = at(pair, LANES)
        keys = k[:, cols]
        values = v[:, cols]
        queries = q[:, cols]
        backs = c_row[:, cols]
        product = backs.astype(F32) * o[:, cols].astype(F32)
        for half in range(2):
            head = 2 * pair + half
            dot_sum = jnp.sum(half_of(product, half), axis=-1, keepdims=True)
            tacc[...] = jnp.zeros_like(tacc)
            for tile in range(length // WIDE):
                rows = pl.ds(tile * WIDE, WIDE)
                back = dot_nt(half_of(backs[tile * WIDE : (tile + 1) * WIDE], half), values)
                for part in range(WIDE // block):
                    base = tile * WIDE + part * block
                    start = vec_len // 2 - base
                    score = probs[head, pl.ds(base, block), :].astype(F32) * (
                        back[part * block : (part + 1) * block] - dot_sum[base : base + block]
                    )
                    tacc[:, pl.ds(start, length)] += score
                    dsc[pl.ds(base, block), pl.ds(half * length, length)] = score.astype(BF)
            rows = tacc[...]
            size = block
            while size > 8:
                size //= 2
                rows = rows[:size] + pltpu.roll(rows[size:], vec_len - size, 1)
            for shift in (4, 2, 1):
                rows = jnp.where((sub & shift) != 0, pltpu.roll(rows, vec_len - shift, 1), rows)
            vec[pl.ds(head, 1), :] = jnp.sum(rows, axis=0, keepdims=True)
        z[0, :, cols] = (
            dot_nn(dsc[:, pl.ds(0, length)], half_of(keys, 0)) + dot_nn(dsc[:, pl.ds(length, length)], half_of(keys, 1))
        ).astype(BF)
        z[1, :, cols] = (
            dot_tn(dsc[:, pl.ds(0, length)], half_of(queries, 0)) + dot_tn(dsc[:, pl.ds(length, length)], half_of(queries, 1))
        ).astype(BF)
        z[2, :, cols] = (
            dot_tn(probs[2 * pair], half_of(backs, 0)) + dot_tn(probs[2 * pair + 1], half_of(backs, 1))
        ).astype(BF)

    own_y.wait()
    y_sent()
    for pair in range(pairs):
        attend_back(pair)
        tick(("h", pair, 0))

    def back_project(index):
        cols = at(index, WIDE)
        span_cols = pl.ds(0, width)
        mid[:, cols] = (
            dot_nt(z[0, :, span_cols], wq[cols, :])
            + dot_nt(z[1, :, span_cols], wk[cols, :])
            + dot_nt(z[2, :, span_cols], wv[cols, :])
        )

    loop(width // WIDE, back_project)
    tick(("d", 0, 0))

    def back_first(index):
        rows = at(index, block)
        values = x_row[rows, :].astype(F32)
        back = mid[rows, :]
        factor = lax.rsqrt(jnp.mean(values * values, axis=-1, keepdims=True) + EPS)
        sums[0:1, :] += jnp.sum(back * values * factor, axis=0, keepdims=True)
        scaled = back * gain_one
        inside = jnp.mean(scaled * values, axis=-1, keepdims=True)
        total = acc_b[rows, :] + factor * scaled - values * (factor * factor * factor * inside)
        du[rows, pl.ds(0, width)] = total.astype(BF)

    loop(seq_count, back_first)
    table_sum = lax.dot_general(
        vec[pl.ds(0, heads), :],
        one_hot,
        (((1,), (1,)), ((), ())),
        precision=HIGH,
        preferred_element_type=F32,
    )
    small[0] = jnp.zeros(small.shape[1:], F32)
    for share in range(GROUP):
        own = pl.ds(share, 1)
        small[0, own, pl.ds(0, row_share)] = sums[0:1, share * row_share : (share + 1) * row_share]
        small[0, own, pl.ds(LANES, row_share)] = sums[1:2, share * row_share : (share + 1) * row_share]
    small[0, pl.ds(8, heads), pl.ds(0, bucket_count)] = table_sum
    small_copy(0).start()
    own_i.start()
    tick(("i", 0, 0))

    turn(o)

    def attn_out_tile(chunk, tile, place):
        put(chunk, dot_nn(turned[...], n2[:, at(tile, WIDE)]), place)

    chunk = tiles(ATTN_SPLIT, chunk, "a", 0, attn_out_tile)
    turn(n1)
    for group in range(width // WIDE):

        def group_tile(chunk, tile, place):
            put(chunk, dot_nn(turned[...], z[tile, :, pl.ds(group * WIDE, WIDE)]), place)

        chunk = tiles(GROUP_SPLIT[group], chunk, "g", group, group_tile)
    tick(("e", 0, 0))
    for step in range(5):
        small_copy(step).wait_send()
    settle()
    own_i.wait()
    for other in row_devs:
        y_arrived(other)
        i_arrived(other)
    x_sent()
    c_sent()
    i_sent()


PLAN = {
    ("y", 0, 0): (("y", 0),),
    ("n", 0, 1): ((0, 0), ("y", 1)),
    ("s", 0, 0): ((0, 1), (0, 2)),
    ("o", 1, 1): (("y", 2),),
    ("n", 1, 0): ((1, 0),),
    ("n", 1, 1): ((1, 1),),
    ("s", 1, 0): ((0, 3), (0, 4), (0, 5), (0, 6)),
    ("u", 2, 0): ((2, 0), (1, 2)),
    ("o", 2, 0): ((2, 1),),
    ("o", 2, 1): ((1, 3),),
    ("s", 2, 0): ((2, 2),),
    ("r", 0, 0): ((2, 3), (1, 4)),
    ("r", 0, 1): ((1, 5),),
    ("h", 0, 0): ((0, 7), (0, 8), (0, 9), (0, 10), (0, 11)),
    ("h", 1, 0): ((3, 0), (3, 1), (2, 4), (2, 5), (1, 6)),
    ("h", 2, 0): ((1, 7),),
    ("h", 3, 0): ((3, 2),),
    ("h", 4, 0): ((4, 0), (3, 3), (2, 6)),
    ("h", 5, 0): ((4, 1), (2, 7), (1, 8)),
    ("d", 0, 0): ((4, 2), (1, 9)),
    ("i", 0, 0): ((5, 0), (5, 1), (4, 3), (3, 4), (2, 8), (1, 10), ("i", 0)),
    ("a", 0, 0): ((5, 2), (3, 5), (2, 9), (1, 11), ("s", 0)),
    ("g", 0, 0): ((5, 3), (3, 6), (2, 10)),
    ("g", 1, 0): ((4, 4), (3, 7), (0, 12), ("s", 1)),
    ("g", 2, 0): ((2, 11), (0, 13)),
    ("e", 0, 0): (("s", 2), (4, 5), (3, 8), (5, 4), (1, 12), (0, 14), (4, 6), (5, 5), (4, 7), ("i", 1), (3, 9), (1, 13), (0, 15), (5, 6), (4, 8), (2, 12), (3, 10), (3, 11), (5, 7), ("s", 3), (1, 14), (2, 13), (0, 16), (1, 15), (5, 8), (1, 16), (2, 14), (2, 15), (4, 9), (2, 16), (4, 10), (5, 9), (3, 12), (4, 11), ("s", 4), (5, 10), ("i", 2), (3, 13), (5, 11), (4, 12), (3, 14), (3, 15), (4, 13), (3, 16), (4, 14), (5, 12), (4, 15), (4, 16), (5, 13), (5, 14), (5, 15), (5, 16)),
}


def unpack_kernel(parts, row_share, shares_hbm, small_hbm, layer_in, grad_in_in, *refs):
    outs, held, (shares, small, through, sems, in_sems) = refs[:11], refs[11:20], refs[20:]
    moves = [pltpu.make_async_copy(through.at[index], outs[index], sems.at[index]) for index in range(2)]
    loads = [
        pltpu.make_async_copy(src, dst, in_sems.at[index])
        for index, (src, dst) in enumerate(
            ((shares_hbm, shares), (small_hbm, small), (layer_in, through.at[0]), (grad_in_in, through.at[1]))
        )
    ]
    for copy in loads:
        copy.start()
    for copy in loads:
        copy.wait()
    for copy in moves:
        copy.start()
    gq, gk, gv, go, gi, gf, gain_a, gain_f, table = held
    blocks = gq.shape[1] // LANES
    part_rows = blocks * LANES + GROUP * row_share

    def take(start, rows):
        return shares[pl.ds(start, rows), :].astype(F32)

    def give(index):
        moves.append(pltpu.make_async_copy(held[index], outs[2 + index], sems.at[2 + index]))
        moves[-1].start()

    for part in range(parts):
        for col in range(blocks):
            gf[pl.ds(part * LANES, LANES), pl.ds(col * LANES, LANES)] = take(part * part_rows + col * LANES, LANES)
    give(5)
    for part in range(parts):
        base = part * part_rows + blocks * LANES
        for share in range(GROUP):
            gi[:, pl.ds((share * parts + part) * LANES, LANES)] = take(base + share * row_share, row_share)
    give(4)
    base = parts * part_rows
    for col in range(blocks):
        go[:, pl.ds(col * LANES, LANES)] = take(base + col * row_share, row_share)
    give(3)
    for index, ref in enumerate((gq, gk, gv)):
        for group in range(blocks // 2):
            for side in range(2):
                place = base + (1 + group) * blocks * row_share + (2 * index + side) * row_share
                ref[:, pl.ds(group * WIDE + side * LANES, LANES)] = take(place, row_share)
        give(index)
    own = lax.broadcasted_iota(jnp.int32, (GROUP, row_share), 0) == lax.axis_index("dp") % GROUP
    for first, ref in ((0, gain_a), (LANES, gain_f)):
        ref[...] = jnp.sum(jnp.where(own, small[pl.ds(0, GROUP), pl.ds(first, row_share)], 0.0), axis=0)
    table[...] = small[pl.ds(8, table.shape[0]), pl.ds(0, table.shape[1])]
    for index in (6, 7, 8):
        give(index)
    for copy in moves:
        copy.wait()


def on_device(
    dp_count,
    hidden_in,
    query_lengths,
    doc_lengths,
    w_query,
    w_key,
    w_value,
    w_attn_out,
    w_inner,
    w_outer,
    gain_attn,
    gain_ffn,
    bias_table,
    cotangent,
):
    rows, block, width = hidden_in.shape
    length = rows * block
    bucket_count, heads = bias_table.shape
    ffn = w_inner.shape[1]
    part_cols = GROUP * LANES
    parts = ffn // part_cols
    vec_len = 2 * length
    lo_count = dp_count // GROUP
    row_share = width // GROUP

    def vm(*shape, dtype=BF):
        return pltpu.VMEM(shape, dtype)

    def dma(count):
        return pltpu.SemaphoreType.DMA((count,))

    hbm = pl.BlockSpec(memory_space=pl.ANY)
    vmem = pl.BlockSpec(memory_space=pltpu.VMEM)
    smem = pl.BlockSpec(memory_space=pltpu.SMEM)
    small_rows = 8 + heads
    small_cols = 2 * LANES
    total_rows = sum(chunk_rows(row_share))
    layer_raw, grad_raw, shares, small = pl.pallas_call(
        partial(layer_kernel, lo_count),
        out_shape=(
            jax.ShapeDtypeStruct(hidden_in.shape, BF),
            jax.ShapeDtypeStruct(hidden_in.shape, BF),
            jax.ShapeDtypeStruct((total_rows, LANES), BF),
            jax.ShapeDtypeStruct((small_rows, small_cols), F32),
        ),
        in_specs=[hbm, hbm, smem, smem] + [hbm] * 9,
        out_specs=(hbm, hbm, hbm, vmem),
        scratch_shapes=[
            vm(length, width),
            vm(length, width),
            vm(width, width),
            vm(width, width),
            vm(width, width),
            vm(width, width),
            vm(parts, width, part_cols),
            vm(parts, part_cols, width),
            vm(length, width),
            vm(length, width),
            vm(length, width),
            vm(length, width),
            vm(heads, length, length),
            vm(length, width),
            vm(length, width),
            vm(width),
            vm(width),
            vm(heads, bucket_count),
            vm(part_cols, length),
            vm(width, length),
            vm(length, width, dtype=F32),
            vm(length, width, dtype=F32),
            vm(parts, length, part_cols),
            vm(length, part_cols),
            vm(heads, block, vec_len),
            vm(16, vec_len, dtype=F32),
            vm(8, width, dtype=F32),
            vm(length, 2 * length),
            vm(block, vec_len, dtype=F32),
            vm(SLOTS, 2, 2, 2, max(chunk_rows(row_share)), LANES),
            vm(2, 2, total_rows, LANES),
            vm(2, total_rows, LANES),
            vm(total_rows, LANES),
            vm(total_rows, LANES),
            vm(total_rows, LANES),
            vm(5, small_rows, small_cols, dtype=F32),
            vm(5, small_rows, small_cols, dtype=F32),
            dma(4 + 2 * parts),
            dma(7),
        ]
        + [dma(rows)] * 8
        + [dma(CHUNKS)] * 13
        + [dma(5)] * 2,
        compiler_params=pltpu.CompilerParams(
            collective_id=0, has_side_effects=True, vmem_limit_bytes=64 * 2**20 - 2**19
        ),
    )(
        hidden_in,
        cotangent,
        query_lengths,
        doc_lengths,
        w_query,
        w_key,
        w_value,
        w_attn_out,
        w_inner,
        w_outer,
        gain_attn,
        gain_ffn,
        bias_table.T,
    )
    grad_shapes = [(row_share, width)] * 4 + [(row_share, ffn), (ffn // GROUP, width), (row_share,), (row_share,)]
    grad_shapes.append((heads, bucket_count))
    layer_out, grad_in, *grads = pl.pallas_call(
        partial(unpack_kernel, parts, row_share),
        out_shape=[jax.ShapeDtypeStruct(hidden_in.shape, BF)] * 2
        + [jax.ShapeDtypeStruct(shape, F32) for shape in grad_shapes],
        in_specs=[hbm] * 4,
        out_specs=[hbm] * 11,
        scratch_shapes=[vm(*shape, dtype=F32) for shape in grad_shapes]
        + [vm(total_rows, LANES), vm(small_rows, small_cols, dtype=F32), vm(2, *hidden_in.shape), dma(11), dma(4)],
        compiler_params=pltpu.CompilerParams(vmem_limit_bytes=64 * 2**20 - 2**19),
    )(shares, small, layer_raw, grad_raw)
    if lo_count > 1:
        high = lax.axis_index("dp") // lo_count

        def spread(part):
            whole = jnp.zeros((GROUP,) + part.shape, F32)
            whole = lax.dynamic_update_index_in_dim(whole, part, high, 0)
            whole = whole.reshape((GROUP * part.shape[0],) + part.shape[1:])
            return lax.psum_scatter(whole, "dp", scatter_dimension=0, tiled=True)

        small = lax.psum(small, "dp") / GROUP
        gain_rows = width // dp_count
        start = lax.axis_index("dp") * gain_rows
        gains = [
            lax.dynamic_slice_in_dim(small[:GROUP, first : first + row_share].reshape(width), start, gain_rows)
            for first in (0, LANES)
        ]
        grads = [spread(part) for part in grads[:6]] + gains + [small[8 : 8 + heads, :bucket_count]]
    return (layer_out, grad_in, *grads[:8], grads[8].T)


def solution(mesh):
    return jax.shard_map(
        partial(on_device, mesh.shape["dp"]),
        mesh=mesh,
        in_specs=(
            P("dp", "seq", None),
            P("dp"),
            P("dp"),
            P(),
            P(),
            P(),
            P(),
            P(),
            P(),
            P(),
            P(),
            P(),
            P("dp", "seq", None),
        ),
        out_specs=(
            P("dp", "seq", None),
            P("dp", "seq", None),
            P("dp", None),
            P("dp", None),
            P("dp", None),
            P("dp", None),
            P("dp", None),
            P("dp", None),
            P("dp"),
            P("dp"),
            P(),
        ),
        check_vma=False,
    )
```

```python
from functools import partial

import jax
import jax.numpy as jnp
from jax import lax
from jax.experimental import pallas as pl
from jax.experimental.pallas import tpu as pltpu
from jax.sharding import PartitionSpec as P

EPS = 1e-06
NEG = -1000000000.0
LIMITS = (12, 16, 23, 32, 46, 64, 91)
HIGH = lax.Precision.HIGHEST
MESH = pl.DeviceIdType.MESH
BF = jnp.bfloat16
F32 = jnp.float32

GROUP = 8
LANES = 128
WIDE = 256
SLOTS = 5
OUTER_SPLIT = ((2, 1), (2, 1), (2, 1))
INNER_SPLIT = ((2, 2), (2, 2), (2, 2))
ATTN_SPLIT = (3,)
GROUP_SPLIT = ((3,), (3,), (2, 1))


def chunk_rows(row_share):
    rows = []
    for outer, inner in zip(OUTER_SPLIT, INNER_SPLIT):
        rows += [count * 2 * LANES for count in outer] + [count * 2 * row_share for count in inner]
    for split in (ATTN_SPLIT,) + GROUP_SPLIT:
        rows += [count * 2 * row_share for count in split]
    return rows


CHUNKS = len(chunk_rows(96))


def dot_nn(left, right):
    return jnp.dot(left, right, preferred_element_type=F32)


def dot_nt(left, right):
    return lax.dot_general(left, right, (((1,), (1,)), ((), ())), preferred_element_type=F32)


def dot_tn(left, right):
    return lax.dot_general(left, right, (((0,), (0,)), ((), ())), preferred_element_type=F32)


def buckets(relative):
    distance = jnp.abs(relative)
    far_bucket = 8 + sum(((distance >= thresh).astype(jnp.int32) for thresh in LIMITS))
    return jnp.where(relative > 0, 16, 0) + jnp.where(distance < 8, distance, far_bucket)


def loop(count, body):
    lax.fori_loop(0, count, lambda index, none: (body(index), none)[1], None)


def at(index, size):
    if isinstance(index, int):
        return pl.ds(index * size, size)
    return pl.ds(pl.multiple_of(index * size, size), size)


def layer_kernel(
    lo_count,
    hidden,
    cot,
    query_len,
    doc_len,
    wq_hbm,
    wk_hbm,
    wv_hbm,
    wo_hbm,
    w1_hbm,
    w2_hbm,
    gain1_hbm,
    gain2_hbm,
    table_hbm,
    layer_out,
    grad_in,
    shares,
    small_out,
    x_row,
    c_row,
    wq,
    wk,
    wv,
    wo,
    w1,
    w2,
    n1,
    q,
    k,
    v,
    probs,
    o,
    n2,
    gain1,
    gain2,
    table,
    z_turned,
    turned,
    mid,
    acc_b,
    z,
    du,
    bias,
    vec,
    sums,
    dsc,
    tacc,
    grads,
    r_core,
    r_first,
    r_second,
    z_end,
    z_mid,
    small,
    small_in,
    w_sem,
    own_sem,
    x_send,
    x_recv,
    c_send,
    c_recv,
    y_send,
    y_recv,
    i_send,
    i_recv,
    core_send,
    core_recv,
    first_send,
    first_recv,
    second_send,
    second_recv,
    end_send,
    end_recv,
    mid_send,
    mid_recv,
    back_send,
    back_recv,
    share_sem,
    small_send,
    small_recv,
):
    dp = lax.axis_index("dp")
    sq = lax.axis_index("seq")
    seq_count, block, width = hidden.shape
    length = x_row.shape[0]
    heads, bucket_count = table.shape
    pairs = heads // 2
    row_share = width // GROUP
    parts = w1_hbm.shape[1] // (GROUP * LANES)
    part_cols = GROUP * LANES
    vec_len = vec.shape[1]

    high = dp // lo_count
    bit0 = lax.rem(high, 2)
    bit1 = lax.rem(high // 2, 2)
    bit2 = lax.rem(high // 4, 2)
    step1 = 2 * lo_count * (1 - 2 * bit1)
    step2 = 4 * lo_count * (1 - 2 * bit2)
    core_dev = (dp + lo_count * (1 - 2 * bit0), sq)
    first_dev = (dp + (1 - bit0) * step1 + bit0 * step2, sq)
    second_dev = (dp + bit0 * step1 + (1 - bit0) * step2, sq)
    first_bit = (1 - bit0) * bit1 + bit0 * bit2
    second_bit = (1 - bit0) * bit2 + bit0 * bit1
    pair_dev = (dp, sq + 1 - 2 * lax.rem(sq, 2))
    mid_dev = (dp, 3 - sq)
    is_end = jnp.logical_or(sq == 0, sq == seq_count - 1)
    is_mid = jnp.logical_not(is_end)
    row_devs = [lax.rem(sq + step, seq_count) for step in range(1, seq_count)]

    def remote(src, dst, send, recv, device):
        return pltpu.make_async_remote_copy(
            src_ref=src, dst_ref=dst, send_sem=send, recv_sem=recv, device_id=device, device_id_type=MESH
        )

    barrier = pltpu.get_barrier_semaphore()
    for device in [core_dev, first_dev, second_dev] + [(dp, other) for other in row_devs]:
        pl.semaphore_signal(barrier, inc=1, device_id=device, device_id_type=MESH)
    pl.semaphore_wait(barrier, 3 + len(row_devs))

    def deal(src_of, dst_of, send, recv):
        def copy(index):
            other = row_devs[index]
            return remote(src_of(other), dst_of(sq), send.at[index], recv.at[sq], (dp, other))

        def start(index):
            copy(index).start()

        def arrived(other):
            remote(src_of(other), dst_of(other), send.at[0], recv.at[other], (dp, other)).wait_recv()

        def sent():
            for index in range(len(row_devs)):
                copy(index).wait_send()

        return start, arrived, sent

    x_start, x_arrived, x_sent = deal(
        lambda other: hidden.at[other], lambda src: x_row.at[at(src, block)], x_send, x_recv
    )
    c_start, c_arrived, c_sent = deal(
        lambda other: cot.at[other], lambda src: c_row.at[at(src, block)], c_send, c_recv
    )
    y_start, y_arrived, y_sent = deal(
        lambda other: dsc.at[at(other, block), pl.ds(0, width)], lambda src: layer_out.at[src], y_send, y_recv
    )
    i_start, i_arrived, i_sent = deal(
        lambda other: du.at[at(other, block), pl.ds(0, width)], lambda src: grad_in.at[src], i_send, i_recv
    )
    own_x = pltpu.make_async_copy(hidden.at[sq], x_row.at[at(sq, block)], own_sem.at[0])
    own_c = pltpu.make_async_copy(cot.at[sq], c_row.at[at(sq, block)], own_sem.at[1])
    own_y = pltpu.make_async_copy(dsc.at[at(sq, block), pl.ds(0, width)], layer_out.at[sq], own_sem.at[2])
    own_i = pltpu.make_async_copy(du.at[at(sq, block), pl.ds(0, width)], grad_in.at[sq], own_sem.at[3])

    for index in range(len(row_devs)):
        x_start(index)
    own_x.start()
    params = [
        pltpu.make_async_copy(src, dst, own_sem.at[4 + index])
        for index, (src, dst) in enumerate(((gain1_hbm, gain1), (gain2_hbm, gain2), (table_hbm, table)))
    ]
    for copy in params:
        copy.start()
    square = [
        pltpu.make_async_copy(src, dst, w_sem.at[index])
        for index, (src, dst) in enumerate(((wq_hbm, wq), (wk_hbm, wk), (wv_hbm, wv), (wo_hbm, wo)))
    ]
    for copy in square:
        copy.start()

    def part_copies(part):
        span = parts * LANES
        copies = []
        for share in range(GROUP):
            place = pl.ds(share * span + part * LANES, LANES)
            cols = pl.ds(share * LANES, LANES)
            copies.append(pltpu.make_async_copy(w1_hbm.at[:, place], w1.at[part, :, cols], w_sem.at[4 + 2 * part]))
            copies.append(pltpu.make_async_copy(w2_hbm.at[place], w2.at[part, cols], w_sem.at[5 + 2 * part]))
        return copies

    def part_wait(part):
        pltpu.make_async_copy(w1.at[part], w1.at[part], w_sem.at[4 + 2 * part]).wait()
        pltpu.make_async_copy(w2.at[part], w2.at[part], w_sem.at[5 + 2 * part]).wait()

    for part in range(parts):
        for copy in part_copies(part):
            copy.start()
    own_c.start()

    sizes = chunk_rows(row_share)

    def span(chunk):
        return pl.ds(sum(sizes[:chunk]), sizes[chunk])

    def piece(ref, chunk, *index):
        lead = index + (slice(None),) * (len(ref.shape) - 2 - len(index))
        return ref.at[lead + (span(chunk),)]

    def grad_half(chunk, side):
        return grads.at[chunk % SLOTS, side, :, :, pl.ds(0, sizes[chunk])]

    def core_copy(chunk):
        return remote(
            grad_half(chunk, 1 - bit0), piece(r_core, chunk), core_send.at[chunk], core_recv.at[chunk], core_dev
        )

    def first_copy(chunk):
        return remote(
            piece(r_core, chunk, 1 - first_bit),
            piece(r_first, chunk),
            first_send.at[chunk],
            first_recv.at[chunk],
            first_dev,
        )

    def second_copy(chunk):
        return remote(
            piece(r_first, chunk, 1 - second_bit),
            piece(r_second, chunk),
            second_send.at[chunk],
            second_recv.at[chunk],
            second_dev,
        )

    def end_copy(chunk):
        return remote(
            piece(r_second, chunk), piece(z_end, chunk), end_send.at[chunk], end_recv.at[chunk], pair_dev
        )

    def mid_copy(chunk):
        return remote(
            piece(r_second, chunk), piece(z_mid, chunk), mid_send.at[chunk], mid_recv.at[chunk], mid_dev
        )

    def back_copy(chunk):
        return remote(
            piece(z_end, chunk), piece(shares, chunk), back_send.at[chunk], back_recv.at[chunk], pair_dev
        )

    def share_copy(chunk):
        return pltpu.make_async_copy(piece(z_end, chunk), piece(shares, chunk), share_sem.at[chunk])

    def core_done(chunk):
        copy = core_copy(chunk)
        copy.wait_recv()

        def add(index):
            one, two = index // 2, lax.rem(index, 2)
            r_core[one, two, span(chunk)] += grads[chunk % SLOTS, bit0, one, two, pl.ds(0, sizes[chunk])]

        loop(4, add)
        first_copy(chunk).start()
        copy.wait_send()

    def first_done(chunk):
        first_copy(chunk).wait_recv()

        def add(index):
            r_first[index, span(chunk)] += r_core[first_bit, index, span(chunk)]

        loop(2, add)
        second_copy(chunk).start()

    def second_done(chunk):
        second_copy(chunk).wait_recv()
        r_second[span(chunk)] += r_first[second_bit, span(chunk)]

        @pl.when(is_end)
        def _():
            end_copy(chunk).start()

    def end_done(chunk):
        @pl.when(is_mid)
        def _():
            end_copy(chunk).wait_recv()
            r_second[span(chunk)] += z_end[span(chunk)]
            mid_copy(chunk).start()

    def mid_done(chunk):
        @pl.when(is_mid)
        def _():
            mid_copy(chunk).wait_recv()
            z_end[span(chunk)] = r_second[span(chunk)] + z_mid[span(chunk)]
            back_copy(chunk).start()
            share_copy(chunk).start()

    def back_done(chunk):
        @pl.when(is_end)
        def _():
            back_copy(chunk).wait_recv()

    stages = (core_done, first_done, second_done, end_done, mid_done, back_done)

    def settle():
        for chunk in range(CHUNKS):
            first_copy(chunk).wait_send()
            second_copy(chunk).wait_send()

        @pl.when(is_end)
        def _():
            for chunk in range(CHUNKS):
                end_copy(chunk).wait_send()

        @pl.when(is_mid)
        def _():
            for chunk in range(CHUNKS):
                mid_copy(chunk).wait_send()
                back_copy(chunk).wait_send()
                share_copy(chunk).wait()

    def small_copy(step):
        device = (core_dev, (dp + step1, sq), (dp + step2, sq), pair_dev, (dp, lax.rem(sq + 2, 4)))[step]
        return remote(small.at[step], small_in.at[step], small_send.at[step], small_recv.at[step], device)

    def small_done(step):
        small_copy(step).wait_recv()
        if step < 4:
            small[step + 1] = small[step] + small_in[step]
            small_copy(step + 1).start()
        else:
            small_out[...] = small[step] + small_in[step]

    def tick(spot):
        for what, index in PLAN.get(spot, ()):
            if what == "y":
                y_start(index)
            elif what == "i":
                i_start(index)
            elif what == "s":
                small_done(index)
            else:
                stages[what](index)

    def tiles(split, first, kind, part, body):
        done = 0
        for place, count in enumerate(split):
            chunk = first + place
            if count == 1:
                body(chunk, done, 0)
            else:
                loop(count, lambda index: body(chunk, done + index, index))
            core_copy(chunk).start()
            tick((kind, part, place))
            done += count
        return first + len(split)

    def place_of(share):
        one, two, three = share % 2, (share // 2) % 2, share // 4
        return (one, two, three) if one == 0 else (one, three, two)

    for copy in params:
        copy.wait()
    distance = lax.broadcasted_iota(jnp.int32, (1, vec_len), 1) - vec_len // 2
    bucket_row = buckets(distance)
    one_hot = (
        jnp.broadcast_to(bucket_row, (bucket_count, vec_len))
        == lax.broadcasted_iota(jnp.int32, (bucket_count, vec_len), 0)
    ).astype(F32)
    vec[pl.ds(0, heads), :] = dot_nn(table[...], one_hot.astype(BF))
    sub = lax.broadcasted_iota(jnp.int32, (8, vec_len), 0)

    def build_bias(head):
        rows = jnp.broadcast_to(vec[pl.ds(head, 1), :], (8, vec_len))
        for shift in (1, 2, 4):
            rows = jnp.where((sub & shift) != 0, pltpu.roll(rows, shift, 1), rows)
        shift = 8
        while shift < block:
            rows = jnp.concatenate([rows, pltpu.roll(rows, shift, 1)], axis=0)
            shift *= 2
        bias[head] = rows.astype(BF)

    loop(heads, build_bias)

    total_len = query_len[sq] + doc_len[sq]
    key_mask = jnp.where(
        lax.broadcasted_iota(jnp.int32, (1, length), 1) < total_len, jnp.float32(0), jnp.float32(NEG)
    )
    low_lanes = lax.broadcasted_iota(jnp.int32, (1, LANES), 1) < LANES // 2

    def half_of(values, half):
        keep = low_lanes if half == 0 else jnp.logical_not(low_lanes)
        return jnp.where(keep, values, jnp.zeros_like(values))

    gain_one = gain1[...].astype(F32).reshape(1, width)
    gain_two = gain2[...].astype(F32).reshape(1, width)

    own_x.wait()
    for other in row_devs:
        x_arrived(other)
    for index in range(len(row_devs)):
        c_start(index)

    def norm_first(index):
        rows = at(index, block)
        values = x_row[rows, :].astype(F32)
        factor = lax.rsqrt(jnp.mean(values * values, axis=-1, keepdims=True) + EPS)
        n1[rows, :] = (values * factor * gain_one).astype(BF)

    loop(seq_count, norm_first)
    for copy in square:
        copy.wait()

    def project(index):
        cols = at(index, WIDE)
        q[:, cols] = dot_nn(n1[...], wq[:, cols]).astype(BF)
        k[:, cols] = dot_nn(n1[...], wk[:, cols]).astype(BF)
        v[:, cols] = dot_nn(n1[...], wv[:, cols]).astype(BF)

    loop(width // WIDE, project)

    def attend(pair):
        cols = at(pair, LANES)
        keys = k[:, cols]
        values = v[:, cols]
        for tile in range(length // WIDE):
            rows = pl.ds(tile * WIDE, WIDE)
            queries = q[rows, cols]
            total = None
            for half in range(2):
                head = 2 * pair + half
                scores = dot_nt(half_of(queries, half), keys)
                weights = []
                for part in range(WIDE // block):
                    start = vec_len // 2 - tile * WIDE - part * block
                    here = scores[part * block : (part + 1) * block]
                    here = here + bias[head, :, pl.ds(start, length)].astype(F32) + key_mask
                    here = jnp.exp(here - jnp.max(here, axis=-1, keepdims=True))
                    scale = 1.0 / jnp.sum(here, axis=-1, keepdims=True)
                    weights.append((here * scale).astype(BF))
                weights = jnp.concatenate(weights, axis=0)
                probs[head, rows, :] = weights
                term = dot_nn(weights, half_of(values, half))
                total = term if total is None else total + term
            o[rows, cols] = total.astype(BF)

    loop(pairs, attend)

    def attn_out(index):
        cols = at(index, WIDE)
        mid[:, cols] = x_row[:, cols].astype(F32) + dot_nn(o[...], wo[:, cols])

    loop(width // WIDE, attn_out)

    def norm_second(index):
        rows = at(index, block)
        values = mid[rows, :]
        factor = lax.rsqrt(jnp.mean(values * values, axis=-1, keepdims=True) + EPS)
        n2[rows, :] = (values * factor * gain_two).astype(BF)

    loop(seq_count, norm_second)

    def turn(source):
        def body(index):
            span = at(index, LANES)
            turned[span, :] = source[:, span].T

        loop(width // LANES, body)

    def put(chunk, values, tile):
        rows = values.shape[0] // GROUP
        for share in range(GROUP):
            for side in range(2):
                one, two, three = place_of(share)
                place = (2 * tile + side) * rows
                if not isinstance(tile, int):
                    place = pl.multiple_of(place, rows)
                grads[chunk % SLOTS, one, two, three, pl.ds(place, rows), :] = values[
                    share * rows : (share + 1) * rows, side * LANES : (side + 1) * LANES
                ].astype(BF)

    row_blocks = length // block
    for part in range(parts):
        part_wait(part)

        def forward(index):
            cols = at(index, WIDE)
            inner = dot_nn(n2[...], w1[part, :, cols])
            square_in = inner * inner
            bend = jnp.tanh(inner * (0.7978845608028654 + (0.7978845608028654 * 0.044715) * square_in))
            gate = 0.5 + 0.5 * bend
            active = inner * gate
            z[part, :, cols] = active.astype(BF)
            slope = 1.5957691216057308 + (6 * 0.7978845608028654 * 0.044715) * square_in
            slope = (gate + active * ((1 - gate) * slope)).astype(BF)
            for rows in range(row_blocks):
                bias[part * row_blocks + rows, :, cols] = slope[rows * block : (rows + 1) * block]

        def forward_two(index):
            forward(2 * index)
            forward(2 * index + 1)

        loop(part_cols // (2 * WIDE), forward_two)

    def layer_tile(index):
        cols = at(index, WIDE)
        total = mid[:, cols]
        for part in range(parts):
            total = total + dot_nn(z[part], w2[part, :, cols])
        dsc[:, cols] = total.astype(BF)

    loop(width // WIDE, layer_tile)
    own_y.start()
    tick(("y", 0, 0))
    turn(n2)
    own_c.wait()
    for other in row_devs:
        c_arrived(other)

    chunk = 0
    for part in range(parts):

        def backward(index):
            cols = at(index, WIDE)
            back = dot_nt(c_row[...], w2[part, cols, :])
            for rows in range(row_blocks):
                span_rows = pl.ds(rows * block, block)
                slope = bias[part * row_blocks + rows, :, cols].astype(F32)
                du[span_rows, cols] = (back[rows * block : (rows + 1) * block] * slope).astype(BF)
            z_turned[cols, :] = z[part, :, cols].T

        loop(part_cols // WIDE, backward)
        tick(("u", part, 0))

        def outer_tile(chunk, tile, place):
            put(chunk, dot_nn(z_turned[...], c_row[:, at(tile, WIDE)]), place)

        chunk = tiles(OUTER_SPLIT[part], chunk, "o", part, outer_tile)

        def inner_tile(chunk, tile, place):
            put(chunk, dot_nn(turned[...], du[:, at(tile, WIDE)]), place)

        chunk = tiles(INNER_SPLIT[part], chunk, "n", part, inner_tile)

        def add_up(index):
            cols = at(index, WIDE)
            back = dot_nt(du[...], w1[part, cols, :])
            if part == 0:
                acc_b[:, cols] = back
            else:
                acc_b[:, cols] += back

        loop(width // WIDE, add_up)
        tick(("s", part, 0))

    sums[...] = jnp.zeros_like(sums)

    def back_second(index):
        rows = at(index, block)
        values = mid[rows, :]
        back = acc_b[rows, :]
        factor = lax.rsqrt(jnp.mean(values * values, axis=-1, keepdims=True) + EPS)
        sums[1:2, :] += jnp.sum(back * values * factor, axis=0, keepdims=True)
        scaled = back * gain_two
        inside = jnp.mean(scaled * values, axis=-1, keepdims=True)
        total = c_row[rows, :].astype(F32) + factor * scaled - values * (factor * factor * factor * inside)
        acc_b[rows, :] = total
        n2[rows, :] = total.astype(BF)

    loop(seq_count, back_second)
    tick(("r", 0, 0))

    def back_out(index):
        cols = at(index, WIDE)
        c_row[:, cols] = dot_nt(n2[...], wo[cols, :]).astype(BF)

    loop(width // WIDE, back_out)
    tick(("r", 0, 1))

    def attend_back(pair):
        cols = at(pair, LANES)
        keys = k[:, cols]
        values = v[:, cols]
        queries = q[:, cols]
        backs = c_row[:, cols]
        product = backs.astype(F32) * o[:, cols].astype(F32)
        for half in range(2):
            head = 2 * pair + half
            dot_sum = jnp.sum(half_of(product, half), axis=-1, keepdims=True)
            tacc[...] = jnp.zeros_like(tacc)
            for tile in range(length // WIDE):
                rows = pl.ds(tile * WIDE, WIDE)
                back = dot_nt(half_of(backs[tile * WIDE : (tile + 1) * WIDE], half), values)
                for part in range(WIDE // block):
                    base = tile * WIDE + part * block
                    start = vec_len // 2 - base
                    score = probs[head, pl.ds(base, block), :].astype(F32) * (
                        back[part * block : (part + 1) * block] - dot_sum[base : base + block]
                    )
                    tacc[:, pl.ds(start, length)] += score
                    dsc[pl.ds(base, block), pl.ds(half * length, length)] = score.astype(BF)
            rows = tacc[...]
            size = block
            while size > 8:
                size //= 2
                rows = rows[:size] + pltpu.roll(rows[size:], vec_len - size, 1)
            for shift in (4, 2, 1):
                rows = jnp.where((sub & shift) != 0, pltpu.roll(rows, vec_len - shift, 1), rows)
            vec[pl.ds(head, 1), :] = jnp.sum(rows, axis=0, keepdims=True)
        z[0, :, cols] = (
            dot_nn(dsc[:, pl.ds(0, length)], half_of(keys, 0)) + dot_nn(dsc[:, pl.ds(length, length)], half_of(keys, 1))
        ).astype(BF)
        z[1, :, cols] = (
            dot_tn(dsc[:, pl.ds(0, length)], half_of(queries, 0)) + dot_tn(dsc[:, pl.ds(length, length)], half_of(queries, 1))
        ).astype(BF)
        z[2, :, cols] = (
            dot_tn(probs[2 * pair], half_of(backs, 0)) + dot_tn(probs[2 * pair + 1], half_of(backs, 1))
        ).astype(BF)

    own_y.wait()
    y_sent()
    for pair in range(pairs):
        attend_back(pair)
        tick(("h", pair, 0))

    def back_project(index):
        cols = at(index, WIDE)
        span_cols = pl.ds(0, width)
        mid[:, cols] = (
            dot_nt(z[0, :, span_cols], wq[cols, :])
            + dot_nt(z[1, :, span_cols], wk[cols, :])
            + dot_nt(z[2, :, span_cols], wv[cols, :])
        )

    loop(width // WIDE, back_project)
    tick(("d", 0, 0))

    def back_first(index):
        rows = at(index, block)
        values = x_row[rows, :].astype(F32)
        back = mid[rows, :]
        factor = lax.rsqrt(jnp.mean(values * values, axis=-1, keepdims=True) + EPS)
        sums[0:1, :] += jnp.sum(back * values * factor, axis=0, keepdims=True)
        scaled = back * gain_one
        inside = jnp.mean(scaled * values, axis=-1, keepdims=True)
        total = acc_b[rows, :] + factor * scaled - values * (factor * factor * factor * inside)
        du[rows, pl.ds(0, width)] = total.astype(BF)

    loop(seq_count, back_first)
    table_sum = lax.dot_general(
        vec[pl.ds(0, heads), :],
        one_hot,
        (((1,), (1,)), ((), ())),
        precision=HIGH,
        preferred_element_type=F32,
    )
    small[0] = jnp.zeros(small.shape[1:], F32)
    for share in range(GROUP):
        own = pl.ds(share, 1)
        small[0, own, pl.ds(0, row_share)] = sums[0:1, share * row_share : (share + 1) * row_share]
        small[0, own, pl.ds(LANES, row_share)] = sums[1:2, share * row_share : (share + 1) * row_share]
    small[0, pl.ds(8, heads), pl.ds(0, bucket_count)] = table_sum
    small_copy(0).start()
    own_i.start()
    tick(("i", 0, 0))

    turn(o)

    def attn_out_tile(chunk, tile, place):
        put(chunk, dot_nn(turned[...], n2[:, at(tile, WIDE)]), place)

    chunk = tiles(ATTN_SPLIT, chunk, "a", 0, attn_out_tile)
    turn(n1)
    for group in range(width // WIDE):

        def group_tile(chunk, tile, place):
            put(chunk, dot_nn(turned[...], z[tile, :, pl.ds(group * WIDE, WIDE)]), place)

        chunk = tiles(GROUP_SPLIT[group], chunk, "g", group, group_tile)
    tick(("e", 0, 0))
    for step in range(5):
        small_copy(step).wait_send()
    settle()
    own_i.wait()
    for other in row_devs:
        y_arrived(other)
        i_arrived(other)
    x_sent()
    c_sent()
    i_sent()


PLAN = {
    ("y", 0, 0): (("y", 0),),
    ("n", 0, 1): ((0, 0), ("y", 1)),
    ("s", 0, 0): ((0, 1), (0, 2)),
    ("o", 1, 1): (("y", 2),),
    ("n", 1, 0): ((1, 0),),
    ("n", 1, 1): ((1, 1),),
    ("s", 1, 0): ((0, 3), (0, 4), (0, 5), (0, 6)),
    ("u", 2, 0): ((2, 0), (1, 2)),
    ("o", 2, 0): ((2, 1),),
    ("o", 2, 1): ((1, 3),),
    ("s", 2, 0): ((2, 2),),
    ("r", 0, 0): ((2, 3), (1, 4)),
    ("r", 0, 1): ((1, 5),),
    ("h", 0, 0): ((0, 7), (0, 8), (0, 9), (0, 10), (0, 11)),
    ("h", 1, 0): ((3, 0), (3, 1), (2, 4), (2, 5), (1, 6)),
    ("h", 2, 0): ((1, 7),),
    ("h", 3, 0): ((3, 2),),
    ("h", 4, 0): ((4, 0), (3, 3), (2, 6)),
    ("h", 5, 0): ((4, 1), (2, 7), (1, 8)),
    ("d", 0, 0): ((4, 2), (1, 9)),
    ("i", 0, 0): ((5, 0), (5, 1), (4, 3), (3, 4), (2, 8), (1, 10), ("i", 0)),
    ("a", 0, 0): ((5, 2), (3, 5), (2, 9), (1, 11), ("s", 0)),
    ("g", 0, 0): ((5, 3), (3, 6), (2, 10)),
    ("g", 1, 0): ((4, 4), (3, 7), (0, 12), ("s", 1)),
    ("g", 2, 0): ((2, 11), (0, 13)),
    ("e", 0, 0): (("s", 2), (4, 5), (3, 8), (5, 4), (1, 12), (0, 14), (4, 6), (5, 5), (4, 7), ("i", 1), (3, 9), (1, 13), (0, 15), (5, 6), (4, 8), (2, 12), (3, 10), (3, 11), (5, 7), ("s", 3), (1, 14), (2, 13), (0, 16), (1, 15), (5, 8), (1, 16), (2, 14), (2, 15), (4, 9), (2, 16), (4, 10), (5, 9), (3, 12), (4, 11), ("s", 4), (5, 10), ("i", 2), (3, 13), (5, 11), (4, 12), (3, 14), (3, 15), (4, 13), (3, 16), (4, 14), (5, 12), (4, 15), (4, 16), (5, 13), (5, 14), (5, 15), (5, 16)),
}


def unpack_kernel(parts, row_share, shares_hbm, small_hbm, layer_in, grad_in_in, *refs):
    outs, held, (shares, small, through, sems, in_sems) = refs[:11], refs[11:20], refs[20:]
    moves = [pltpu.make_async_copy(through.at[index], outs[index], sems.at[index]) for index in range(2)]
    gq, gk, gv, go, gi, gf, gain_a, gain_f, table = held
    blocks = gq.shape[1] // LANES
    part_rows = blocks * LANES + GROUP * row_share

    def load_share(index, rows):
        place = pl.ds(index * part_rows, rows)
        return pltpu.make_async_copy(shares_hbm.at[place], shares.at[place], in_sems.at[3 + index])

    pieces = [load_share(part, part_rows) for part in range(parts)]
    pieces.append(load_share(parts, shares.shape[0] - parts * part_rows))
    others = [
        pltpu.make_async_copy(src, dst, in_sems.at[index])
        for index, (src, dst) in enumerate(
            ((small_hbm, small), (layer_in, through.at[0]), (grad_in_in, through.at[1]))
        )
    ]
    for copy in pieces + others:
        copy.start()

    def take(start, rows):
        return shares[pl.ds(start, rows), :].astype(F32)

    def give(index):
        moves.append(pltpu.make_async_copy(held[index], outs[2 + index], sems.at[2 + index]))
        moves[-1].start()

    for part in range(parts):
        pieces[part].wait()
        own_rows = pl.ds(part * LANES, LANES)
        for col in range(blocks):
            gf[own_rows, pl.ds(col * LANES, LANES)] = take(part * part_rows + col * LANES, LANES)
        moves.append(pltpu.make_async_copy(gf.at[own_rows], outs[7].at[own_rows], sems.at[11 + part]))
        moves[-1].start()
        base = part * part_rows + blocks * LANES
        for share in range(GROUP):
            gi[:, pl.ds((share * parts + part) * LANES, LANES)] = take(base + share * row_share, row_share)
    give(4)
    for copy in others:
        copy.wait()
    for copy in moves[:2]:
        copy.start()
    pieces[parts].wait()
    base = parts * part_rows
    for col in range(blocks):
        go[:, pl.ds(col * LANES, LANES)] = take(base + col * row_share, row_share)
    give(3)
    for index, ref in enumerate((gq, gk, gv)):
        for group in range(blocks // 2):
            for side in range(2):
                place = base + (1 + group) * blocks * row_share + (2 * index + side) * row_share
                ref[:, pl.ds(group * WIDE + side * LANES, LANES)] = take(place, row_share)
        give(index)
    own = lax.broadcasted_iota(jnp.int32, (GROUP, row_share), 0) == lax.axis_index("dp") % GROUP
    for first, ref in ((0, gain_a), (LANES, gain_f)):
        ref[...] = jnp.sum(jnp.where(own, small[pl.ds(0, GROUP), pl.ds(first, row_share)], 0.0), axis=0)
    table[...] = small[pl.ds(8, table.shape[0]), pl.ds(0, table.shape[1])]
    for index in (6, 7, 8):
        give(index)
    for copy in moves:
        copy.wait()


def on_device(
    dp_count,
    hidden_in,
    query_lengths,
    doc_lengths,
    w_query,
    w_key,
    w_value,
    w_attn_out,
    w_inner,
    w_outer,
    gain_attn,
    gain_ffn,
    bias_table,
    cotangent,
):
    rows, block, width = hidden_in.shape
    length = rows * block
    bucket_count, heads = bias_table.shape
    ffn = w_inner.shape[1]
    part_cols = GROUP * LANES
    parts = ffn // part_cols
    vec_len = 2 * length
    lo_count = dp_count // GROUP
    row_share = width // GROUP

    def vm(*shape, dtype=BF):
        return pltpu.VMEM(shape, dtype)

    def dma(count):
        return pltpu.SemaphoreType.DMA((count,))

    hbm = pl.BlockSpec(memory_space=pl.ANY)
    vmem = pl.BlockSpec(memory_space=pltpu.VMEM)
    smem = pl.BlockSpec(memory_space=pltpu.SMEM)
    small_rows = 8 + heads
    small_cols = 2 * LANES
    total_rows = sum(chunk_rows(row_share))
    layer_raw, grad_raw, shares, small = pl.pallas_call(
        partial(layer_kernel, lo_count),
        out_shape=(
            jax.ShapeDtypeStruct(hidden_in.shape, BF),
            jax.ShapeDtypeStruct(hidden_in.shape, BF),
            jax.ShapeDtypeStruct((total_rows, LANES), BF),
            jax.ShapeDtypeStruct((small_rows, small_cols), F32),
        ),
        in_specs=[hbm, hbm, smem, smem] + [hbm] * 9,
        out_specs=(hbm, hbm, hbm, vmem),
        scratch_shapes=[
            vm(length, width),
            vm(length, width),
            vm(width, width),
            vm(width, width),
            vm(width, width),
            vm(width, width),
            vm(parts, width, part_cols),
            vm(parts, part_cols, width),
            vm(length, width),
            vm(length, width),
            vm(length, width),
            vm(length, width),
            vm(heads, length, length),
            vm(length, width),
            vm(length, width),
            vm(width),
            vm(width),
            vm(heads, bucket_count),
            vm(part_cols, length),
            vm(width, length),
            vm(length, width, dtype=F32),
            vm(length, width, dtype=F32),
            vm(parts, length, part_cols),
            vm(length, part_cols),
            vm(heads, block, vec_len),
            vm(16, vec_len, dtype=F32),
            vm(8, width, dtype=F32),
            vm(length, 2 * length),
            vm(block, vec_len, dtype=F32),
            vm(SLOTS, 2, 2, 2, max(chunk_rows(row_share)), LANES),
            vm(2, 2, total_rows, LANES),
            vm(2, total_rows, LANES),
            vm(total_rows, LANES),
            vm(total_rows, LANES),
            vm(total_rows, LANES),
            vm(5, small_rows, small_cols, dtype=F32),
            vm(5, small_rows, small_cols, dtype=F32),
            dma(4 + 2 * parts),
            dma(7),
        ]
        + [dma(rows)] * 8
        + [dma(CHUNKS)] * 13
        + [dma(5)] * 2,
        compiler_params=pltpu.CompilerParams(
            collective_id=0, has_side_effects=True, vmem_limit_bytes=64 * 2**20 - 2**19
        ),
    )(
        hidden_in,
        cotangent,
        query_lengths,
        doc_lengths,
        w_query,
        w_key,
        w_value,
        w_attn_out,
        w_inner,
        w_outer,
        gain_attn,
        gain_ffn,
        bias_table.T,
    )
    grad_shapes = [(row_share, width)] * 4 + [(row_share, ffn), (ffn // GROUP, width), (row_share,), (row_share,)]
    grad_shapes.append((heads, bucket_count))
    layer_out, grad_in, *grads = pl.pallas_call(
        partial(unpack_kernel, parts, row_share),
        out_shape=[jax.ShapeDtypeStruct(hidden_in.shape, BF)] * 2
        + [jax.ShapeDtypeStruct(shape, F32) for shape in grad_shapes],
        in_specs=[hbm] * 4,
        out_specs=[hbm] * 11,
        scratch_shapes=[vm(*shape, dtype=F32) for shape in grad_shapes]
        + [vm(total_rows, LANES), vm(small_rows, small_cols, dtype=F32), vm(2, *hidden_in.shape), dma(11 + parts), dma(4 + parts)],
        compiler_params=pltpu.CompilerParams(vmem_limit_bytes=64 * 2**20 - 2**19),
    )(shares, small, layer_raw, grad_raw)
    if lo_count > 1:
        high = lax.axis_index("dp") // lo_count

        def spread(part):
            whole = jnp.zeros((GROUP,) + part.shape, F32)
            whole = lax.dynamic_update_index_in_dim(whole, part, high, 0)
            whole = whole.reshape((GROUP * part.shape[0],) + part.shape[1:])
            return lax.psum_scatter(whole, "dp", scatter_dimension=0, tiled=True)

        small = lax.psum(small, "dp") / GROUP
        gain_rows = width // dp_count
        start = lax.axis_index("dp") * gain_rows
        gains = [
            lax.dynamic_slice_in_dim(small[:GROUP, first : first + row_share].reshape(width), start, gain_rows)
            for first in (0, LANES)
        ]
        grads = [spread(part) for part in grads[:6]] + gains + [small[8 : 8 + heads, :bucket_count]]
    return (layer_out, grad_in, *grads[:8], grads[8].T)


def solution(mesh):
    return jax.shard_map(
        partial(on_device, mesh.shape["dp"]),
        mesh=mesh,
        in_specs=(
            P("dp", "seq", None),
            P("dp"),
            P("dp"),
            P(),
            P(),
            P(),
            P(),
            P(),
            P(),
            P(),
            P(),
            P(),
            P("dp", "seq", None),
        ),
        out_specs=(
            P("dp", "seq", None),
            P("dp", "seq", None),
            P("dp", None),
            P("dp", None),
            P("dp", None),
            P("dp", None),
            P("dp", None),
            P("dp", None),
            P("dp"),
            P("dp"),
            P(),
        ),
        check_vma=False,
    )
```

```python
from functools import partial

import jax
import jax.numpy as jnp
from jax import lax
from jax.experimental import pallas as pl
from jax.experimental.pallas import tpu as pltpu
from jax.sharding import PartitionSpec as P

EPS = 1e-06
NEG = -1000000000.0
LIMITS = (12, 16, 23, 32, 46, 64, 91)
HIGH = lax.Precision.HIGHEST
MESH = pl.DeviceIdType.MESH
BF = jnp.bfloat16
F32 = jnp.float32

GROUP = 8
LANES = 128
WIDE = 256
SLOTS = 5
OUTER_SPLIT = ((2, 1), (2, 1), (2, 1))
INNER_SPLIT = ((2, 2), (2, 2), (2, 2))
ATTN_SPLIT = (3,)
GROUP_SPLIT = ((3,), (3,), (2, 1))


def chunk_rows(row_share):
    rows = []
    for outer, inner in zip(OUTER_SPLIT, INNER_SPLIT):
        rows += [count * 2 * LANES for count in outer] + [count * 2 * row_share for count in inner]
    for split in (ATTN_SPLIT,) + GROUP_SPLIT:
        rows += [count * 2 * row_share for count in split]
    return rows


CHUNKS = len(chunk_rows(96))


def dot_nn(left, right):
    return jnp.dot(left, right, preferred_element_type=F32)


def dot_nt(left, right):
    return lax.dot_general(left, right, (((1,), (1,)), ((), ())), preferred_element_type=F32)


def dot_tn(left, right):
    return lax.dot_general(left, right, (((0,), (0,)), ((), ())), preferred_element_type=F32)


def buckets(relative):
    distance = jnp.abs(relative)
    far_bucket = 8 + sum(((distance >= thresh).astype(jnp.int32) for thresh in LIMITS))
    return jnp.where(relative > 0, 16, 0) + jnp.where(distance < 8, distance, far_bucket)


def loop(count, body):
    lax.fori_loop(0, count, lambda index, none: (body(index), none)[1], None)


def at(index, size):
    if isinstance(index, int):
        return pl.ds(index * size, size)
    return pl.ds(pl.multiple_of(index * size, size), size)


def layer_kernel(
    lo_count,
    hidden,
    cot,
    query_len,
    doc_len,
    wq_hbm,
    wk_hbm,
    wv_hbm,
    wo_hbm,
    w1_hbm,
    w2_hbm,
    gain1_hbm,
    gain2_hbm,
    table_hbm,
    layer_out,
    grad_in,
    shares,
    small_out,
    x_row,
    c_row,
    wq,
    wk,
    wv,
    wo,
    w1,
    w2,
    n1,
    q,
    k,
    v,
    probs,
    o,
    n2,
    gain1,
    gain2,
    table,
    z_turned,
    turned,
    mid,
    acc_b,
    z,
    du,
    bias,
    vec,
    sums,
    dsc,
    tacc,
    grads,
    r_core,
    r_first,
    r_second,
    z_end,
    z_mid,
    small,
    small_in,
    w_sem,
    own_sem,
    x_send,
    x_recv,
    c_send,
    c_recv,
    y_send,
    y_recv,
    i_send,
    i_recv,
    core_send,
    core_recv,
    first_send,
    first_recv,
    second_send,
    second_recv,
    end_send,
    end_recv,
    mid_send,
    mid_recv,
    back_send,
    back_recv,
    share_sem,
    small_send,
    small_recv,
):
    dp = lax.axis_index("dp")
    sq = lax.axis_index("seq")
    seq_count, block, width = hidden.shape
    length = x_row.shape[0]
    heads, bucket_count = table.shape
    pairs = heads // 2
    row_share = width // GROUP
    parts = w1_hbm.shape[1] // (GROUP * LANES)
    part_cols = GROUP * LANES
    vec_len = vec.shape[1]

    high = dp // lo_count
    bit0 = lax.rem(high, 2)
    bit1 = lax.rem(high // 2, 2)
    bit2 = lax.rem(high // 4, 2)
    step1 = 2 * lo_count * (1 - 2 * bit1)
    step2 = 4 * lo_count * (1 - 2 * bit2)
    core_dev = (dp + lo_count * (1 - 2 * bit0), sq)
    first_dev = (dp + (1 - bit0) * step1 + bit0 * step2, sq)
    second_dev = (dp + bit0 * step1 + (1 - bit0) * step2, sq)
    first_bit = (1 - bit0) * bit1 + bit0 * bit2
    second_bit = (1 - bit0) * bit2 + bit0 * bit1
    pair_dev = (dp, sq + 1 - 2 * lax.rem(sq, 2))
    mid_dev = (dp, 3 - sq)
    is_end = jnp.logical_or(sq == 0, sq == seq_count - 1)
    is_mid = jnp.logical_not(is_end)
    row_devs = [lax.rem(sq + step, seq_count) for step in range(1, seq_count)]

    def remote(src, dst, send, recv, device):
        return pltpu.make_async_remote_copy(
            src_ref=src, dst_ref=dst, send_sem=send, recv_sem=recv, device_id=device, device_id_type=MESH
        )

    barrier = pltpu.get_barrier_semaphore()
    for device in [core_dev, first_dev, second_dev] + [(dp, other) for other in row_devs]:
        pl.semaphore_signal(barrier, inc=1, device_id=device, device_id_type=MESH)
    pl.semaphore_wait(barrier, 3 + len(row_devs))

    def deal(src_of, dst_of, send, recv):
        def copy(index):
            other = row_devs[index]
            return remote(src_of(other), dst_of(sq), send.at[index], recv.at[sq], (dp, other))

        def start(index):
            copy(index).start()

        def arrived(other):
            remote(src_of(other), dst_of(other), send.at[0], recv.at[other], (dp, other)).wait_recv()

        def sent():
            for index in range(len(row_devs)):
                copy(index).wait_send()

        return start, arrived, sent

    x_start, x_arrived, x_sent = deal(
        lambda other: hidden.at[other], lambda src: x_row.at[at(src, block)], x_send, x_recv
    )
    c_start, c_arrived, c_sent = deal(
        lambda other: cot.at[other], lambda src: c_row.at[at(src, block)], c_send, c_recv
    )
    y_start, y_arrived, y_sent = deal(
        lambda other: dsc.at[at(other, block), pl.ds(0, width)], lambda src: layer_out.at[src], y_send, y_recv
    )
    i_start, i_arrived, i_sent = deal(
        lambda other: du.at[at(other, block), pl.ds(0, width)], lambda src: grad_in.at[src], i_send, i_recv
    )
    own_x = pltpu.make_async_copy(hidden.at[sq], x_row.at[at(sq, block)], own_sem.at[0])
    own_c = pltpu.make_async_copy(cot.at[sq], c_row.at[at(sq, block)], own_sem.at[1])
    own_y = pltpu.make_async_copy(dsc.at[at(sq, block), pl.ds(0, width)], layer_out.at[sq], own_sem.at[2])
    own_i = pltpu.make_async_copy(du.at[at(sq, block), pl.ds(0, width)], grad_in.at[sq], own_sem.at[3])

    for index in range(len(row_devs)):
        x_start(index)
    own_x.start()
    params = [
        pltpu.make_async_copy(src, dst, own_sem.at[4 + index])
        for index, (src, dst) in enumerate(((gain1_hbm, gain1), (gain2_hbm, gain2), (table_hbm, table)))
    ]
    for copy in params:
        copy.start()
    square = [
        pltpu.make_async_copy(src, dst, w_sem.at[index])
        for index, (src, dst) in enumerate(((wq_hbm, wq), (wk_hbm, wk), (wv_hbm, wv), (wo_hbm, wo)))
    ]
    for copy in square:
        copy.start()

    def part_copies(part):
        span = parts * LANES
        copies = []
        for share in range(GROUP):
            place = pl.ds(share * span + part * LANES, LANES)
            cols = pl.ds(share * LANES, LANES)
            copies.append(pltpu.make_async_copy(w1_hbm.at[:, place], w1.at[part, :, cols], w_sem.at[4 + 2 * part]))
            copies.append(pltpu.make_async_copy(w2_hbm.at[place], w2.at[part, cols], w_sem.at[5 + 2 * part]))
        return copies

    def part_wait(part):
        pltpu.make_async_copy(w1.at[part], w1.at[part], w_sem.at[4 + 2 * part]).wait()
        pltpu.make_async_copy(w2.at[part], w2.at[part], w_sem.at[5 + 2 * part]).wait()

    for part in range(parts):
        for copy in part_copies(part):
            copy.start()
    own_c.start()

    sizes = chunk_rows(row_share)

    def span(chunk):
        return pl.ds(sum(sizes[:chunk]), sizes[chunk])

    def piece(ref, chunk, *index):
        lead = index + (slice(None),) * (len(ref.shape) - 2 - len(index))
        return ref.at[lead + (span(chunk),)]

    def grad_half(chunk, side):
        return grads.at[chunk % SLOTS, side, :, :, pl.ds(0, sizes[chunk])]

    def core_copy(chunk):
        return remote(
            grad_half(chunk, 1 - bit0), piece(r_core, chunk), core_send.at[chunk], core_recv.at[chunk], core_dev
        )

    def first_copy(chunk):
        return remote(
            piece(r_core, chunk, 1 - first_bit),
            piece(r_first, chunk),
            first_send.at[chunk],
            first_recv.at[chunk],
            first_dev,
        )

    def second_copy(chunk):
        return remote(
            piece(r_first, chunk, 1 - second_bit),
            piece(r_second, chunk),
            second_send.at[chunk],
            second_recv.at[chunk],
            second_dev,
        )

    def end_copy(chunk):
        return remote(
            piece(r_second, chunk), piece(z_end, chunk), end_send.at[chunk], end_recv.at[chunk], pair_dev
        )

    def mid_copy(chunk):
        return remote(
            piece(r_second, chunk), piece(z_mid, chunk), mid_send.at[chunk], mid_recv.at[chunk], mid_dev
        )

    def back_copy(chunk):
        return remote(
            piece(z_end, chunk), piece(shares, chunk), back_send.at[chunk], back_recv.at[chunk], pair_dev
        )

    def share_copy(chunk):
        return pltpu.make_async_copy(piece(z_end, chunk), piece(shares, chunk), share_sem.at[chunk])

    def core_done(chunk):
        copy = core_copy(chunk)
        copy.wait_recv()

        def add(index):
            one, two = index // 2, lax.rem(index, 2)
            r_core[one, two, span(chunk)] += grads[chunk % SLOTS, bit0, one, two, pl.ds(0, sizes[chunk])]

        loop(4, add)
        first_copy(chunk).start()
        copy.wait_send()

    def first_done(chunk):
        first_copy(chunk).wait_recv()

        def add(index):
            r_first[index, span(chunk)] += r_core[first_bit, index, span(chunk)]

        loop(2, add)
        second_copy(chunk).start()

    def second_done(chunk):
        second_copy(chunk).wait_recv()
        r_second[span(chunk)] += r_first[second_bit, span(chunk)]

        @pl.when(is_end)
        def _():
            end_copy(chunk).start()

    def end_done(chunk):
        @pl.when(is_mid)
        def _():
            end_copy(chunk).wait_recv()
            r_second[span(chunk)] += z_end[span(chunk)]
            mid_copy(chunk).start()

    def mid_done(chunk):
        @pl.when(is_mid)
        def _():
            mid_copy(chunk).wait_recv()
            z_end[span(chunk)] = r_second[span(chunk)] + z_mid[span(chunk)]
            back_copy(chunk).start()
            share_copy(chunk).start()

    def back_done(chunk):
        @pl.when(is_end)
        def _():
            back_copy(chunk).wait_recv()

    stages = (core_done, first_done, second_done, end_done, mid_done, back_done)

    def settle():
        for chunk in range(CHUNKS):
            first_copy(chunk).wait_send()
            second_copy(chunk).wait_send()

        @pl.when(is_end)
        def _():
            for chunk in range(CHUNKS):
                end_copy(chunk).wait_send()

        @pl.when(is_mid)
        def _():
            for chunk in range(CHUNKS):
                mid_copy(chunk).wait_send()
                back_copy(chunk).wait_send()
                share_copy(chunk).wait()

    def small_copy(step):
        device = (core_dev, (dp + step1, sq), (dp + step2, sq), pair_dev, (dp, lax.rem(sq + 2, 4)))[step]
        return remote(small.at[step], small_in.at[step], small_send.at[step], small_recv.at[step], device)

    def small_done(step):
        small_copy(step).wait_recv()
        if step < 4:
            small[step + 1] = small[step] + small_in[step]
            small_copy(step + 1).start()
        else:
            small_out[...] = small[step] + small_in[step]

    def tick(spot):
        for what, index in PLAN.get(spot, ()):
            if what == "y":
                y_start(index)
            elif what == "i":
                i_start(index)
            elif what == "s":
                small_done(index)
            else:
                stages[what](index)

    def tiles(split, first, kind, part, body):
        done = 0
        for place, count in enumerate(split):
            chunk = first + place
            if count == 1:
                body(chunk, done, 0)
            else:
                loop(count, lambda index: body(chunk, done + index, index))
            core_copy(chunk).start()
            tick((kind, part, place))
            done += count
        return first + len(split)

    def place_of(share):
        one, two, three = share % 2, (share // 2) % 2, share // 4
        return (one, two, three) if one == 0 else (one, three, two)

    for copy in params:
        copy.wait()
    distance = lax.broadcasted_iota(jnp.int32, (1, vec_len), 1) - vec_len // 2
    bucket_row = buckets(distance)
    one_hot = (
        jnp.broadcast_to(bucket_row, (bucket_count, vec_len))
        == lax.broadcasted_iota(jnp.int32, (bucket_count, vec_len), 0)
    ).astype(F32)
    vec[pl.ds(0, heads), :] = dot_nn(table[...], one_hot.astype(BF))
    sub = lax.broadcasted_iota(jnp.int32, (8, vec_len), 0)

    def build_bias(head):
        rows = jnp.broadcast_to(vec[pl.ds(head, 1), :], (8, vec_len))
        for shift in (1, 2, 4):
            rows = jnp.where((sub & shift) != 0, pltpu.roll(rows, shift, 1), rows)
        shift = 8
        while shift < block:
            rows = jnp.concatenate([rows, pltpu.roll(rows, shift, 1)], axis=0)
            shift *= 2
        bias[head] = rows.astype(BF)

    loop(heads, build_bias)

    total_len = query_len[sq] + doc_len[sq]
    key_mask = jnp.where(
        lax.broadcasted_iota(jnp.int32, (1, length), 1) < total_len, jnp.float32(0), jnp.float32(NEG)
    )
    low_lanes = lax.broadcasted_iota(jnp.int32, (1, LANES), 1) < LANES // 2

    def half_of(values, half):
        keep = low_lanes if half == 0 else jnp.logical_not(low_lanes)
        return jnp.where(keep, values, jnp.zeros_like(values))

    gain_one = gain1[...].astype(F32).reshape(1, width)
    gain_two = gain2[...].astype(F32).reshape(1, width)

    def norm_first(index):
        rows = at(index, block)
        values = x_row[rows, :].astype(F32)
        factor = lax.rsqrt(jnp.mean(values * values, axis=-1, keepdims=True) + EPS)
        n1[rows, :] = (values * factor * gain_one).astype(BF)

    own_x.wait()
    norm_first(sq)
    for other in row_devs[:-1]:
        x_arrived(other)
        norm_first(other)
    x_arrived(row_devs[-1])
    for index in range(len(row_devs)):
        c_start(index)
    norm_first(row_devs[-1])
    for copy in square:
        copy.wait()

    def project(index):
        cols = at(index, WIDE)
        q[:, cols] = dot_nn(n1[...], wq[:, cols]).astype(BF)
        k[:, cols] = dot_nn(n1[...], wk[:, cols]).astype(BF)
        v[:, cols] = dot_nn(n1[...], wv[:, cols]).astype(BF)

    loop(width // WIDE, project)

    def attend(pair):
        cols = at(pair, LANES)
        keys = k[:, cols]
        values = v[:, cols]
        for tile in range(length // WIDE):
            rows = pl.ds(tile * WIDE, WIDE)
            queries = q[rows, cols]
            total = None
            for half in range(2):
                head = 2 * pair + half
                scores = dot_nt(half_of(queries, half), keys)
                weights = []
                for part in range(WIDE // block):
                    start = vec_len // 2 - tile * WIDE - part * block
                    here = scores[part * block : (part + 1) * block]
                    here = here + bias[head, :, pl.ds(start, length)].astype(F32) + key_mask
                    here = jnp.exp(here - jnp.max(here, axis=-1, keepdims=True))
                    scale = 1.0 / jnp.sum(here, axis=-1, keepdims=True)
                    weights.append((here * scale).astype(BF))
                weights = jnp.concatenate(weights, axis=0)
                probs[head, rows, :] = weights
                term = dot_nn(weights, half_of(values, half))
                total = term if total is None else total + term
            o[rows, cols] = total.astype(BF)

    loop(pairs, attend)

    def attn_out(index):
        cols = at(index, WIDE)
        mid[:, cols] = x_row[:, cols].astype(F32) + dot_nn(o[...], wo[:, cols])

    loop(width // WIDE, attn_out)

    def norm_second(index):
        rows = at(index, block)
        values = mid[rows, :]
        factor = lax.rsqrt(jnp.mean(values * values, axis=-1, keepdims=True) + EPS)
        n2[rows, :] = (values * factor * gain_two).astype(BF)

    loop(seq_count, norm_second)

    def turn(source):
        def body(index):
            span = at(index, LANES)
            turned[span, :] = source[:, span].T

        loop(width // LANES, body)

    def put(chunk, values, tile):
        rows = values.shape[0] // GROUP
        for share in range(GROUP):
            for side in range(2):
                one, two, three = place_of(share)
                place = (2 * tile + side) * rows
                if not isinstance(tile, int):
                    place = pl.multiple_of(place, rows)
                grads[chunk % SLOTS, one, two, three, pl.ds(place, rows), :] = values[
                    share * rows : (share + 1) * rows, side * LANES : (side + 1) * LANES
                ].astype(BF)

    row_blocks = length // block
    for part in range(parts):
        part_wait(part)

        def forward(index):
            cols = at(index, WIDE)
            inner = dot_nn(n2[...], w1[part, :, cols])
            square_in = inner * inner
            bend = jnp.tanh(inner * (0.7978845608028654 + (0.7978845608028654 * 0.044715) * square_in))
            gate = 0.5 + 0.5 * bend
            active = inner * gate
            z[part, :, cols] = active.astype(BF)
            slope = 1.5957691216057308 + (6 * 0.7978845608028654 * 0.044715) * square_in
            slope = (gate + active * ((1 - gate) * slope)).astype(BF)
            for rows in range(row_blocks):
                bias[part * row_blocks + rows, :, cols] = slope[rows * block : (rows + 1) * block]

        def forward_two(index):
            forward(2 * index)
            forward(2 * index + 1)

        loop(part_cols // (2 * WIDE), forward_two)

    def layer_tile(index):
        cols = at(index, WIDE)
        total = mid[:, cols]
        for part in range(parts):
            total = total + dot_nn(z[part], w2[part, :, cols])
        dsc[:, cols] = total.astype(BF)

    loop(width // WIDE, layer_tile)
    own_y.start()
    tick(("y", 0, 0))
    turn(n2)
    own_c.wait()
    for other in row_devs:
        c_arrived(other)

    chunk = 0
    for part in range(parts):

        def backward(index):
            cols = at(index, WIDE)
            back = dot_nt(c_row[...], w2[part, cols, :])
            for rows in range(row_blocks):
                span_rows = pl.ds(rows * block, block)
                slope = bias[part * row_blocks + rows, :, cols].astype(F32)
                du[span_rows, cols] = (back[rows * block : (rows + 1) * block] * slope).astype(BF)
            z_turned[cols, :] = z[part, :, cols].T

        loop(part_cols // WIDE, backward)
        tick(("u", part, 0))

        def outer_tile(chunk, tile, place):
            put(chunk, dot_nn(z_turned[...], c_row[:, at(tile, WIDE)]), place)

        chunk = tiles(OUTER_SPLIT[part], chunk, "o", part, outer_tile)

        def inner_tile(chunk, tile, place):
            put(chunk, dot_nn(turned[...], du[:, at(tile, WIDE)]), place)

        chunk = tiles(INNER_SPLIT[part], chunk, "n", part, inner_tile)

        def add_up(index):
            cols = at(index, WIDE)
            back = dot_nt(du[...], w1[part, cols, :])
            if part == 0:
                acc_b[:, cols] = back
            else:
                acc_b[:, cols] += back

        loop(width // WIDE, add_up)
        tick(("s", part, 0))

    sums[...] = jnp.zeros_like(sums)

    def back_second(index):
        rows = at(index, block)
        values = mid[rows, :]
        back = acc_b[rows, :]
        factor = lax.rsqrt(jnp.mean(values * values, axis=-1, keepdims=True) + EPS)
        sums[1:2, :] += jnp.sum(back * values * factor, axis=0, keepdims=True)
        scaled = back * gain_two
        inside = jnp.mean(scaled * values, axis=-1, keepdims=True)
        total = c_row[rows, :].astype(F32) + factor * scaled - values * (factor * factor * factor * inside)
        acc_b[rows, :] = total
        n2[rows, :] = total.astype(BF)

    loop(seq_count, back_second)
    tick(("r", 0, 0))

    def back_out(index):
        cols = at(index, WIDE)
        c_row[:, cols] = dot_nt(n2[...], wo[cols, :]).astype(BF)

    loop(width // WIDE, back_out)
    tick(("r", 0, 1))

    def attend_back(pair):
        cols = at(pair, LANES)
        keys = k[:, cols]
        values = v[:, cols]
        queries = q[:, cols]
        backs = c_row[:, cols]
        product = backs.astype(F32) * o[:, cols].astype(F32)
        for half in range(2):
            head = 2 * pair + half
            dot_sum = jnp.sum(half_of(product, half), axis=-1, keepdims=True)
            tacc[...] = jnp.zeros_like(tacc)
            for tile in range(length // WIDE):
                rows = pl.ds(tile * WIDE, WIDE)
                back = dot_nt(half_of(backs[tile * WIDE : (tile + 1) * WIDE], half), values)
                for part in range(WIDE // block):
                    base = tile * WIDE + part * block
                    start = vec_len // 2 - base
                    score = probs[head, pl.ds(base, block), :].astype(F32) * (
                        back[part * block : (part + 1) * block] - dot_sum[base : base + block]
                    )
                    tacc[:, pl.ds(start, length)] += score
                    dsc[pl.ds(base, block), pl.ds(half * length, length)] = score.astype(BF)
            rows = tacc[...]
            size = block
            while size > 8:
                size //= 2
                rows = rows[:size] + pltpu.roll(rows[size:], vec_len - size, 1)
            for shift in (4, 2, 1):
                rows = jnp.where((sub & shift) != 0, pltpu.roll(rows, vec_len - shift, 1), rows)
            vec[pl.ds(head, 1), :] = jnp.sum(rows, axis=0, keepdims=True)
        z[0, :, cols] = (
            dot_nn(dsc[:, pl.ds(0, length)], half_of(keys, 0)) + dot_nn(dsc[:, pl.ds(length, length)], half_of(keys, 1))
        ).astype(BF)
        z[1, :, cols] = (
            dot_tn(dsc[:, pl.ds(0, length)], half_of(queries, 0)) + dot_tn(dsc[:, pl.ds(length, length)], half_of(queries, 1))
        ).astype(BF)
        z[2, :, cols] = (
            dot_tn(probs[2 * pair], half_of(backs, 0)) + dot_tn(probs[2 * pair + 1], half_of(backs, 1))
        ).astype(BF)

    own_y.wait()
    y_sent()
    for pair in range(pairs):
        attend_back(pair)
        tick(("h", pair, 0))

    def back_project(index):
        cols = at(index, WIDE)
        span_cols = pl.ds(0, width)
        mid[:, cols] = (
            dot_nt(z[0, :, span_cols], wq[cols, :])
            + dot_nt(z[1, :, span_cols], wk[cols, :])
            + dot_nt(z[2, :, span_cols], wv[cols, :])
        )

    loop(width // WIDE, back_project)
    tick(("d", 0, 0))

    def back_first(index):
        rows = at(index, block)
        values = x_row[rows, :].astype(F32)
        back = mid[rows, :]
        factor = lax.rsqrt(jnp.mean(values * values, axis=-1, keepdims=True) + EPS)
        sums[0:1, :] += jnp.sum(back * values * factor, axis=0, keepdims=True)
        scaled = back * gain_one
        inside = jnp.mean(scaled * values, axis=-1, keepdims=True)
        total = acc_b[rows, :] + factor * scaled - values * (factor * factor * factor * inside)
        du[rows, pl.ds(0, width)] = total.astype(BF)

    loop(seq_count, back_first)
    table_sum = lax.dot_general(
        vec[pl.ds(0, heads), :],
        one_hot,
        (((1,), (1,)), ((), ())),
        precision=HIGH,
        preferred_element_type=F32,
    )
    small[0] = jnp.zeros(small.shape[1:], F32)
    for share in range(GROUP):
        own = pl.ds(share, 1)
        small[0, own, pl.ds(0, row_share)] = sums[0:1, share * row_share : (share + 1) * row_share]
        small[0, own, pl.ds(LANES, row_share)] = sums[1:2, share * row_share : (share + 1) * row_share]
    small[0, pl.ds(8, heads), pl.ds(0, bucket_count)] = table_sum
    small_copy(0).start()
    own_i.start()
    tick(("i", 0, 0))

    turn(o)

    def attn_out_tile(chunk, tile, place):
        put(chunk, dot_nn(turned[...], n2[:, at(tile, WIDE)]), place)

    chunk = tiles(ATTN_SPLIT, chunk, "a", 0, attn_out_tile)
    turn(n1)
    for group in range(width // WIDE):

        def group_tile(chunk, tile, place):
            put(chunk, dot_nn(turned[...], z[tile, :, pl.ds(group * WIDE, WIDE)]), place)

        chunk = tiles(GROUP_SPLIT[group], chunk, "g", group, group_tile)
    tick(("e", 0, 0))
    for step in range(5):
        small_copy(step).wait_send()
    settle()
    own_i.wait()
    for other in row_devs:
        y_arrived(other)
        i_arrived(other)
    x_sent()
    c_sent()
    i_sent()


PLAN = {
    ("y", 0, 0): (("y", 0),),
    ("n", 0, 1): ((0, 0), ("y", 1)),
    ("s", 0, 0): ((0, 1), (0, 2)),
    ("o", 1, 1): (("y", 2),),
    ("n", 1, 0): ((1, 0),),
    ("n", 1, 1): ((1, 1),),
    ("s", 1, 0): ((0, 3), (0, 4), (0, 5), (0, 6)),
    ("u", 2, 0): ((2, 0), (1, 2)),
    ("o", 2, 0): ((2, 1),),
    ("o", 2, 1): ((1, 3),),
    ("s", 2, 0): ((2, 2),),
    ("r", 0, 0): ((2, 3), (1, 4)),
    ("r", 0, 1): ((1, 5),),
    ("h", 0, 0): ((0, 7), (0, 8), (0, 9), (0, 10), (0, 11)),
    ("h", 1, 0): ((3, 0), (3, 1), (2, 4), (2, 5), (1, 6)),
    ("h", 2, 0): ((1, 7),),
    ("h", 3, 0): ((3, 2),),
    ("h", 4, 0): ((4, 0), (3, 3), (2, 6)),
    ("h", 5, 0): ((4, 1), (2, 7), (1, 8)),
    ("d", 0, 0): ((4, 2), (1, 9)),
    ("i", 0, 0): ((5, 0), (5, 1), (4, 3), (3, 4), (2, 8), (1, 10), ("i", 0)),
    ("a", 0, 0): ((5, 2), (3, 5), (2, 9), (1, 11), ("s", 0)),
    ("g", 0, 0): ((5, 3), (3, 6), (2, 10)),
    ("g", 1, 0): ((4, 4), (3, 7), (0, 12), ("s", 1)),
    ("g", 2, 0): ((2, 11), (0, 13)),
    ("e", 0, 0): (("s", 2), (4, 5), (3, 8), (5, 4), (1, 12), (0, 14), (4, 6), (5, 5), (4, 7), ("i", 1), (3, 9), (1, 13), (0, 15), (5, 6), (4, 8), (2, 12), (3, 10), (3, 11), (5, 7), ("s", 3), (1, 14), (2, 13), (0, 16), (1, 15), (5, 8), (1, 16), (2, 14), (2, 15), (4, 9), (2, 16), (4, 10), (5, 9), (3, 12), (4, 11), ("s", 4), (5, 10), ("i", 2), (3, 13), (5, 11), (4, 12), (3, 14), (3, 15), (4, 13), (3, 16), (4, 14), (5, 12), (4, 15), (4, 16), (5, 13), (5, 14), (5, 15), (5, 16)),
}


def unpack_kernel(parts, row_share, shares_hbm, small_hbm, layer_in, grad_in_in, *refs):
    outs, held, (shares, small, through, sems, in_sems) = refs[:11], refs[11:20], refs[20:]
    moves = [pltpu.make_async_copy(through.at[index], outs[index], sems.at[index]) for index in range(2)]
    gq, gk, gv, go, gi, gf, gain_a, gain_f, table = held
    blocks = gq.shape[1] // LANES
    part_rows = blocks * LANES + GROUP * row_share

    def load_share(index, rows):
        place = pl.ds(index * part_rows, rows)
        return pltpu.make_async_copy(shares_hbm.at[place], shares.at[place], in_sems.at[3 + index])

    pieces = [load_share(part, part_rows) for part in range(parts)]
    pieces.append(load_share(parts, shares.shape[0] - parts * part_rows))
    others = [
        pltpu.make_async_copy(src, dst, in_sems.at[index])
        for index, (src, dst) in enumerate(
            ((small_hbm, small), (layer_in, through.at[0]), (grad_in_in, through.at[1]))
        )
    ]
    for copy in pieces + others:
        copy.start()

    def take(start, rows):
        return shares[pl.ds(start, rows), :].astype(F32)

    def give(index):
        moves.append(pltpu.make_async_copy(held[index], outs[2 + index], sems.at[2 + index]))
        moves[-1].start()

    for part in range(parts):
        pieces[part].wait()
        own_rows = pl.ds(part * LANES, LANES)
        for col in range(blocks):
            gf[own_rows, pl.ds(col * LANES, LANES)] = take(part * part_rows + col * LANES, LANES)
        moves.append(pltpu.make_async_copy(gf.at[own_rows], outs[7].at[own_rows], sems.at[11 + part]))
        moves[-1].start()
        base = part * part_rows + blocks * LANES
        for share in range(GROUP):
            gi[:, pl.ds((share * parts + part) * LANES, LANES)] = take(base + share * row_share, row_share)
    give(4)
    for copy in others:
        copy.wait()
    for copy in moves[:2]:
        copy.start()
    pieces[parts].wait()
    base = parts * part_rows
    for col in range(blocks):
        go[:, pl.ds(col * LANES, LANES)] = take(base + col * row_share, row_share)
    give(3)
    for index, ref in enumerate((gq, gk, gv)):
        for group in range(blocks // 2):
            for side in range(2):
                place = base + (1 + group) * blocks * row_share + (2 * index + side) * row_share
                ref[:, pl.ds(group * WIDE + side * LANES, LANES)] = take(place, row_share)
        give(index)
    own = lax.broadcasted_iota(jnp.int32, (GROUP, row_share), 0) == lax.axis_index("dp") % GROUP
    for first, ref in ((0, gain_a), (LANES, gain_f)):
        ref[...] = jnp.sum(jnp.where(own, small[pl.ds(0, GROUP), pl.ds(first, row_share)], 0.0), axis=0)
    table[...] = small[pl.ds(8, table.shape[0]), pl.ds(0, table.shape[1])]
    for index in (6, 7, 8):
        give(index)
    for copy in moves:
        copy.wait()


def on_device(
    dp_count,
    hidden_in,
    query_lengths,
    doc_lengths,
    w_query,
    w_key,
    w_value,
    w_attn_out,
    w_inner,
    w_outer,
    gain_attn,
    gain_ffn,
    bias_table,
    cotangent,
):
    rows, block, width = hidden_in.shape
    length = rows * block
    bucket_count, heads = bias_table.shape
    ffn = w_inner.shape[1]
    part_cols = GROUP * LANES
    parts = ffn // part_cols
    vec_len = 2 * length
    lo_count = dp_count // GROUP
    row_share = width // GROUP

    def vm(*shape, dtype=BF):
        return pltpu.VMEM(shape, dtype)

    def dma(count):
        return pltpu.SemaphoreType.DMA((count,))

    hbm = pl.BlockSpec(memory_space=pl.ANY)
    vmem = pl.BlockSpec(memory_space=pltpu.VMEM)
    smem = pl.BlockSpec(memory_space=pltpu.SMEM)
    small_rows = 8 + heads
    small_cols = 2 * LANES
    total_rows = sum(chunk_rows(row_share))
    layer_raw, grad_raw, shares, small = pl.pallas_call(
        partial(layer_kernel, lo_count),
        out_shape=(
            jax.ShapeDtypeStruct(hidden_in.shape, BF),
            jax.ShapeDtypeStruct(hidden_in.shape, BF),
            jax.ShapeDtypeStruct((total_rows, LANES), BF),
            jax.ShapeDtypeStruct((small_rows, small_cols), F32),
        ),
        in_specs=[hbm, hbm, smem, smem] + [hbm] * 9,
        out_specs=(hbm, hbm, hbm, vmem),
        scratch_shapes=[
            vm(length, width),
            vm(length, width),
            vm(width, width),
            vm(width, width),
            vm(width, width),
            vm(width, width),
            vm(parts, width, part_cols),
            vm(parts, part_cols, width),
            vm(length, width),
            vm(length, width),
            vm(length, width),
            vm(length, width),
            vm(heads, length, length),
            vm(length, width),
            vm(length, width),
            vm(width),
            vm(width),
            vm(heads, bucket_count),
            vm(part_cols, length),
            vm(width, length),
            vm(length, width, dtype=F32),
            vm(length, width, dtype=F32),
            vm(parts, length, part_cols),
            vm(length, part_cols),
            vm(heads, block, vec_len),
            vm(16, vec_len, dtype=F32),
            vm(8, width, dtype=F32),
            vm(length, 2 * length),
            vm(block, vec_len, dtype=F32),
            vm(SLOTS, 2, 2, 2, max(chunk_rows(row_share)), LANES),
            vm(2, 2, total_rows, LANES),
            vm(2, total_rows, LANES),
            vm(total_rows, LANES),
            vm(total_rows, LANES),
            vm(total_rows, LANES),
            vm(5, small_rows, small_cols, dtype=F32),
            vm(5, small_rows, small_cols, dtype=F32),
            dma(4 + 2 * parts),
            dma(7),
        ]
        + [dma(rows)] * 8
        + [dma(CHUNKS)] * 13
        + [dma(5)] * 2,
        compiler_params=pltpu.CompilerParams(
            collective_id=0, has_side_effects=True, vmem_limit_bytes=64 * 2**20 - 2**19
        ),
    )(
        hidden_in,
        cotangent,
        query_lengths,
        doc_lengths,
        w_query,
        w_key,
        w_value,
        w_attn_out,
        w_inner,
        w_outer,
        gain_attn,
        gain_ffn,
        bias_table.T,
    )
    grad_shapes = [(row_share, width)] * 4 + [(row_share, ffn), (ffn // GROUP, width), (row_share,), (row_share,)]
    grad_shapes.append((heads, bucket_count))
    layer_out, grad_in, *grads = pl.pallas_call(
        partial(unpack_kernel, parts, row_share),
        out_shape=[jax.ShapeDtypeStruct(hidden_in.shape, BF)] * 2
        + [jax.ShapeDtypeStruct(shape, F32) for shape in grad_shapes],
        in_specs=[hbm] * 4,
        out_specs=[hbm] * 11,
        scratch_shapes=[vm(*shape, dtype=F32) for shape in grad_shapes]
        + [vm(total_rows, LANES), vm(small_rows, small_cols, dtype=F32), vm(2, *hidden_in.shape), dma(11 + parts), dma(4 + parts)],
        compiler_params=pltpu.CompilerParams(vmem_limit_bytes=64 * 2**20 - 2**19),
    )(shares, small, layer_raw, grad_raw)
    if lo_count > 1:
        high = lax.axis_index("dp") // lo_count

        def spread(part):
            whole = jnp.zeros((GROUP,) + part.shape, F32)
            whole = lax.dynamic_update_index_in_dim(whole, part, high, 0)
            whole = whole.reshape((GROUP * part.shape[0],) + part.shape[1:])
            return lax.psum_scatter(whole, "dp", scatter_dimension=0, tiled=True)

        small = lax.psum(small, "dp") / GROUP
        gain_rows = width // dp_count
        start = lax.axis_index("dp") * gain_rows
        gains = [
            lax.dynamic_slice_in_dim(small[:GROUP, first : first + row_share].reshape(width), start, gain_rows)
            for first in (0, LANES)
        ]
        grads = [spread(part) for part in grads[:6]] + gains + [small[8 : 8 + heads, :bucket_count]]
    return (layer_out, grad_in, *grads[:8], grads[8].T)


def solution(mesh):
    return jax.shard_map(
        partial(on_device, mesh.shape["dp"]),
        mesh=mesh,
        in_specs=(
            P("dp", "seq", None),
            P("dp"),
            P("dp"),
            P(),
            P(),
            P(),
            P(),
            P(),
            P(),
            P(),
            P(),
            P(),
            P("dp", "seq", None),
        ),
        out_specs=(
            P("dp", "seq", None),
            P("dp", "seq", None),
            P("dp", None),
            P("dp", None),
            P("dp", None),
            P("dp", None),
            P("dp", None),
            P("dp", None),
            P("dp"),
            P("dp"),
            P(),
        ),
        check_vma=False,
    )
```
